32 devices in a mesh: role: 2 (over y), band: 4 (over z), turn: 4 (over x, core).
Axes of the slice: x: 2, y: 2, z: 4, core: 2. Of those that a mesh axis runs over, the one named last changes fastest.
Arguments:
- voltages: bfloat16 [8, 2, 256, 3840], P(('role', 'band'), None, 'turn'), may hold values from -6 to 6
- station_flags: int32 [256], P('turn'), may hold values 0 or 1
- filter_taps: bfloat16 [8, 256, 256], replicated, may hold values from -0.125 to 0.125
- kernel_rows: bfloat16 [8, 1, 32, 256], P(('role', 'band')), may hold values from -0.375 to 0.375
- kernel_cols: bfloat16 [8, 1, 32, 256], P(('role', 'band')), may hold values from -0.375 to 0.375
- cell_index: int32 [2, 1024, 1], P(None, ('role', 'band', 'turn')), may hold values from 0 to 4095
Outputs:
- image: float32 [32, 128], P(('role', 'band', 'turn'))
The draws below stay inside these ranges and needn't reach their ends.
All inputs are finite; a program needn't handle non-finite values. No bound on the sum of `station_flags` on one device may be relied on, other than what follows from the above.
Results may differ from the reference program's by a relative error of at most 0.0071.
Values may be sent and summed in bfloat16 or wider, within the bound.
No kernel may reach another device: no remote copies, remote signals or barrier semaphores. Data moves between devices by JAX's collectives and lax.ppermute only.
A program may use at most 64 MiB of HBM per device.

```python
import math
import jax
import jax.numpy as jnp
from jax import lax

STATIONS = 256
FINE = 128
TAPS = 8
FRAMES = 8
BLK = 256
SU = 32
SV = 32
NGRID = 4096
MW = 128
COARSE = 8
CHANNELS = 1024
NBLK = 1
LW = 32


def touch_ends(values, rng, smallest, top_value):
    index_at = [jax.random.randint(jax.random.fold_in(rng, axis), (), 0, length) for axis, length in enumerate(values.shape)]
    widest = values.shape.index(max(values.shape))
    neighbour = index_at[:widest] + [(index_at[widest] + 1) % values.shape[widest]] + index_at[widest + 1:]
    return values.at[tuple(index_at)].set(smallest).at[tuple(neighbour)].set(top_value)


def level_of(own_key, dims, split, low, largest):
    level = 1.0
    for dim, parts in split:
        heights = jax.random.uniform(jax.random.fold_in(jax.random.fold_in(own_key, 6), dim), (parts,), jnp.float32, low / len(split), largest / len(split))
        level = level * jnp.repeat(jnp.exp(heights), dims[dim] // parts).reshape((-1,) + (1,) * (len(dims) - 1 - dim))
    return level


def noise(own_key, extent, width, most, split=(), held_as=jnp.bfloat16):
    values = jax.random.normal(own_key, extent, jnp.float32) * width
    if len(split) > 0:
        values = level_of(own_key, extent, split, -0.22, 0.18) * values
    return jnp.clip(values, min=-most, max=most).astype(held_as)


def setup_inputs(seed: int = 0) -> dict:
    streams_of = jax.random.split(jax.random.key(seed), 7)
    voltages = noise(streams_of[0], (COARSE, 2, STATIONS, (FRAMES + TAPS - 1) * 2 * FINE), 1.0, 6.0, ((0, 8), (2, 4)))
    station_flags = touch_ends((jax.random.randint(streams_of[1], (STATIONS,), 0, 8) < 7).astype(jnp.int32), jax.random.fold_in(streams_of[1], 1), 0, 1)
    filter_taps = noise(streams_of[2], (TAPS, 2 * FINE, 2 * FINE), (TAPS * 2 * FINE) ** -0.5, 0.125)
    kernel_rows = noise(streams_of[3], (COARSE, NBLK, SU, BLK), BLK ** -0.5, 0.375, ((0, 8),))
    kernel_cols = noise(streams_of[4], (COARSE, NBLK, SV, BLK), BLK ** -0.5, 0.375, ((0, 8),))
    cell_index = touch_ends(jax.random.randint(streams_of[5], (2, CHANNELS, NBLK * NBLK), 0, NGRID), jax.random.fold_in(streams_of[5], 1), 0, NGRID - 1).astype(jnp.int32)
    return {"voltages": voltages, "station_flags": station_flags, "filter_taps": filter_taps, "kernel_rows": kernel_rows, "kernel_cols": kernel_cols, "cell_index": cell_index}


HIGHEST = lax.Precision.HIGHEST

def channelize(voltages, station_flags, filter_taps):
    polars, station_rows, sample_width = voltages.shape
    tap_count, two_fine, _ = filter_taps.shape
    block_total = sample_width // two_fine
    frames = block_total - tap_count + 1
    flagged = voltages * station_flags[None, :, None].astype(voltages.dtype)
    blocks = flagged.reshape(polars * station_rows, block_total, two_fine)
    running = jnp.zeros((polars * station_rows * frames, two_fine), jnp.float32)
    for tap_index in range(tap_count):
        segment = blocks[:, tap_index:tap_index + frames, :].reshape(polars * station_rows * frames, two_fine)
        running = running + jnp.dot(segment, filter_taps[tap_index], preferred_element_type=jnp.float32)
    fine_count = two_fine // 2
    result = running.astype(jnp.bfloat16).reshape(polars, station_rows, frames, 2, fine_count)
    return jnp.transpose(result, (4, 0, 1, 3, 2)).reshape(fine_count, polars, station_rows, 2 * frames)

def correlate(spectra):
    frames = spectra.shape[3] // 2
    station_count = spectra.shape[2]
    swapped = jnp.concatenate([-spectra[..., frames:], spectra[..., :frames]], axis=3)
    stacked = jnp.concatenate([spectra, swapped], axis=2)
    products = jnp.einsum('fpsa,fpka->fpsk', spectra.astype(jnp.float32), stacked.astype(jnp.float32), precision=HIGHEST)
    stokes = (products[:, 0] + products[:, 1]) * (1.0 / frames)
    return jnp.stack([stokes[:, :, :station_count], stokes[:, :, station_count:]]).astype(jnp.bfloat16)

def subgrids(visibility, kernel_rows, kernel_cols):
    fine_local = visibility.shape[1]
    station_count = visibility.shape[2]
    block_count, sub_u, block_width = kernel_rows.shape
    sub_v = kernel_cols.shape[1]
    station_rows = visibility.reshape(2, fine_local, block_count, block_width, station_count)
    partial_value = jnp.einsum('iab,xfibs->xfias', kernel_rows.astype(jnp.float32), station_rows.astype(jnp.float32), precision=HIGHEST)
    partial_value = partial_value.reshape(2, fine_local, block_count, sub_u, block_count, block_width)
    result = jnp.einsum('xfiajc,jdc->xfijad', partial_value, kernel_cols.astype(jnp.float32), precision=HIGHEST)
    return result.reshape(2, fine_local, block_count * block_count, sub_u * sub_v).astype(jnp.bfloat16)

def fine_subgrids(spectra, kernel_rows, kernel_cols):

    def one_fine(spec_one):
        return subgrids(correlate(spec_one[None]), kernel_rows, kernel_cols)[:, 0]
    stacked = lax.map(one_fine, spectra)
    return jnp.transpose(stacked, (1, 0, 2, 3))

def phase_table(positions, offset_count, pixels, grid_size):
    offsets = jnp.arange(offset_count, dtype=jnp.int32)
    position = positions[:, None, None].astype(jnp.int32) + offsets[None, :, None]
    phase_turns = jnp.mod(position * pixels[None, None, :], grid_size)
    angles = phase_turns.astype(jnp.float32) * (2.0 * math.pi / grid_size)
    return (jnp.cos(angles).astype(jnp.bfloat16), jnp.sin(angles).astype(jnp.bfloat16))

def image_rows(subgrid, positions, row_first, row_count, row_total, sub_u, sub_v, col_total, grid_size):
    count_sub = subgrid.shape[1]
    row_pix = row_first + jnp.arange(row_count, dtype=jnp.int32) - row_total // 2
    col_pix = jnp.arange(col_total, dtype=jnp.int32) - col_total // 2
    row_cos, row_sin = phase_table(positions[0], sub_u, row_pix, grid_size)
    col_cos, col_sin = phase_table(positions[1], sub_v, col_pix, grid_size)
    sub_cells = subgrid.reshape(2, count_sub, sub_u, sub_v).astype(jnp.float32)
    row_cos = row_cos.astype(jnp.float32)
    row_sin = row_sin.astype(jnp.float32)
    proj_real = (jnp.einsum('nal,nab->nbl', row_cos, sub_cells[0], precision=HIGHEST) - jnp.einsum('nal,nab->nbl', row_sin, sub_cells[1], precision=HIGHEST)).astype(jnp.bfloat16)
    proj_imag = (jnp.einsum('nal,nab->nbl', row_cos, sub_cells[1], precision=HIGHEST) + jnp.einsum('nal,nab->nbl', row_sin, sub_cells[0], precision=HIGHEST)).astype(jnp.bfloat16)
    return jnp.einsum('nbl,nbm->lm', proj_real.astype(jnp.float32), col_cos.astype(jnp.float32), precision=HIGHEST) - jnp.einsum('nbl,nbm->lm', proj_imag.astype(jnp.float32), col_sin.astype(jnp.float32), precision=HIGHEST)

def reference(voltages, station_flags, filter_taps, kernel_rows, kernel_cols, cell_index):
    positions_all = jnp.transpose(cell_index.reshape(2, COARSE, FINE * NBLK * NBLK), (1, 0, 2))

    def per_coarse(running, inputs_now):
        volt_now, rows_now, cols_now, places_now = inputs_now
        spectra = channelize(volt_now, station_flags, filter_taps)
        subgrid = fine_subgrids(spectra, rows_now, cols_now).reshape(2, FINE * NBLK * NBLK, SU * SV)
        return (running + image_rows(subgrid, places_now, 0, LW, LW, SU, SV, MW, NGRID), None)
    running, _ = lax.scan(per_coarse, jnp.zeros((LW, MW), jnp.float32), (voltages, kernel_rows, kernel_cols, positions_all))
    scale_factor = 4.0 / math.sqrt(CHANNELS * NBLK * NBLK * SU * SV)
    return running * scale_factor
```

```python
import functools
import math

import jax
import jax.numpy as jnp
import numpy as np
from jax import lax
from jax.experimental import pallas as pl
from jax.experimental.pallas import tpu as pltpu
from jax.sharding import PartitionSpec as P

NGRID = 4096
MW = 128
ROWS_DEV = 1
DIGIT = 64
PAD_ROWS = 16
VMEM_BYTES = 40 * 1024 * 1024


def spectra_kernel(pairs_each, volt_ref, flag_ref, taps_ref, rows_ref, cols_ref, cell_ref, out_ref):
    turn = lax.axis_index("turn")
    _, station_rows, width = volt_ref.shape
    taps, two_fine, _ = taps_ref.shape
    frames = width // two_fine - taps + 1
    dests = out_ref.shape[0]
    both = jnp.concatenate([rows_ref[...], cols_ref[...]], axis=0).astype(jnp.float32)
    weights = jnp.zeros((both.shape[0], station_rows), jnp.float32)
    for group in range(dests):
        piece = both[:, group * station_rows : (group + 1) * station_rows]
        weights = jnp.where(turn == group, piece, weights)
    weights = (weights * flag_ref[...].astype(jnp.float32)).astype(jnp.bfloat16)

    filt = taps_ref[...].reshape(taps * two_fine, two_fine)
    cells_rows = both.shape[0]
    for dest in range(dests):
        pairs = range(dest * pairs_each, (dest + 1) * pairs_each)
        lhs = jnp.concatenate(
            [
                volt_ref[pair // frames, :, (pair % frames) * two_fine : (pair % frames + taps) * two_fine]
                for pair in pairs
            ],
            axis=0,
        )
        spectra = jnp.dot(lhs, filt, preferred_element_type=jnp.float32).astype(jnp.bfloat16)
        for index in range(pairs_each):
            gridded = jnp.dot(
                weights,
                spectra[index * station_rows : (index + 1) * station_rows],
                preferred_element_type=jnp.float32,
            )
            out_ref[dest, index * cells_rows : (index + 1) * cells_rows] = gridded.astype(jnp.bfloat16)

    cell = cell_ref[...]
    count = cell.shape[1]
    wide = jnp.concatenate([cell] * (two_fine // count), axis=1)
    lane = lax.broadcasted_iota(jnp.int32, wide.shape, 1)
    wide = jnp.where((lane >= turn * count) & (lane < (turn + 1) * count), wide, 0)
    digits = jnp.concatenate([wide // DIGIT, wide % DIGIT], axis=0).astype(jnp.float32)
    digits = jnp.concatenate([digits, jnp.zeros((PAD_ROWS - 4, two_fine), jnp.float32)], axis=0)
    for dest in range(dests):
        out_ref[dest, pairs_each * cells_rows :] = digits.astype(jnp.bfloat16)


def image_kernel(pairs_each, row_total, got_ref, row_dft_ref, col_dft_ref, out_ref):
    fine = got_ref.shape[2] // 2
    sub = row_dft_ref.shape[1] // 4
    total = got_ref[0].astype(jnp.float32)
    for source in range(1, got_ref.shape[0]):
        total = total + got_ref[source].astype(jnp.float32)
    digits = total[pairs_each * 2 * sub :]
    cell_u = (digits[0:1, :fine] * DIGIT + digits[2:3, :fine]).astype(jnp.int32)
    cell_v = (digits[1:2, :fine] * DIGIT + digits[3:4, :fine]).astype(jnp.int32)

    def phase(cell, count):
        pixel = lax.broadcasted_iota(jnp.int32, (count, fine), 0) - count // 2
        angle = ((cell * pixel) & (NGRID - 1)).astype(jnp.float32) * (2.0 * math.pi / NGRID)
        return jnp.cos(angle), jnp.sin(angle)

    def transform(dft_ref, first, cos, sin):
        held = jnp.concatenate(
            [
                jnp.concatenate(
                    [
                        total[index * 2 * sub + first : index * 2 * sub + first + sub, :fine],
                        total[index * 2 * sub + first : index * 2 * sub + first + sub, fine:],
                    ],
                    axis=0,
                )
                for index in range(pairs_each)
            ],
            axis=1,
        ).astype(jnp.bfloat16)
        plain = jnp.dot(dft_ref[...], jnp.concatenate([held, held], axis=0), preferred_element_type=jnp.float32)
        half = plain.shape[0] // 2
        real, imag = plain[:half], plain[half:]
        cos = jnp.concatenate([cos] * pairs_each, axis=1)
        sin = jnp.concatenate([sin] * pairs_each, axis=1)
        return real * cos - imag * sin, real * sin + imag * cos

    row_real, row_imag = transform(row_dft_ref, 0, *phase(cell_u, row_total))
    col_real, col_imag = transform(col_dft_ref, sub, *phase(cell_v, MW))
    left = jnp.concatenate([row_real, -row_imag], axis=1).astype(jnp.bfloat16)
    right = jnp.concatenate([col_real, col_imag], axis=1).astype(jnp.bfloat16)
    out_ref[...] = lax.dot_general(
        left, right, (((1,), (1,)), ((), ())), preferred_element_type=jnp.float32
    )


def dft_matrix(pixels, cells, conjugate):
    angle = 2.0 * np.pi / NGRID * np.outer(np.arange(pixels) - pixels // 2, np.arange(cells))
    cos, sin = np.cos(angle), np.sin(angle)
    sign = -1.0 if conjugate else 1.0
    whole = np.block([[cos, -sign * sin], [sin, sign * cos]]).astype(np.float32)
    high = whole.astype(jnp.bfloat16)
    low = (whole - high.astype(np.float32)).astype(jnp.bfloat16)
    return np.concatenate([high, low], axis=1)


def call(kernel, out_shape, args):
    return pl.pallas_call(
        kernel,
        out_shape=out_shape,
        in_specs=[pl.BlockSpec(memory_space=pltpu.VMEM)] * len(args),
        out_specs=pl.BlockSpec(memory_space=pltpu.VMEM),
        compiler_params=pltpu.CompilerParams(vmem_limit_bytes=VMEM_BYTES),
    )(*args)


def local(voltages, station_flags, filter_taps, kernel_rows, kernel_cols, cell_index):
    polars, _, width = voltages.shape[1:]
    taps, two_fine, _ = filter_taps.shape
    sub_u, sub_v = kernel_rows.shape[2], kernel_cols.shape[2]
    turns = lax.axis_size("turn")
    everyone = ("role", "band", "turn")
    row_total = ROWS_DEV * lax.axis_size(everyone)
    channels = two_fine // 2 * lax.axis_size("role") * lax.axis_size("band")
    frames = width // two_fine - taps + 1
    scale_factor = 4.0 / math.sqrt(channels * sub_u * sub_v) / frames
    pairs_each = polars * frames // turns
    sent_rows = pairs_each * (sub_u + sub_v) + PAD_ROWS

    sent = call(
        functools.partial(spectra_kernel, pairs_each),
        jax.ShapeDtypeStruct((turns, sent_rows, two_fine), jnp.bfloat16),
        (
            voltages[0],
            station_flags.reshape(1, -1),
            filter_taps,
            kernel_rows[0, 0],
            kernel_cols[0, 0],
            cell_index.reshape(2, -1),
        ),
    )
    got = lax.all_to_all(sent, "turn", split_axis=0, concat_axis=0, tiled=True)
    part = call(
        functools.partial(image_kernel, pairs_each, row_total),
        jax.ShapeDtypeStruct((row_total, MW), jnp.float32),
        (
            got,
            jnp.asarray(dft_matrix(row_total, sub_u, False)),
            jnp.asarray(dft_matrix(MW, sub_v, True)),
        ),
    )
    rows = lax.all_to_all(part, everyone, split_axis=0, concat_axis=0, tiled=True)
    return jnp.sum(rows.reshape(-1, ROWS_DEV, MW), axis=0) * scale_factor


def solution(mesh):
    in_specs = (
        P(("role", "band"), None, "turn", None),
        P("turn"),
        P(),
        P(("role", "band"), None, None, None),
        P(("role", "band"), None, None, None),
        P(None, ("role", "band", "turn"), None),
    )
    out_specs = P(("role", "band", "turn"), None)
    return jax.shard_map(local, mesh=mesh, in_specs=in_specs, out_specs=out_specs, check_vma=False)
```

```python
import functools
import math

import jax
import jax.numpy as jnp
import numpy as np
from jax import lax
from jax.experimental import pallas as pl
from jax.experimental.pallas import tpu as pltpu
from jax.sharding import PartitionSpec as P

NGRID = 4096
MW = 128
ROWS_DEV = 1
DIGIT = 64
PAD_ROWS = 16
VMEM_BYTES = 24 * 1024 * 1024
FULL_VMEM_BYTES = 60 * 1024 * 1024


def partner(me, step, count):
    return me ^ step if count & (count - 1) == 0 else (me + step) % count


def spectra_kernel(
    far,
    pairs_each,
    volt_ref,
    flag_ref,
    taps_ref,
    rows_ref,
    cols_ref,
    cell_ref,
    *refs,
):
    turns = lax.axis_size("turn")
    half = turns // 2
    volt, taps_in, flag, rows, cols, cell_in, sems = refs[-7:]
    outs = refs[-7 - half : -7]
    turn = lax.axis_index("turn")
    side = turn // half ^ int(far)
    taps, two_fine, _ = taps_ref.shape
    station_rows, width = volt.shape
    copies = [
        pltpu.make_async_copy(source, dest, sems.at[index])
        for index, (source, dest) in enumerate(
            (
                (volt_ref.at[0, side], volt),
                (taps_ref, taps_in),
                (rows_ref.at[0, 0], rows),
                (cols_ref.at[0, 0], cols),
                (flag_ref, flag),
                (cell_ref, cell_in),
            )
        )
    ]
    for copy in copies:
        copy.start()
    for copy in copies[2:]:
        copy.wait()
    both = jnp.concatenate([rows[...], cols[...]], axis=0).astype(jnp.float32)
    cells_rows = both.shape[0]
    weights = jnp.zeros((cells_rows, station_rows), jnp.float32)
    for group in range(turns):
        piece = both[:, group * station_rows : (group + 1) * station_rows]
        weights = jnp.where(turn == group, piece, weights)
    weights = (weights * flag[...].astype(jnp.float32)).astype(jnp.bfloat16)

    cell = cell_in[...]
    count = cell.shape[1]
    wide = jnp.concatenate([cell] * (two_fine // count), axis=1)
    lane = lax.broadcasted_iota(jnp.int32, wide.shape, 1)
    wide = jnp.where((lane >= turn * count) & (lane < (turn + 1) * count), wide, 0)
    digits = jnp.concatenate([wide // DIGIT, wide % DIGIT], axis=0).astype(jnp.float32)
    digits = jnp.concatenate([digits, jnp.zeros((PAD_ROWS - 4, two_fine), jnp.float32)], axis=0)
    for out in outs:
        out[pairs_each * cells_rows :] = digits.astype(jnp.bfloat16)

    for copy in copies[:2]:
        copy.wait()
    filt = taps_in[...].reshape(taps * two_fine, two_fine)
    for step, out in enumerate(outs):
        first = (turn % half ^ step) * pairs_each
        lhs = jnp.concatenate(
            [
                volt[:, pl.ds(pl.multiple_of((first + index) * two_fine, two_fine), taps * two_fine)]
                for index in range(pairs_each)
            ],
            axis=0,
        )
        spectra = jnp.dot(lhs, filt, preferred_element_type=jnp.float32).astype(jnp.bfloat16)
        for index in range(pairs_each):
            gridded = jnp.dot(
                weights,
                spectra[index * station_rows : (index + 1) * station_rows],
                preferred_element_type=jnp.float32,
            )
            out[index * cells_rows : (index + 1) * cells_rows] = gridded.astype(jnp.bfloat16)


def split_terms(value):
    high = value.astype(jnp.bfloat16)
    return high, (value - high.astype(jnp.float32)).astype(jnp.bfloat16)


def image_kernel(pairs_each, sources, *refs):
    got = refs[:sources]
    row_dft_ref, col_dft_ref = refs[sources : sources + 2]
    outs, held_ref = refs[sources + 2 : -1], refs[-1]
    fine = got[0].shape[1] // 2
    sub = row_dft_ref.shape[1] // 6
    roles, bands, turns = (lax.axis_size(name) for name in ("role", "band", "turn"))
    row_total = roles * bands * turns * ROWS_DEV
    total = got[0][...].astype(jnp.float32)
    for source in got[1:]:
        total = total + source[...].astype(jnp.float32)
    digits = total[pairs_each * 2 * sub :]
    cell_u = (digits[0:1, :fine] * DIGIT + digits[2:3, :fine]).astype(jnp.int32)
    cell_v = (digits[1:2, :fine] * DIGIT + digits[3:4, :fine]).astype(jnp.int32)

    def phase(cell, pixel):
        angle = ((cell * pixel) & (NGRID - 1)).astype(jnp.float32) * (2.0 * math.pi / NGRID)
        return jnp.cos(angle), jnp.sin(angle)

    def transform(dft_ref, first, cos, sin):
        held = jnp.concatenate(
            [
                jnp.concatenate(
                    [
                        total[index * 2 * sub + first : index * 2 * sub + first + sub, :fine],
                        total[index * 2 * sub + first : index * 2 * sub + first + sub, fine:],
                    ],
                    axis=0,
                )
                for index in range(pairs_each)
            ],
            axis=1,
        )
        high, low = split_terms(held)
        plain = jnp.dot(
            dft_ref[...].astype(jnp.bfloat16), jnp.concatenate([high, high, low], axis=0), preferred_element_type=jnp.float32
        )
        half = plain.shape[0] // 2
        real, imag = plain[:half], plain[half:]
        cos = jnp.concatenate([cos] * pairs_each, axis=1)
        sin = jnp.concatenate([sin] * pairs_each, axis=1)
        return real * cos - imag * sin, real * sin + imag * cos

    place = lax.broadcasted_iota(jnp.int32, (row_total, fine), 0)
    inner, here = place // ROWS_DEV, place % ROWS_DEV
    row_role, row_turn, row_band = inner // (turns * bands), inner // bands % turns, inner % bands
    row = ((row_role * bands + row_band) * turns + row_turn) * ROWS_DEV + here
    row_real, row_imag = transform(row_dft_ref, 0, *phase(cell_u, row - row_total // 2))
    col = lax.broadcasted_iota(jnp.int32, (MW, fine), 0)
    col_real, col_imag = transform(col_dft_ref, sub, *phase(cell_v, col - MW // 2))
    left_high, left_low = split_terms(jnp.concatenate([row_real, -row_imag], axis=1))
    right_high, right_low = split_terms(jnp.concatenate([col_real, col_imag], axis=1))

    def product(left, right):
        return lax.dot_general(left, right, (((1,), (1,)), ((), ())), preferred_element_type=jnp.float32)

    held_ref[...] = product(left_high, right_high) + (
        product(left_high, right_low) + product(left_low, right_high)
    )
    me = lax.axis_index("role") * turns + lax.axis_index("turn")
    rows = bands * ROWS_DEV
    for step, out in enumerate(outs):
        out[...] = held_ref[pl.ds(partner(me, step, roles * turns) * rows, rows)]


def band_kernel(sources, *refs):
    outs, held_ref = refs[sources:-1], refs[-1]
    total = refs[0][...]
    for source in refs[1:sources]:
        total = total + source[...]
    held_ref[...] = total
    bands = lax.axis_size("band")
    for step, out in enumerate(outs):
        out[...] = held_ref[pl.ds(partner(lax.axis_index("band"), step, bands) * ROWS_DEV, ROWS_DEV)]


def final_kernel(scale_factor, *refs):
    total = refs[0][...]
    for source in refs[1:-1]:
        total = total + source[...]
    refs[-1][...] = total * scale_factor


def dft_matrix(pixel, cells, conjugate):
    angle = 2.0 * np.pi / NGRID * np.outer(pixel, np.arange(cells))
    cos, sin = np.cos(angle), np.sin(angle)
    sign = -1.0 if conjugate else 1.0
    whole = np.block([[cos, -sign * sin], [sin, sign * cos]]).astype(np.float32)
    high = whole.astype(jnp.bfloat16)
    low = (whole - high.astype(np.float32)).astype(jnp.bfloat16)
    return np.concatenate([high, low, high], axis=1).astype(np.float32)


def call(kernel, shapes, args, space=pltpu.VMEM, scratch=(), flops=0):
    moved = sum(math.prod(shape.shape) * shape.dtype.itemsize for shape in [*shapes, *args])
    return pl.pallas_call(
        kernel,
        out_shape=shapes,
        in_specs=[pl.BlockSpec(memory_space=space)] * len(args),
        out_specs=[pl.BlockSpec(memory_space=pltpu.VMEM)] * len(shapes),
        scratch_shapes=scratch,
        compiler_params=pltpu.CompilerParams(
            vmem_limit_bytes=VMEM_BYTES if space == pltpu.VMEM else FULL_VMEM_BYTES
        ),
        cost_estimate=pl.CostEstimate(flops=flops, bytes_accessed=moved, transcendentals=0),
    )(*args)


def permute(parts, axes):
    count = lax.axis_size(axes)
    return [parts[0]] + [
        lax.ppermute(parts[step], axes, [(source, partner(source, step, count)) for source in range(count)])
        for step in range(1, count)
    ]


def local(voltages, station_flags, filter_taps, kernel_rows, kernel_cols, cell_index):
    _, polars, station_rows, width = voltages.shape
    taps, two_fine, _ = filter_taps.shape
    sub_u, sub_v = kernel_rows.shape[2], kernel_cols.shape[2]
    roles, bands, turns = (lax.axis_size(name) for name in ("role", "band", "turn"))
    row_total = ROWS_DEV * roles * bands * turns
    channels = two_fine // 2 * roles * bands
    frames = width // two_fine - taps + 1
    scale_factor = 4.0 / math.sqrt(channels * sub_u * sub_v) / frames
    pairs_each = polars * frames // turns
    sent = jax.ShapeDtypeStruct((pairs_each * (sub_u + sub_v) + PAD_ROWS, two_fine), jnp.bfloat16)

    flags = station_flags.reshape(1, -1)
    cells = cell_index.reshape(2, -1)
    half = turns // 2

    def spectra(far, after):
        return call(
            functools.partial(spectra_kernel, far, pairs_each),
            [sent] * half,
            (voltages, flags, filter_taps, kernel_rows, kernel_cols, cells, *after),
            space=pltpu.HBM,
            scratch=[
                pltpu.VMEM((station_rows, width), voltages.dtype),
                pltpu.VMEM(filter_taps.shape, filter_taps.dtype),
                pltpu.VMEM(flags.shape, flags.dtype),
                pltpu.VMEM(kernel_rows.shape[2:], kernel_rows.dtype),
                pltpu.VMEM(kernel_cols.shape[2:], kernel_cols.dtype),
                pltpu.VMEM(cells.shape, cells.dtype),
                pltpu.SemaphoreType.DMA((6,)),
            ],
            flops=2 * frames * station_rows * taps * two_fine * two_fine,
        )

    far = spectra(True, [])
    near = spectra(False, far[:1])
    got = permute([*near, *far], "turn")

    place = np.arange(row_total)
    inner, here = place // ROWS_DEV, place % ROWS_DEV
    row_role, row_turn, row_band = inner // (turns * bands), inner // bands % turns, inner % bands
    row = ((row_role * bands + row_band) * turns + row_turn) * ROWS_DEV + here
    parts = call(
        functools.partial(image_kernel, pairs_each, turns),
        [jax.ShapeDtypeStruct((bands * ROWS_DEV, MW), jnp.float32)] * (roles * turns),
        (
            *got,
            jnp.asarray(dft_matrix(row - row_total // 2, sub_u, False)),
            jnp.asarray(dft_matrix(np.arange(MW) - MW // 2, sub_v, True)),
        ),
        scratch=[pltpu.VMEM((row_total, MW), jnp.float32)],
    )
    got = permute(parts, ("role", "turn"))
    parts = call(
        functools.partial(band_kernel, len(got)),
        [jax.ShapeDtypeStruct((ROWS_DEV, MW), jnp.float32)] * bands,
        tuple(got),
        scratch=[pltpu.VMEM((bands * ROWS_DEV, MW), jnp.float32)],
    )
    got = permute(parts, "band")
    return call(
        functools.partial(final_kernel, scale_factor),
        [jax.ShapeDtypeStruct((ROWS_DEV, MW), jnp.float32)],
        tuple(got),
    )[0]


def solution(mesh):
    in_specs = (
        P(("role", "band"), None, "turn", None),
        P("turn"),
        P(),
        P(("role", "band"), None, None, None),
        P(("role", "band"), None, None, None),
        P(None, ("role", "band", "turn"), None),
    )
    out_specs = P(("role", "band", "turn"), None)
    return jax.shard_map(local, mesh=mesh, in_specs=in_specs, out_specs=out_specs, check_vma=False)
```

```python
import functools
import math

import jax
import jax.numpy as jnp
import numpy as np
from jax import lax
from jax.experimental import pallas as pl
from jax.experimental.pallas import tpu as pltpu
from jax.sharding import PartitionSpec as P

NGRID = 4096
MW = 128
ROWS_DEV = 1
DIGIT = 64
PAD_ROWS = 16
VMEM_BYTES = 24 * 1024 * 1024


def weights_kernel(*refs):
    turns = lax.axis_size("turn")
    turn = lax.axis_index("turn")
    rows, cols, *rest = refs[:6]
    weights_ref, digits_ref = refs[-2:]
    both = jnp.concatenate([rows[0, 0], cols[0, 0]], axis=0).astype(jnp.float32)
    lanes = digits_ref.shape[1]
    weights = []
    digits = jnp.zeros((4, lanes), jnp.float32)
    for index, (flag, cell) in enumerate((rest[:2], rest[2:])):
        place = turn ^ index
        stations = flag.shape[1]
        weight = jnp.zeros((both.shape[0], stations), jnp.float32)
        for group in range(turns):
            weight = jnp.where(place == group, both[:, group * stations : (group + 1) * stations], weight)
        weights.append(weight * flag[...].astype(jnp.float32))
        count = cell.shape[1]
        wide = jnp.concatenate([cell[...]] * (lanes // count), axis=1)
        lane = lax.broadcasted_iota(jnp.int32, wide.shape, 1)
        wide = jnp.where((lane >= place * count) & (lane < (place + 1) * count), wide, 0)
        digits = digits + jnp.concatenate([wide // DIGIT, wide % DIGIT], axis=0).astype(jnp.float32)
    weights_ref[...] = jnp.concatenate(weights, axis=1).astype(jnp.bfloat16)
    digits = jnp.concatenate([digits, jnp.zeros((PAD_ROWS - 4, lanes), jnp.float32)], axis=0)
    digits_ref[...] = digits.astype(jnp.bfloat16)


def spectra_kernel(steps, frames_each, own_ref, other_ref, taps_ref, weights_ref, digits_ref, *refs):
    outs = refs[-len(steps) :]
    volts = (own_ref, other_ref)
    turn = lax.axis_index("turn")
    chip, core = turn // 2, turn % 2
    taps, two_fine, _ = taps_ref.shape
    station_rows = own_ref.shape[2]
    cells_rows = weights_ref.shape[0]
    filt = taps_ref[...].reshape(taps * two_fine, two_fine)
    for step, out in zip(steps, outs):
        first = (chip ^ step) * frames_each
        lhs = jnp.concatenate(
            [
                volts[index][0, core, :, pl.ds(pl.multiple_of((first + frame) * two_fine, two_fine), taps * two_fine)]
                for frame in range(frames_each)
                for index in range(2)
            ],
            axis=0,
        )
        spectra = jnp.dot(lhs, filt, preferred_element_type=jnp.float32).astype(jnp.bfloat16)
        for frame in range(frames_each):
            gridded = jnp.dot(
                weights_ref[...],
                spectra[frame * 2 * station_rows : (frame + 1) * 2 * station_rows],
                preferred_element_type=jnp.float32,
            )
            out[frame * cells_rows : (frame + 1) * cells_rows] = gridded.astype(jnp.bfloat16)
        out[frames_each * cells_rows :] = digits_ref[...]


def split_terms(value):
    high = value.astype(jnp.bfloat16)
    return high, (value - high.astype(jnp.float32)).astype(jnp.bfloat16)


def image_kernel(pairs_each, sources, *refs):
    got = refs[:sources]
    row_dft_ref, col_dft_ref, out_ref = refs[sources:]
    fine = got[0].shape[1] // 2
    sub = row_dft_ref.shape[1] // 6
    row_total = out_ref.shape[0]
    total = got[0][...].astype(jnp.float32)
    for source in got[1:]:
        total = total + source[...].astype(jnp.float32)
    digits = total[pairs_each * 2 * sub :]
    cell_u = (digits[0:1, :fine] * DIGIT + digits[2:3, :fine]).astype(jnp.int32)
    cell_v = (digits[1:2, :fine] * DIGIT + digits[3:4, :fine]).astype(jnp.int32)

    def phase(cell, pixel):
        angle = ((cell * pixel) & (NGRID - 1)).astype(jnp.float32) * (2.0 * math.pi / NGRID)
        return jnp.cos(angle), jnp.sin(angle)

    def transform(dft_ref, first, cos, sin):
        held = jnp.concatenate(
            [
                jnp.concatenate(
                    [
                        total[index * 2 * sub + first : index * 2 * sub + first + sub, :fine],
                        total[index * 2 * sub + first : index * 2 * sub + first + sub, fine:],
                    ],
                    axis=0,
                )
                for index in range(pairs_each)
            ],
            axis=1,
        )
        high, low = split_terms(held)
        plain = jnp.dot(
            dft_ref[...].astype(jnp.bfloat16), jnp.concatenate([high, high, low], axis=0), preferred_element_type=jnp.float32
        )
        half = plain.shape[0] // 2
        real, imag = plain[:half], plain[half:]
        cos = jnp.concatenate([cos] * pairs_each, axis=1)
        sin = jnp.concatenate([sin] * pairs_each, axis=1)
        return real * cos - imag * sin, real * sin + imag * cos

    row = lax.broadcasted_iota(jnp.int32, (row_total, fine), 0)
    row_real, row_imag = transform(row_dft_ref, 0, *phase(cell_u, row - row_total // 2))
    col = lax.broadcasted_iota(jnp.int32, (MW, fine), 0)
    col_real, col_imag = transform(col_dft_ref, sub, *phase(cell_v, col - MW // 2))
    left_high, left_low = split_terms(jnp.concatenate([row_real, -row_imag], axis=1))
    right_high, right_low = split_terms(jnp.concatenate([col_real, col_imag], axis=1))

    def product(left, right):
        return lax.dot_general(left, right, (((1,), (1,)), ((), ())), preferred_element_type=jnp.float32)

    out_ref[...] = product(left_high, right_high) + (
        product(left_high, right_low) + product(left_low, right_high)
    )


def final_kernel(scale_factor, in_ref, out_ref):
    out_ref[...] = jnp.sum(in_ref[...], axis=0) * scale_factor


def dft_matrix(pixel, cells, conjugate):
    angle = 2.0 * np.pi / NGRID * np.outer(pixel, np.arange(cells))
    cos, sin = np.cos(angle), np.sin(angle)
    sign = -1.0 if conjugate else 1.0
    whole = np.block([[cos, -sign * sin], [sin, sign * cos]]).astype(np.float32)
    high = whole.astype(jnp.bfloat16)
    low = (whole - high.astype(np.float32)).astype(jnp.bfloat16)
    return np.concatenate([high, low, high], axis=1).astype(np.float32)


def call(kernel, shapes, args, flops=0):
    moved = sum(math.prod(shape.shape) * shape.dtype.itemsize for shape in [*shapes, *args])
    return pl.pallas_call(
        kernel,
        out_shape=shapes,
        in_specs=[pl.BlockSpec(memory_space=pltpu.VMEM)] * len(args),
        out_specs=[pl.BlockSpec(memory_space=pltpu.VMEM)] * len(shapes),
        compiler_params=pltpu.CompilerParams(vmem_limit_bytes=VMEM_BYTES),
        cost_estimate=pl.CostEstimate(flops=flops, bytes_accessed=moved, transcendentals=0),
    )(*args)


def local(voltages, station_flags, filter_taps, kernel_rows, kernel_cols, cell_index):
    _, polars, station_rows, width = voltages.shape
    taps, two_fine, _ = filter_taps.shape
    sub_u, sub_v = kernel_rows.shape[2], kernel_cols.shape[2]
    everyone = ("role", "band", "turn")
    turns = lax.axis_size("turn")
    chips = turns // polars
    row_total = ROWS_DEV * lax.axis_size(everyone)
    channels = two_fine // 2 * lax.axis_size("role") * lax.axis_size("band")
    frames = width // two_fine - taps + 1
    scale_factor = 4.0 / math.sqrt(channels * sub_u * sub_v) / frames
    frames_each = frames // chips

    own = [voltages, station_flags.reshape(1, -1), cell_index.reshape(2, -1)]
    swap = [(source, source ^ 1) for source in range(turns)]
    other = [lax.ppermute(value, "turn", swap) for value in own]

    small = (kernel_rows, kernel_cols, *own[1:], *other[1:])
    shapes = [
        jax.ShapeDtypeStruct((sub_u + sub_v, 2 * station_rows), jnp.bfloat16),
        jax.ShapeDtypeStruct((PAD_ROWS, two_fine), jnp.bfloat16),
    ]
    prepared = call(
        weights_kernel,
        shapes,
        (*small, filter_taps, voltages),
    )

    def spectra(steps, after):
        return call(
            functools.partial(spectra_kernel, steps, frames_each),
            [jax.ShapeDtypeStruct((frames_each * (sub_u + sub_v) + PAD_ROWS, two_fine), jnp.bfloat16)] * len(steps),
            (voltages, other[0], filter_taps, *prepared, *after),
            flops=4 * len(steps) * frames_each * station_rows * taps * two_fine * two_fine,
        )

    far = spectra(range(1, chips), [])
    near = spectra([0], far[:1])
    got = [*near] + [
        lax.ppermute(part, "turn", [(source, source ^ (step * polars)) for source in range(turns)])
        for step, part in enumerate(far, 1)
    ]
    part = call(
        functools.partial(image_kernel, frames_each, len(got)),
        [jax.ShapeDtypeStruct((row_total, MW), jnp.float32)],
        (
            *got,
            jnp.asarray(dft_matrix(np.arange(row_total) - row_total // 2, sub_u, False)),
            jnp.asarray(dft_matrix(np.arange(MW) - MW // 2, sub_v, True)),
        ),
    )[0]
    rows = lax.all_to_all(part, everyone, split_axis=0, concat_axis=0, tiled=True)
    return call(
        functools.partial(final_kernel, scale_factor),
        [jax.ShapeDtypeStruct((ROWS_DEV, MW), jnp.float32)],
        (rows.reshape(-1, ROWS_DEV, MW),),
    )[0]


def solution(mesh):
    in_specs = (
        P(("role", "band"), None, "turn", None),
        P("turn"),
        P(),
        P(("role", "band"), None, None, None),
        P(("role", "band"), None, None, None),
        P(None, ("role", "band", "turn"), None),
    )
    out_specs = P(("role", "band", "turn"), None)
    return jax.shard_map(local, mesh=mesh, in_specs=in_specs, out_specs=out_specs, check_vma=False)
```

```python
import functools
import math

import jax
import jax.numpy as jnp
import numpy as np
from jax import lax
from jax.experimental import pallas as pl
from jax.experimental.pallas import tpu as pltpu
from jax.sharding import PartitionSpec as P

NGRID = 4096
MW = 128
ROWS_DEV = 1
DIGIT = 64
PAD_ROWS = 16
VMEM_BYTES = 24 * 1024 * 1024


def digits_kernel(own_ref, other_ref, out_ref):
    turn = lax.axis_index("turn")
    lanes = out_ref.shape[1]
    digits = jnp.zeros((4, lanes), jnp.float32)
    for index, cell in enumerate((own_ref[...], other_ref[...])):
        place = turn ^ index
        count = cell.shape[1]
        wide = jnp.concatenate([cell] * (lanes // count), axis=1)
        lane = lax.broadcasted_iota(jnp.int32, wide.shape, 1)
        wide = jnp.where((lane >= place * count) & (lane < (place + 1) * count), wide, 0)
        digits = digits + jnp.concatenate([wide // DIGIT, wide % DIGIT], axis=0).astype(jnp.float32)
    digits = jnp.concatenate([digits, jnp.zeros((PAD_ROWS - 4, lanes), jnp.float32)], axis=0)
    out_ref[...] = digits.astype(jnp.bfloat16)


def gridding_weights(rows_ref, cols_ref, flag_refs):
    turns = lax.axis_size("turn")
    turn = lax.axis_index("turn")
    both = jnp.concatenate([rows_ref[0, 0], cols_ref[0, 0]], axis=0).astype(jnp.float32)
    weights = []
    for index, flag in enumerate(flag_refs):
        stations = flag.shape[1]
        weight = jnp.zeros((both.shape[0], stations), jnp.float32)
        for group in range(turns):
            piece = both[:, group * stations : (group + 1) * stations]
            weight = jnp.where(turn ^ index == group, piece, weight)
        weights.append(weight * flag[...].astype(jnp.float32))
    return jnp.concatenate(weights, axis=1).astype(jnp.bfloat16)


def spectra_kernel(steps, frames_each, own_ref, other_ref, taps_ref, digits_ref, rows_ref, cols_ref, *refs):
    outs = refs[-len(steps) :]
    volts = (own_ref, other_ref)
    turn = lax.axis_index("turn")
    chip, core = turn // 2, turn % 2
    taps, two_fine, _ = taps_ref.shape
    station_rows = own_ref.shape[2]
    weights = gridding_weights(rows_ref, cols_ref, refs[:2])
    cells_rows = weights.shape[0]
    filt = taps_ref[...].reshape(taps * two_fine, two_fine)
    for step, out in zip(steps, outs):
        first = (chip ^ step) * frames_each
        lhs = jnp.concatenate(
            [
                volts[index][0, core, :, pl.ds(pl.multiple_of((first + frame) * two_fine, two_fine), taps * two_fine)]
                for frame in range(frames_each)
                for index in range(2)
            ],
            axis=0,
        )
        spectra = jnp.dot(lhs, filt, preferred_element_type=jnp.float32).astype(jnp.bfloat16)
        for frame in range(frames_each):
            gridded = jnp.dot(
                weights,
                spectra[frame * 2 * station_rows : (frame + 1) * 2 * station_rows],
                preferred_element_type=jnp.float32,
            )
            out[frame * cells_rows : (frame + 1) * cells_rows] = gridded.astype(jnp.bfloat16)
        out[frames_each * cells_rows :] = digits_ref[...]


def split_terms(value):
    high = value.astype(jnp.bfloat16)
    return high, (value - high.astype(jnp.float32)).astype(jnp.bfloat16)


def image_kernel(pairs_each, sources, *refs):
    got = refs[:sources]
    row_dft_ref, col_dft_ref, out_ref = refs[sources:]
    fine = got[0].shape[1] // 2
    sub = row_dft_ref.shape[1] // 6
    row_total = out_ref.shape[0]
    total = got[0][...].astype(jnp.float32)
    for source in got[1:]:
        total = total + source[...].astype(jnp.float32)
    digits = total[pairs_each * 2 * sub :]
    cell_u = (digits[0:1, :fine] * DIGIT + digits[2:3, :fine]).astype(jnp.int32)
    cell_v = (digits[1:2, :fine] * DIGIT + digits[3:4, :fine]).astype(jnp.int32)

    def phase(cell, pixel):
        angle = ((cell * pixel) & (NGRID - 1)).astype(jnp.float32) * (2.0 * math.pi / NGRID)
        return jnp.cos(angle), jnp.sin(angle)

    def transform(dft_ref, first, cos, sin):
        held = jnp.concatenate(
            [
                jnp.concatenate(
                    [
                        total[index * 2 * sub + first : index * 2 * sub + first + sub, :fine],
                        total[index * 2 * sub + first : index * 2 * sub + first + sub, fine:],
                    ],
                    axis=0,
                )
                for index in range(pairs_each)
            ],
            axis=1,
        )
        high, low = split_terms(held)
        plain = jnp.dot(
            dft_ref[...].astype(jnp.bfloat16), jnp.concatenate([high, high, low], axis=0), preferred_element_type=jnp.float32
        )
        half = plain.shape[0] // 2
        real, imag = plain[:half], plain[half:]
        cos = jnp.concatenate([cos] * pairs_each, axis=1)
        sin = jnp.concatenate([sin] * pairs_each, axis=1)
        return real * cos - imag * sin, real * sin + imag * cos

    row = lax.broadcasted_iota(jnp.int32, (row_total, fine), 0)
    row_real, row_imag = transform(row_dft_ref, 0, *phase(cell_u, row - row_total // 2))
    col = lax.broadcasted_iota(jnp.int32, (MW, fine), 0)
    col_real, col_imag = transform(col_dft_ref, sub, *phase(cell_v, col - MW // 2))
    left_high, left_low = split_terms(jnp.concatenate([row_real, -row_imag], axis=1))
    right_high, right_low = split_terms(jnp.concatenate([col_real, col_imag], axis=1))

    def product(left, right):
        return lax.dot_general(left, right, (((1,), (1,)), ((), ())), preferred_element_type=jnp.float32)

    out_ref[...] = product(left_high, right_high) + (
        product(left_high, right_low) + product(left_low, right_high)
    )


def final_kernel(scale_factor, in_ref, out_ref):
    out_ref[...] = jnp.sum(in_ref[...], axis=0) * scale_factor


def dft_matrix(pixel, cells, conjugate):
    angle = 2.0 * np.pi / NGRID * np.outer(pixel, np.arange(cells))
    cos, sin = np.cos(angle), np.sin(angle)
    sign = -1.0 if conjugate else 1.0
    whole = np.block([[cos, -sign * sin], [sin, sign * cos]]).astype(np.float32)
    high = whole.astype(jnp.bfloat16)
    low = (whole - high.astype(np.float32)).astype(jnp.bfloat16)
    return np.concatenate([high, low, high], axis=1).astype(np.float32)


def call(kernel, shapes, args, flops=0):
    moved = sum(math.prod(shape.shape) * shape.dtype.itemsize for shape in [*shapes, *args])
    return pl.pallas_call(
        kernel,
        out_shape=shapes,
        in_specs=[pl.BlockSpec(memory_space=pltpu.VMEM)] * len(args),
        out_specs=[pl.BlockSpec(memory_space=pltpu.VMEM)] * len(shapes),
        compiler_params=pltpu.CompilerParams(vmem_limit_bytes=VMEM_BYTES),
        cost_estimate=pl.CostEstimate(flops=flops, bytes_accessed=moved, transcendentals=0),
    )(*args)


def local(voltages, station_flags, filter_taps, kernel_rows, kernel_cols, cell_index):
    _, polars, station_rows, width = voltages.shape
    taps, two_fine, _ = filter_taps.shape
    sub_u, sub_v = kernel_rows.shape[2], kernel_cols.shape[2]
    everyone = ("role", "band", "turn")
    turns = lax.axis_size("turn")
    chips = turns // polars
    row_total = ROWS_DEV * lax.axis_size(everyone)
    channels = two_fine // 2 * lax.axis_size("role") * lax.axis_size("band")
    frames = width // two_fine - taps + 1
    scale_factor = 4.0 / math.sqrt(channels * sub_u * sub_v) / frames
    frames_each = frames // chips

    own = [voltages, station_flags.reshape(1, -1), cell_index.reshape(2, -1)]
    swap = [(source, source ^ 1) for source in range(turns)]
    other = [lax.ppermute(value, "turn", swap) for value in own]

    digits = call(
        digits_kernel,
        [jax.ShapeDtypeStruct((PAD_ROWS, two_fine), jnp.bfloat16)],
        (own[2], other[2]),
        flops=2 * voltages.size * two_fine * taps,
    )[0]

    def spectra(steps, after):
        return call(
            functools.partial(spectra_kernel, steps, frames_each),
            [jax.ShapeDtypeStruct((frames_each * (sub_u + sub_v) + PAD_ROWS, two_fine), jnp.bfloat16)] * len(steps),
            (voltages, other[0], filter_taps, digits, kernel_rows, kernel_cols, own[1], other[1], *after),
            flops=4 * len(steps) * frames_each * station_rows * taps * two_fine * two_fine,
        )

    far = spectra(range(1, chips), [])
    near = spectra([0], far[:1])
    got = [*near] + [
        lax.ppermute(part, "turn", [(source, source ^ (step * polars)) for source in range(turns)])
        for step, part in enumerate(far, 1)
    ]
    part = call(
        functools.partial(image_kernel, frames_each, len(got)),
        [jax.ShapeDtypeStruct((row_total, MW), jnp.float32)],
        (
            *got,
            jnp.asarray(dft_matrix(np.arange(row_total) - row_total // 2, sub_u, False)),
            jnp.asarray(dft_matrix(np.arange(MW) - MW // 2, sub_v, True)),
        ),
    )[0]
    rows = lax.all_to_all(part, everyone, split_axis=0, concat_axis=0, tiled=True)
    return call(
        functools.partial(final_kernel, scale_factor),
        [jax.ShapeDtypeStruct((ROWS_DEV, MW), jnp.float32)],
        (rows.reshape(-1, ROWS_DEV, MW),),
    )[0]


def solution(mesh):
    in_specs = (
        P(("role", "band"), None, "turn", None),
        P("turn"),
        P(),
        P(("role", "band"), None, None, None),
        P(("role", "band"), None, None, None),
        P(None, ("role", "band", "turn"), None),
    )
    out_specs = P(("role", "band", "turn"), None)
    return jax.shard_map(local, mesh=mesh, in_specs=in_specs, out_specs=out_specs, check_vma=False)
```

```python
import functools
import math

import jax
import jax.numpy as jnp
import numpy as np
from jax import lax
from jax.experimental import pallas as pl
from jax.experimental.pallas import tpu as pltpu
from jax.sharding import PartitionSpec as P

NGRID = 4096
MW = 128
ROWS_DEV = 1
DIGIT = 64
PAD_ROWS = 16
VMEM_BYTES = 24 * 1024 * 1024
GATHER_BYTES = 1024 * 1024


def digits_kernel(own_ref, other_ref, out_ref):
    turn = lax.axis_index("turn")
    lanes = out_ref.shape[1]
    digits = jnp.zeros((4, lanes), jnp.float32)
    for index, cell in enumerate((own_ref[...], other_ref[...])):
        place = turn ^ index
        count = cell.shape[1]
        wide = jnp.concatenate([cell] * (lanes // count), axis=1)
        lane = lax.broadcasted_iota(jnp.int32, wide.shape, 1)
        wide = jnp.where((lane >= place * count) & (lane < (place + 1) * count), wide, 0)
        digits = digits + jnp.concatenate([wide // DIGIT, wide % DIGIT], axis=0).astype(jnp.float32)
    digits = jnp.concatenate([digits, jnp.zeros((PAD_ROWS - 4, lanes), jnp.float32)], axis=0)
    out_ref[...] = digits.astype(jnp.bfloat16)


def gridding_weights(rows_ref, cols_ref, flag_refs):
    turns = lax.axis_size("turn")
    turn = lax.axis_index("turn")
    both = jnp.concatenate([rows_ref[0, 0], cols_ref[0, 0]], axis=0).astype(jnp.float32)
    weights = []
    for index, flag in enumerate(flag_refs):
        stations = flag.shape[1]
        weight = jnp.zeros((both.shape[0], stations), jnp.float32)
        for group in range(turns):
            piece = both[:, group * stations : (group + 1) * stations]
            weight = jnp.where(turn ^ index == group, piece, weight)
        weights.append(weight * flag[...].astype(jnp.float32))
    return jnp.concatenate(weights, axis=1).astype(jnp.bfloat16)


def spectra_kernel(steps, frames_each, own_ref, other_ref, taps_ref, digits_ref, rows_ref, cols_ref, *refs):
    outs = refs[-len(steps) :]
    volts = (own_ref, other_ref)
    turn = lax.axis_index("turn")
    chip, core = turn // 2, turn % 2
    taps, two_fine, _ = taps_ref.shape
    station_rows = own_ref.shape[2]
    weights = gridding_weights(rows_ref, cols_ref, refs[:2])
    cells_rows = weights.shape[0]
    filt = taps_ref[...].reshape(taps * two_fine, two_fine)
    for step, out in zip(steps, outs):
        first = (chip ^ step) * frames_each
        lhs = jnp.concatenate(
            [
                volts[index][0, core, :, pl.ds(pl.multiple_of((first + frame) * two_fine, two_fine), taps * two_fine)]
                for frame in range(frames_each)
                for index in range(2)
            ],
            axis=0,
        )
        spectra = jnp.dot(lhs, filt, preferred_element_type=jnp.float32).astype(jnp.bfloat16)
        for frame in range(frames_each):
            gridded = jnp.dot(
                weights,
                spectra[frame * 2 * station_rows : (frame + 1) * 2 * station_rows],
                preferred_element_type=jnp.float32,
            )
            out[frame * cells_rows : (frame + 1) * cells_rows] = gridded.astype(jnp.bfloat16)
        out[frames_each * cells_rows :] = digits_ref[...]


def split_terms(value):
    high = value.astype(jnp.bfloat16)
    return high, (value - high.astype(jnp.float32)).astype(jnp.bfloat16)


def image_kernel(pairs_each, sources, *refs):
    got = refs[:sources]
    row_dft_ref, col_dft_ref, out_ref = refs[sources:]
    fine = got[0].shape[1] // 2
    sub = row_dft_ref.shape[1] // 6
    row_total = out_ref.shape[0]
    total = got[0][...].astype(jnp.float32)
    for source in got[1:]:
        total = total + source[...].astype(jnp.float32)
    digits = total[pairs_each * 2 * sub :]
    cell_u = (digits[0:1, :fine] * DIGIT + digits[2:3, :fine]).astype(jnp.int32)
    cell_v = (digits[1:2, :fine] * DIGIT + digits[3:4, :fine]).astype(jnp.int32)

    def phase(cell, pixel):
        angle = ((cell * pixel) & (NGRID - 1)).astype(jnp.float32) * (2.0 * math.pi / NGRID)
        return jnp.cos(angle), jnp.sin(angle)

    def transform(dft_ref, first, cos, sin):
        held = jnp.concatenate(
            [
                jnp.concatenate(
                    [
                        total[index * 2 * sub + first : index * 2 * sub + first + sub, :fine],
                        total[index * 2 * sub + first : index * 2 * sub + first + sub, fine:],
                    ],
                    axis=0,
                )
                for index in range(pairs_each)
            ],
            axis=1,
        )
        high, low = split_terms(held)
        plain = jnp.dot(
            dft_ref[...].astype(jnp.bfloat16), jnp.concatenate([high, high, low], axis=0), preferred_element_type=jnp.float32
        )
        half = plain.shape[0] // 2
        real, imag = plain[:half], plain[half:]
        cos = jnp.concatenate([cos] * pairs_each, axis=1)
        sin = jnp.concatenate([sin] * pairs_each, axis=1)
        return real * cos - imag * sin, real * sin + imag * cos

    row = lax.broadcasted_iota(jnp.int32, (row_total, fine), 0)
    row_real, row_imag = transform(row_dft_ref, 0, *phase(cell_u, row - row_total // 2))
    col = lax.broadcasted_iota(jnp.int32, (MW, fine), 0)
    col_real, col_imag = transform(col_dft_ref, sub, *phase(cell_v, col - MW // 2))
    left_high, left_low = split_terms(jnp.concatenate([row_real, -row_imag], axis=1))
    right_high, right_low = split_terms(jnp.concatenate([col_real, col_imag], axis=1))

    def product(left, right):
        return lax.dot_general(left, right, (((1,), (1,)), ((), ())), preferred_element_type=jnp.float32)

    out_ref[...] = product(left_high, right_high) + (
        product(left_high, right_low) + product(left_low, right_high)
    )


def final_kernel(scale_factor, in_ref, out_ref):
    if in_ref.shape[1] == ROWS_DEV:
        out_ref[...] = jnp.sum(in_ref[...], axis=0) * scale_factor
        return
    me = (lax.axis_index("role") * lax.axis_size("band") + lax.axis_index("band")) * lax.axis_size("turn")
    me = me + lax.axis_index("turn")
    out_ref[...] = jnp.sum(in_ref[:, pl.ds(me * ROWS_DEV, ROWS_DEV)], axis=0) * scale_factor


def dft_matrix(pixel, cells, conjugate):
    angle = 2.0 * np.pi / NGRID * np.outer(pixel, np.arange(cells))
    cos, sin = np.cos(angle), np.sin(angle)
    sign = -1.0 if conjugate else 1.0
    whole = np.block([[cos, -sign * sin], [sin, sign * cos]]).astype(np.float32)
    high = whole.astype(jnp.bfloat16)
    low = (whole - high.astype(np.float32)).astype(jnp.bfloat16)
    return np.concatenate([high, low, high], axis=1).astype(np.float32)


def call(kernel, shapes, args, flops=0):
    moved = sum(math.prod(shape.shape) * shape.dtype.itemsize for shape in [*shapes, *args])
    return pl.pallas_call(
        kernel,
        out_shape=shapes,
        in_specs=[pl.BlockSpec(memory_space=pltpu.VMEM)] * len(args),
        out_specs=[pl.BlockSpec(memory_space=pltpu.VMEM)] * len(shapes),
        compiler_params=pltpu.CompilerParams(vmem_limit_bytes=VMEM_BYTES),
        cost_estimate=pl.CostEstimate(flops=flops, bytes_accessed=moved, transcendentals=0),
    )(*args)


def local(voltages, station_flags, filter_taps, kernel_rows, kernel_cols, cell_index):
    _, polars, station_rows, width = voltages.shape
    taps, two_fine, _ = filter_taps.shape
    sub_u, sub_v = kernel_rows.shape[2], kernel_cols.shape[2]
    everyone = ("role", "band", "turn")
    turns = lax.axis_size("turn")
    chips = turns // polars
    row_total = ROWS_DEV * lax.axis_size(everyone)
    channels = two_fine // 2 * lax.axis_size("role") * lax.axis_size("band")
    frames = width // two_fine - taps + 1
    scale_factor = 4.0 / math.sqrt(channels * sub_u * sub_v) / frames
    frames_each = frames // chips

    own = [voltages, station_flags.reshape(1, -1), cell_index.reshape(2, -1)]
    swap = [(source, source ^ 1) for source in range(turns)]
    other = [lax.ppermute(value, "turn", swap) for value in own]

    digits = call(
        digits_kernel,
        [jax.ShapeDtypeStruct((PAD_ROWS, two_fine), jnp.bfloat16)],
        (own[2], other[2]),
        flops=2 * voltages.size * two_fine * taps,
    )[0]

    def spectra(steps, after):
        return call(
            functools.partial(spectra_kernel, steps, frames_each),
            [jax.ShapeDtypeStruct((frames_each * (sub_u + sub_v) + PAD_ROWS, two_fine), jnp.bfloat16)] * len(steps),
            (voltages, other[0], filter_taps, digits, kernel_rows, kernel_cols, own[1], other[1], *after),
            flops=4 * len(steps) * frames_each * station_rows * taps * two_fine * two_fine,
        )

    far = spectra(range(1, chips), [])
    near = spectra([0], far[:1])
    got = [*near] + [
        lax.ppermute(part, "turn", [(source, source ^ (step * polars)) for source in range(turns)])
        for step, part in enumerate(far, 1)
    ]
    part = call(
        functools.partial(image_kernel, frames_each, len(got)),
        [jax.ShapeDtypeStruct((row_total, MW), jnp.float32)],
        (
            *got,
            jnp.asarray(dft_matrix(np.arange(row_total) - row_total // 2, sub_u, False)),
            jnp.asarray(dft_matrix(np.arange(MW) - MW // 2, sub_v, True)),
        ),
    )[0]
    if row_total * part.size * part.dtype.itemsize <= GATHER_BYTES:
        rows = lax.all_gather(part, everyone)
    else:
        rows = lax.all_to_all(part, everyone, split_axis=0, concat_axis=0, tiled=True).reshape(-1, ROWS_DEV, MW)
    return call(
        functools.partial(final_kernel, scale_factor),
        [jax.ShapeDtypeStruct((ROWS_DEV, MW), jnp.float32)],
        (rows,),
    )[0]


def solution(mesh):
    in_specs = (
        P(("role", "band"), None, "turn", None),
        P("turn"),
        P(),
        P(("role", "band"), None, None, None),
        P(("role", "band"), None, None, None),
        P(None, ("role", "band", "turn"), None),
    )
    out_specs = P(("role", "band", "turn"), None)
    return jax.shard_map(local, mesh=mesh, in_specs=in_specs, out_specs=out_specs, check_vma=False)
```

```python
import functools
import math

import jax
import jax.numpy as jnp
import numpy as np
from jax import lax
from jax.experimental import pallas as pl
from jax.experimental.pallas import tpu as pltpu
from jax.sharding import Mesh
from jax.sharding import PartitionSpec as P

NGRID = 4096
MW = 128
ROWS_DEV = 1
DIGIT = 64
PAD_ROWS = 16
CORES = 2
TURN = ("chip", "core")
PEERS = ("role", "band", "chip")
VMEM_BYTES = 24 * 1024 * 1024


def digits_kernel(own_ref, other_ref, out_ref):
    turn = lax.axis_index(TURN)
    lanes = out_ref.shape[1]
    digits = jnp.zeros((4, lanes), jnp.float32)
    for index, cell in enumerate((own_ref[...], other_ref[...])):
        place = turn ^ index
        count = cell.shape[1]
        wide = jnp.concatenate([cell] * (lanes // count), axis=1)
        lane = lax.broadcasted_iota(jnp.int32, wide.shape, 1)
        wide = jnp.where((lane >= place * count) & (lane < (place + 1) * count), wide, 0)
        digits = digits + jnp.concatenate([wide // DIGIT, wide % DIGIT], axis=0).astype(jnp.float32)
    digits = jnp.concatenate([digits, jnp.zeros((PAD_ROWS - 4, lanes), jnp.float32)], axis=0)
    out_ref[...] = digits.astype(jnp.bfloat16)


def gridding_weights(rows_ref, cols_ref, flag_refs):
    turns = lax.axis_size(TURN)
    turn = lax.axis_index(TURN)
    both = jnp.concatenate([rows_ref[0, 0], cols_ref[0, 0]], axis=0).astype(jnp.float32)
    weights = []
    for index, flag in enumerate(flag_refs):
        stations = flag.shape[1]
        weight = jnp.zeros((both.shape[0], stations), jnp.float32)
        for group in range(turns):
            piece = both[:, group * stations : (group + 1) * stations]
            weight = jnp.where(turn ^ index == group, piece, weight)
        weights.append(weight * flag[...].astype(jnp.float32))
    return jnp.concatenate(weights, axis=1).astype(jnp.bfloat16)


def spectra_kernel(steps, frames_each, own_ref, other_ref, taps_ref, digits_ref, rows_ref, cols_ref, *refs):
    outs = refs[-len(steps) :]
    volts = (own_ref, other_ref)
    chip, core = lax.axis_index("chip"), lax.axis_index("core")
    taps, two_fine, _ = taps_ref.shape
    station_rows = own_ref.shape[2]
    weights = gridding_weights(rows_ref, cols_ref, refs[:2])
    cells_rows = weights.shape[0]
    filt = taps_ref[...].reshape(taps * two_fine, two_fine)
    for step, out in zip(steps, outs):
        first = (chip ^ step) * frames_each
        lhs = jnp.concatenate(
            [
                volts[index][0, core, :, pl.ds(pl.multiple_of((first + frame) * two_fine, two_fine), taps * two_fine)]
                for frame in range(frames_each)
                for index in range(2)
            ],
            axis=0,
        )
        spectra = jnp.dot(lhs, filt, preferred_element_type=jnp.float32).astype(jnp.bfloat16)
        for frame in range(frames_each):
            gridded = jnp.dot(
                weights,
                spectra[frame * 2 * station_rows : (frame + 1) * 2 * station_rows],
                preferred_element_type=jnp.float32,
            )
            out[frame * cells_rows : (frame + 1) * cells_rows] = gridded.astype(jnp.bfloat16)
        out[frames_each * cells_rows :] = digits_ref[...]


def split_terms(value):
    high = value.astype(jnp.bfloat16)
    return high, (value - high.astype(jnp.float32)).astype(jnp.bfloat16)


def row_order(place, row_total):
    owners = row_total // ROWS_DEV // CORES
    owner, here = place // ROWS_DEV, place % ROWS_DEV
    return (owner % owners * CORES + owner // owners) * ROWS_DEV + here


def image_kernel(pairs_each, sources, *refs):
    got = refs[:sources]
    row_dft_ref, col_dft_ref, kept_ref, given_ref, held_ref = refs[sources:]
    fine = got[0].shape[1] // 2
    sub = row_dft_ref.shape[1] // 6
    row_total = held_ref.shape[0]
    total = got[0][...].astype(jnp.float32)
    for source in got[1:]:
        total = total + source[...].astype(jnp.float32)
    digits = total[pairs_each * 2 * sub :]
    cell_u = (digits[0:1, :fine] * DIGIT + digits[2:3, :fine]).astype(jnp.int32)
    cell_v = (digits[1:2, :fine] * DIGIT + digits[3:4, :fine]).astype(jnp.int32)

    def phase(cell, pixel):
        quarter = NGRID // 4
        turned = (cell * pixel) & (NGRID - 1)
        quadrant = (turned + quarter // 2) // quarter
        angle = (turned - quadrant * quarter).astype(jnp.float32) * (2.0 * math.pi / NGRID)
        square = angle * angle
        sine = angle * (1 + square * (-1 / 6 + square * (1 / 120 + square * (-1 / 5040 + square * (1 / 362880)))))
        cosine = 1 + square * (-1 / 2 + square * (1 / 24 + square * (-1 / 720 + square * (1 / 40320))))
        odd = (quadrant & 1) == 1
        real = jnp.where(odd, sine, cosine)
        imag = jnp.where(odd, cosine, sine)
        return (
            jnp.where(((quadrant + 1) & 2) == 2, -real, real),
            jnp.where((quadrant & 2) == 2, -imag, imag),
        )

    def transform(dft_ref, first, cos, sin):
        held = jnp.concatenate(
            [
                jnp.concatenate(
                    [
                        total[index * 2 * sub + first : index * 2 * sub + first + sub, :fine],
                        total[index * 2 * sub + first : index * 2 * sub + first + sub, fine:],
                    ],
                    axis=0,
                )
                for index in range(pairs_each)
            ],
            axis=1,
        )
        high, low = split_terms(held)
        plain = jnp.dot(
            dft_ref[...].astype(jnp.bfloat16), jnp.concatenate([high, high, low], axis=0), preferred_element_type=jnp.float32
        )
        half = plain.shape[0] // 2
        real, imag = plain[:half], plain[half:]
        cos = jnp.concatenate([cos] * pairs_each, axis=1)
        sin = jnp.concatenate([sin] * pairs_each, axis=1)
        return real * cos - imag * sin, real * sin + imag * cos

    row = row_order(lax.broadcasted_iota(jnp.int32, (row_total, fine), 0), row_total)
    row_real, row_imag = transform(row_dft_ref, 0, *phase(cell_u, row - row_total // 2))
    col = lax.broadcasted_iota(jnp.int32, (MW, fine), 0)
    col_real, col_imag = transform(col_dft_ref, sub, *phase(cell_v, col - MW // 2))
    left_high, left_low = split_terms(jnp.concatenate([row_real, -row_imag], axis=1))
    right_high, right_low = split_terms(jnp.concatenate([col_real, col_imag], axis=1))

    def product(left, right):
        return lax.dot_general(left, right, (((1,), (1,)), ((), ())), preferred_element_type=jnp.float32)

    held_ref[...] = product(left_high, right_high) + (
        product(left_high, right_low) + product(left_low, right_high)
    )
    core, half = lax.axis_index("core"), row_total // CORES
    kept_ref[...] = held_ref[pl.ds(core * half, half)]
    given_ref[...] = held_ref[pl.ds((1 - core) * half, half)]


def add_kernel(left_ref, right_ref, out_ref):
    out_ref[...] = left_ref[...] + right_ref[...]


def final_kernel(scale_factor, in_ref, out_ref):
    out_ref[...] = jnp.sum(in_ref[...], axis=0) * scale_factor


def dft_matrix(pixel, cells, conjugate):
    angle = 2.0 * np.pi / NGRID * np.outer(pixel, np.arange(cells))
    cos, sin = np.cos(angle), np.sin(angle)
    sign = -1.0 if conjugate else 1.0
    whole = np.block([[cos, -sign * sin], [sin, sign * cos]]).astype(np.float32)
    high = whole.astype(jnp.bfloat16)
    low = (whole - high.astype(np.float32)).astype(jnp.bfloat16)
    return np.concatenate([high, low, high], axis=1).astype(np.float32)


def call(kernel, shapes, args, scratch=(), flops=0):
    moved = sum(math.prod(shape.shape) * shape.dtype.itemsize for shape in [*shapes, *args])
    return pl.pallas_call(
        kernel,
        out_shape=shapes,
        in_specs=[pl.BlockSpec(memory_space=pltpu.VMEM)] * len(args),
        out_specs=[pl.BlockSpec(memory_space=pltpu.VMEM)] * len(shapes),
        scratch_shapes=scratch,
        compiler_params=pltpu.CompilerParams(vmem_limit_bytes=VMEM_BYTES),
        cost_estimate=pl.CostEstimate(flops=flops, bytes_accessed=moved, transcendentals=0),
    )(*args)


def local(voltages, station_flags, filter_taps, kernel_rows, kernel_cols, cell_index):
    station_rows, width = voltages.shape[2:]
    taps, two_fine, _ = filter_taps.shape
    sub_u, sub_v = kernel_rows.shape[2], kernel_cols.shape[2]
    turns, chips = lax.axis_size(TURN), lax.axis_size("chip")
    row_total = ROWS_DEV * lax.axis_size(PEERS) * CORES
    channels = two_fine // 2 * lax.axis_size("role") * lax.axis_size("band")
    frames = width // two_fine - taps + 1
    scale_factor = 4.0 / math.sqrt(channels * sub_u * sub_v) / frames
    frames_each = frames // chips

    own = [voltages, station_flags.reshape(1, -1), cell_index.reshape(2, -1)]
    swap = [(core, 1 - core) for core in range(CORES)]
    other = [lax.ppermute(value, "core", swap) for value in own]

    digits = call(
        digits_kernel,
        [jax.ShapeDtypeStruct((PAD_ROWS, two_fine), jnp.bfloat16)],
        (own[2], other[2]),
        flops=2 * voltages.size * two_fine * taps,
    )[0]

    def spectra(steps, after):
        return call(
            functools.partial(spectra_kernel, steps, frames_each),
            [jax.ShapeDtypeStruct((frames_each * (sub_u + sub_v) + PAD_ROWS, two_fine), jnp.bfloat16)] * len(steps),
            (voltages, other[0], filter_taps, digits, kernel_rows, kernel_cols, own[1], other[1], *after),
            flops=4 * len(steps) * frames_each * station_rows * taps * two_fine * two_fine,
        )

    far = spectra(range(1, chips), [])
    near = spectra([0], far[:1])
    got = [*near] + [
        lax.ppermute(part, "chip", [(source, source ^ step) for source in range(chips)])
        for step, part in enumerate(far, 1)
    ]
    pixel = row_order(np.arange(row_total), row_total) - row_total // 2
    half = jax.ShapeDtypeStruct((row_total // CORES, MW), jnp.float32)
    kept, given = call(
        functools.partial(image_kernel, frames_each, len(got)),
        [half, half],
        (
            *got,
            jnp.asarray(dft_matrix(pixel, sub_u, False)),
            jnp.asarray(dft_matrix(np.arange(MW) - MW // 2, sub_v, True)),
        ),
        scratch=[pltpu.VMEM((row_total, MW), jnp.float32)],
    )
    part = call(add_kernel, [half], (kept, lax.ppermute(given, "core", swap)))[0]
    rows = lax.all_to_all(part, PEERS, split_axis=0, concat_axis=0, tiled=True)
    return call(
        functools.partial(final_kernel, scale_factor),
        [jax.ShapeDtypeStruct((ROWS_DEV, MW), jnp.float32)],
        (rows.reshape(-1, ROWS_DEV, MW),),
    )[0]


def solution(mesh):
    roles, bands, turns = (mesh.shape[name] for name in ("role", "band", "turn"))
    split = Mesh(mesh.devices.reshape(roles, bands, turns // CORES, CORES), ("role", "band", *TURN))
    in_specs = (
        P(("role", "band"), None, TURN, None),
        P(TURN),
        P(),
        P(("role", "band"), None, None, None),
        P(("role", "band"), None, None, None),
        P(None, ("role", "band", *TURN), None),
    )
    out_specs = P(("role", "band", *TURN), None)
    return jax.shard_map(local, mesh=split, in_specs=in_specs, out_specs=out_specs, check_vma=False)
```

```python
import functools
import math

import jax
import jax.numpy as jnp
import numpy as np
from jax import lax
from jax.experimental import pallas as pl
from jax.experimental.pallas import tpu as pltpu
from jax.sharding import Mesh
from jax.sharding import PartitionSpec as P

NGRID = 4096
MW = 128
ROWS_DEV = 1
DIGIT = 64
PAD_ROWS = 16
CORES = 2
TURN = ("chip", "core")
EVERYONE = ("role", "band", *TURN)
VMEM_BYTES = 24 * 1024 * 1024


def pack_kernel(flags_ref, cells_ref, out_ref):
    out_ref[...] = jnp.zeros_like(out_ref)
    out_ref[0:2, : cells_ref.shape[1]] = cells_ref[...]
    out_ref[2:3, : flags_ref.shape[1]] = flags_ref[...]


def gridding_weights(rows_ref, cols_ref, packed_ref, turn, stations):
    both = jnp.concatenate([rows_ref[0, 0], cols_ref[0, 0]], axis=0).astype(jnp.float32)
    weights = jnp.zeros((both.shape[0], stations), jnp.float32)
    for group in range(lax.axis_size(TURN)):
        weights = jnp.where(turn == group, both[:, group * stations : (group + 1) * stations], weights)
    return (weights * packed_ref[2:3, :stations].astype(jnp.float32)).astype(jnp.bfloat16)


def cell_digits(packed_refs, count, lanes):
    turn = lax.axis_index(TURN)
    digits = jnp.zeros((4, lanes), jnp.float32)
    for index, packed in enumerate(packed_refs):
        place = turn ^ index
        wide = jnp.concatenate([packed[0:2, :count]] * (lanes // count), axis=1)
        lane = lax.broadcasted_iota(jnp.int32, wide.shape, 1)
        wide = jnp.where((lane >= place * count) & (lane < (place + 1) * count), wide, 0)
        digits = digits + jnp.concatenate([wide // DIGIT, wide % DIGIT], axis=0).astype(jnp.float32)
    digits = jnp.concatenate([digits, jnp.zeros((PAD_ROWS - 4, lanes), jnp.float32)], axis=0)
    return digits.astype(jnp.bfloat16)


def gridded_frames(volt_ref, taps_ref, weights, firsts):
    taps, two_fine, _ = taps_ref.shape
    stations = volt_ref.shape[2]
    core = lax.axis_index("core")
    lhs = jnp.concatenate(
        [
            volt_ref[0, core, :, pl.ds(pl.multiple_of(first * two_fine, two_fine), taps * two_fine)]
            for first in firsts
        ],
        axis=0,
    )
    filt = taps_ref[...].reshape(taps * two_fine, two_fine)
    spectra = jnp.dot(lhs, filt, preferred_element_type=jnp.float32).astype(jnp.bfloat16)
    return [
        jnp.dot(weights, spectra[index * stations : (index + 1) * stations], preferred_element_type=jnp.float32)
        for index in range(len(firsts))
    ]


def own_kernel(volt_ref, taps_ref, rows_ref, cols_ref, packed_ref, out_ref):
    weights = gridding_weights(rows_ref, cols_ref, packed_ref, lax.axis_index(TURN), volt_ref.shape[2])
    rows = weights.shape[0]
    for frame, gridded in enumerate(gridded_frames(volt_ref, taps_ref, weights, range(out_ref.shape[0] // rows))):
        out_ref[frame * rows : (frame + 1) * rows] = gridded


def sum_kernel(step, frames, each, count, volt_ref, taps_ref, rows_ref, cols_ref, own_ref, packed_ref, part_ref, *refs):
    out_ref = refs[-1]
    weights = gridding_weights(rows_ref, cols_ref, packed_ref, lax.axis_index(TURN) ^ 1, volt_ref.shape[2])
    rows = weights.shape[0]
    firsts = [(lax.axis_index("chip") ^ step) * each + frame for frame in frames]
    for index, gridded in enumerate(gridded_frames(volt_ref, taps_ref, weights, firsts)):
        held = part_ref[pl.ds(pl.multiple_of(firsts[index] * rows, rows), rows)]
        out_ref[index * rows : (index + 1) * rows] = (held + gridded).astype(jnp.bfloat16)
    if frames[0] == 0:
        out_ref[len(frames) * rows :] = cell_digits((own_ref, packed_ref), count, out_ref.shape[1])


def split_terms(value):
    high = value.astype(jnp.bfloat16)
    return high, (value - high.astype(jnp.float32)).astype(jnp.bfloat16)


def image_kernel(pairs_each, sources, *refs):
    got = [refs[first : first + sources] for first in range(0, len(refs) - 3, sources)]
    row_dft_ref, col_dft_ref, out_ref = refs[-3:]
    fine = out_ref.shape[1]
    sub = row_dft_ref.shape[1] // 6
    row_total = out_ref.shape[0]
    pieces = []
    for piece in got:
        total = piece[0][...].astype(jnp.float32)
        for source in piece[1:]:
            total = total + source[...].astype(jnp.float32)
        pieces.append(total)
    digits = pieces[0][pieces[0].shape[0] - PAD_ROWS :]
    pieces[0] = pieces[0][: pieces[0].shape[0] - PAD_ROWS]
    total = jnp.concatenate(pieces, axis=0)
    cell_u = (digits[0:1, :fine] * DIGIT + digits[2:3, :fine]).astype(jnp.int32)
    cell_v = (digits[1:2, :fine] * DIGIT + digits[3:4, :fine]).astype(jnp.int32)

    def phase(cell, pixel):
        quarter = NGRID // 4
        turned = (cell * pixel) & (NGRID - 1)
        quadrant = (turned + quarter // 2) // quarter
        angle = (turned - quadrant * quarter).astype(jnp.float32) * (2.0 * math.pi / NGRID)
        square = angle * angle
        sine = angle * (1 + square * (-1 / 6 + square * (1 / 120 + square * (-1 / 5040 + square * (1 / 362880)))))
        cosine = 1 + square * (-1 / 2 + square * (1 / 24 + square * (-1 / 720 + square * (1 / 40320))))
        odd = (quadrant & 1) == 1
        real = jnp.where(odd, sine, cosine)
        imag = jnp.where(odd, cosine, sine)
        return (
            jnp.where(((quadrant + 1) & 2) == 2, -real, real),
            jnp.where((quadrant & 2) == 2, -imag, imag),
        )

    def transform(dft_ref, first, cos, sin):
        held = jnp.concatenate(
            [
                jnp.concatenate(
                    [
                        total[index * 2 * sub + first : index * 2 * sub + first + sub, :fine],
                        total[index * 2 * sub + first : index * 2 * sub + first + sub, fine:],
                    ],
                    axis=0,
                )
                for index in range(pairs_each)
            ],
            axis=1,
        )
        high, low = split_terms(held)
        plain = jnp.dot(
            dft_ref[...].astype(jnp.bfloat16), jnp.concatenate([high, high, low], axis=0), preferred_element_type=jnp.float32
        )
        half = plain.shape[0] // 2
        real, imag = plain[:half], plain[half:]
        cos = jnp.concatenate([cos] * pairs_each, axis=1)
        sin = jnp.concatenate([sin] * pairs_each, axis=1)
        return real * cos - imag * sin, real * sin + imag * cos

    row = lax.broadcasted_iota(jnp.int32, (row_total, fine), 0)
    row_real, row_imag = transform(row_dft_ref, 0, *phase(cell_u, row - row_total // 2))
    col = lax.broadcasted_iota(jnp.int32, (MW, fine), 0)
    col_real, col_imag = transform(col_dft_ref, sub, *phase(cell_v, col - MW // 2))
    left = jnp.concatenate([row_real, -row_imag], axis=1).astype(jnp.bfloat16)
    right = jnp.concatenate([col_real, col_imag], axis=1).astype(jnp.bfloat16)
    out_ref[...] = lax.dot_general(left, right, (((1,), (1,)), ((), ())), preferred_element_type=jnp.float32)


def final_kernel(scale_factor, in_ref, out_ref):
    out_ref[...] = jnp.sum(in_ref[...], axis=0) * scale_factor


def dft_matrix(pixel, cells, conjugate):
    angle = 2.0 * np.pi / NGRID * np.outer(pixel, np.arange(cells))
    cos, sin = np.cos(angle), np.sin(angle)
    sign = -1.0 if conjugate else 1.0
    whole = np.block([[cos, -sign * sin], [sin, sign * cos]]).astype(np.float32)
    high = whole.astype(jnp.bfloat16)
    low = (whole - high.astype(np.float32)).astype(jnp.bfloat16)
    return np.concatenate([high, low, high], axis=1).astype(np.float32)


def call(kernel, shape, args, flops=0):
    moved = sum(math.prod(leaf.shape) * leaf.dtype.itemsize for leaf in [shape, *args])
    return pl.pallas_call(
        kernel,
        out_shape=shape,
        in_specs=[pl.BlockSpec(memory_space=pltpu.VMEM)] * len(args),
        out_specs=pl.BlockSpec(memory_space=pltpu.VMEM),
        compiler_params=pltpu.CompilerParams(vmem_limit_bytes=VMEM_BYTES),
        cost_estimate=pl.CostEstimate(flops=flops, bytes_accessed=moved, transcendentals=0),
    )(*args)


def local(voltages, station_flags, filter_taps, kernel_rows, kernel_cols, cell_index):
    station_rows, width = voltages.shape[2:]
    taps, two_fine, _ = filter_taps.shape
    sub_u, sub_v = kernel_rows.shape[2], kernel_cols.shape[2]
    chips = lax.axis_size("chip")
    row_total = ROWS_DEV * lax.axis_size(EVERYONE)
    channels = two_fine // 2 * lax.axis_size("role") * lax.axis_size("band")
    frames = width // two_fine - taps + 1
    scale_factor = 4.0 / math.sqrt(channels * sub_u * sub_v) / frames
    each = frames // chips
    count = cell_index.shape[1]
    sub_rows = sub_u + sub_v

    swap = [(core, 1 - core) for core in range(CORES)]
    other = lax.ppermute(voltages, "core", swap)
    packed = call(
        pack_kernel,
        jax.ShapeDtypeStruct((8, -(-max(station_rows, count) // 128) * 128), jnp.int32),
        (station_flags.reshape(1, -1), cell_index.reshape(2, -1)),
        flops=2 * voltages.size * two_fine * taps,
    )
    other_packed = lax.ppermute(packed, "core", swap)
    fixed = (filter_taps, kernel_rows, kernel_cols, packed)
    flops = 2 * station_rows * taps * two_fine * two_fine
    part = call(
        own_kernel,
        jax.ShapeDtypeStruct((frames * sub_rows, two_fine), jnp.float32),
        (voltages, *fixed),
        flops=frames * flops,
    )

    half = (each + 1) // 2
    pieces = [list(range(half)), list(range(half, each))] if each > 1 else [[0]]
    after = ()
    sums = {}
    for step in [*range(1, chips), 0]:
        for index, piece in enumerate(pieces):
            made = call(
                functools.partial(sum_kernel, step, piece, each, count),
                jax.ShapeDtypeStruct((len(piece) * sub_rows + (index == 0) * PAD_ROWS, two_fine), jnp.bfloat16),
                (other, *fixed, other_packed, part, *after),
                flops=len(piece) * flops,
            )
            after = (made,)
            if step:
                made = lax.ppermute(made, "chip", [(source, source ^ step) for source in range(chips)])
            sums[index, step] = made
    image = call(
        functools.partial(image_kernel, each, chips),
        jax.ShapeDtypeStruct((row_total, MW), jnp.float32),
        (
            *[sums[index, step] for index in range(len(pieces)) for step in range(chips)],
            jnp.asarray(dft_matrix(np.arange(row_total) - row_total // 2, sub_u, False)),
            jnp.asarray(dft_matrix(np.arange(MW) - MW // 2, sub_v, True)),
        ),
    )
    rows = lax.all_to_all(image, EVERYONE, split_axis=0, concat_axis=0, tiled=True)
    return call(
        functools.partial(final_kernel, scale_factor),
        jax.ShapeDtypeStruct((ROWS_DEV, MW), jnp.float32),
        (rows.reshape(-1, ROWS_DEV, MW),),
    )


def solution(mesh):
    roles, bands, turns = (mesh.shape[name] for name in ("role", "band", "turn"))
    split = Mesh(mesh.devices.reshape(roles, bands, turns // CORES, CORES), EVERYONE)
    in_specs = (
        P(("role", "band"), None, TURN, None),
        P(TURN),
        P(),
        P(("role", "band"), None, None, None),
        P(("role", "band"), None, None, None),
        P(None, EVERYONE, None),
    )
    out_specs = P(EVERYONE, None)
    return jax.shard_map(local, mesh=split, in_specs=in_specs, out_specs=out_specs, check_vma=False)
```

```python
import functools
import math

import jax
import jax.numpy as jnp
from jax import lax
from jax.experimental import pallas as pl
from jax.experimental.pallas import tpu as pltpu
from jax.sharding import Mesh
from jax.sharding import PartitionSpec as P

NGRID = 4096
MW = 128
ROWS_DEV = 1
DIGIT = 64
PAD_ROWS = 16
CORES = 2
TURN = ("chip", "core")
EVERYONE = ("role", "band", *TURN)
VMEM_BYTES = 24 * 1024 * 1024


def split_terms(value):
    high = value.astype(jnp.bfloat16)
    return high, (value - high.astype(jnp.float32)).astype(jnp.bfloat16)


def phase(cell, pixel):
    quarter = NGRID // 4
    turned = (cell * pixel) & (NGRID - 1)
    quadrant = (turned + quarter // 2) // quarter
    angle = (turned - quadrant * quarter).astype(jnp.float32) * (2.0 * math.pi / NGRID)
    square = angle * angle
    sine = angle * (1 + square * (-1 / 6 + square * (1 / 120 + square * (-1 / 5040 + square * (1 / 362880)))))
    cosine = 1 + square * (-1 / 2 + square * (1 / 24 + square * (-1 / 720 + square * (1 / 40320))))
    odd = (quadrant & 1) == 1
    real = jnp.where(odd, sine, cosine)
    imag = jnp.where(odd, cosine, sine)
    return (
        jnp.where(((quadrant + 1) & 2) == 2, -real, real),
        jnp.where((quadrant & 2) == 2, -imag, imag),
    )


def tables_kernel(row_ref, col_ref):
    for out_ref, sign in ((row_ref, 1), (col_ref, -1)):
        pixels, cells = out_ref.shape[0] // 2, out_ref.shape[1] // 6
        place = lax.broadcasted_iota(jnp.int32, (2 * pixels, 2 * cells), 0)
        lane = lax.broadcasted_iota(jnp.int32, (2 * pixels, 2 * cells), 1)
        lower, right = place >= pixels, lane >= cells
        pixel = jnp.where(lower, place - pixels, place) - pixels // 2
        cos, sin = phase(jnp.where(right, lane - cells, lane), pixel)
        value = jnp.where(lower == right, cos, sin)
        value = jnp.where(right & (lower == (sign < 0)), -value, value)
        high, low = split_terms(value)
        out_ref[...] = jnp.concatenate([high, low, high], axis=1)


def pack_kernel(flags_ref, cells_ref, _, out_ref):
    out_ref[...] = jnp.zeros_like(out_ref)
    out_ref[0:2, : cells_ref.shape[1]] = cells_ref[...]
    out_ref[2:3, : flags_ref.shape[1]] = flags_ref[...]


def gridding_weights(rows_ref, cols_ref, packed_ref, turn, stations):
    both = jnp.concatenate([rows_ref[0, 0], cols_ref[0, 0]], axis=0).astype(jnp.float32)
    weights = jnp.zeros((both.shape[0], stations), jnp.float32)
    for group in range(lax.axis_size(TURN)):
        weights = jnp.where(turn == group, both[:, group * stations : (group + 1) * stations], weights)
    return (weights * packed_ref[2:3, :stations].astype(jnp.float32)).astype(jnp.bfloat16)


def cell_digits(packed_refs, count, lanes):
    turn = lax.axis_index(TURN)
    digits = jnp.zeros((4, lanes), jnp.float32)
    for index, packed in enumerate(packed_refs):
        place = turn ^ index
        wide = jnp.concatenate([packed[0:2, :count]] * (lanes // count), axis=1)
        lane = lax.broadcasted_iota(jnp.int32, wide.shape, 1)
        wide = jnp.where((lane >= place * count) & (lane < (place + 1) * count), wide, 0)
        digits = digits + jnp.concatenate([wide // DIGIT, wide % DIGIT], axis=0).astype(jnp.float32)
    digits = jnp.concatenate([digits, jnp.zeros((PAD_ROWS - 4, lanes), jnp.float32)], axis=0)
    return digits.astype(jnp.bfloat16)


def gridded_frames(volt_ref, taps_ref, weights, firsts):
    taps, two_fine, _ = taps_ref.shape
    stations = volt_ref.shape[2]
    core = lax.axis_index("core")
    lhs = jnp.concatenate(
        [
            volt_ref[0, core, :, pl.ds(pl.multiple_of(first * two_fine, two_fine), taps * two_fine)]
            for first in firsts
        ],
        axis=0,
    )
    filt = taps_ref[...].reshape(taps * two_fine, two_fine)
    spectra = jnp.dot(lhs, filt, preferred_element_type=jnp.float32).astype(jnp.bfloat16)
    return [
        jnp.dot(weights, spectra[index * stations : (index + 1) * stations], preferred_element_type=jnp.float32)
        for index in range(len(firsts))
    ]


def own_kernel(volt_ref, taps_ref, rows_ref, cols_ref, packed_ref, out_ref):
    weights = gridding_weights(rows_ref, cols_ref, packed_ref, lax.axis_index(TURN), volt_ref.shape[2])
    rows = weights.shape[0]
    for frame, gridded in enumerate(gridded_frames(volt_ref, taps_ref, weights, range(out_ref.shape[0] // rows))):
        out_ref[frame * rows : (frame + 1) * rows] = gridded


def sum_kernel(step, each, count, volt_ref, taps_ref, rows_ref, cols_ref, own_ref, packed_ref, part_ref, *refs):
    out_ref = refs[-1]
    weights = gridding_weights(rows_ref, cols_ref, packed_ref, lax.axis_index(TURN) ^ 1, volt_ref.shape[2])
    rows = weights.shape[0]
    firsts = [(lax.axis_index("chip") ^ step) * each + frame for frame in range(each)]
    for index, gridded in enumerate(gridded_frames(volt_ref, taps_ref, weights, firsts)):
        held = part_ref[pl.ds(pl.multiple_of(firsts[index] * rows, rows), rows)]
        out_ref[index * rows : (index + 1) * rows] = (held + gridded).astype(jnp.bfloat16)
    out_ref[each * rows :] = cell_digits((own_ref, packed_ref), count, out_ref.shape[1])


def image_kernel(pairs_each, *refs):
    *got, row_dft_ref, col_dft_ref, out_ref = refs
    fine = got[0].shape[1] // 2
    sub = row_dft_ref.shape[1] // 6
    row_total = out_ref.shape[0]
    total = got[0][...].astype(jnp.float32)
    for source in got[1:]:
        total = total + source[...].astype(jnp.float32)
    digits = total[pairs_each * 2 * sub :]
    cell_u = (digits[0:1, :fine] * DIGIT + digits[2:3, :fine]).astype(jnp.int32)
    cell_v = (digits[1:2, :fine] * DIGIT + digits[3:4, :fine]).astype(jnp.int32)

    def transform(dft_ref, first, cos, sin):
        held = jnp.concatenate(
            [
                jnp.concatenate(
                    [
                        total[index * 2 * sub + first : index * 2 * sub + first + sub, :fine],
                        total[index * 2 * sub + first : index * 2 * sub + first + sub, fine:],
                    ],
                    axis=0,
                )
                for index in range(pairs_each)
            ],
            axis=1,
        )
        high, low = split_terms(held)
        plain = jnp.dot(
            dft_ref[...], jnp.concatenate([high, high, low], axis=0), preferred_element_type=jnp.float32
        )
        half = plain.shape[0] // 2
        real, imag = plain[:half], plain[half:]
        cos = jnp.concatenate([cos] * pairs_each, axis=1)
        sin = jnp.concatenate([sin] * pairs_each, axis=1)
        return real * cos - imag * sin, real * sin + imag * cos

    row = lax.broadcasted_iota(jnp.int32, (row_total, fine), 0)
    row_real, row_imag = transform(row_dft_ref, 0, *phase(cell_u, row - row_total // 2))
    col = lax.broadcasted_iota(jnp.int32, (MW, fine), 0)
    col_real, col_imag = transform(col_dft_ref, sub, *phase(cell_v, col - MW // 2))
    left = jnp.concatenate([row_real, -row_imag], axis=1).astype(jnp.bfloat16)
    right = jnp.concatenate([col_real, col_imag], axis=1).astype(jnp.bfloat16)
    out_ref[...] = lax.dot_general(left, right, (((1,), (1,)), ((), ())), preferred_element_type=jnp.float32)


def final_kernel(scale_factor, in_ref, out_ref):
    out_ref[...] = jnp.sum(in_ref[...], axis=0) * scale_factor


def call(kernel, shape, args, flops=0):
    moved = sum(math.prod(leaf.shape) * leaf.dtype.itemsize for leaf in [*jax.tree.leaves(shape), *args])
    return pl.pallas_call(
        kernel,
        out_shape=shape,
        in_specs=[pl.BlockSpec(memory_space=pltpu.VMEM)] * len(args),
        out_specs=jax.tree.map(lambda _: pl.BlockSpec(memory_space=pltpu.VMEM), shape),
        compiler_params=pltpu.CompilerParams(vmem_limit_bytes=VMEM_BYTES),
        cost_estimate=pl.CostEstimate(flops=flops, bytes_accessed=moved, transcendentals=0),
    )(*args)


def local(voltages, station_flags, filter_taps, kernel_rows, kernel_cols, cell_index):
    station_rows, width = voltages.shape[2:]
    taps, two_fine, _ = filter_taps.shape
    sub_u, sub_v = kernel_rows.shape[2], kernel_cols.shape[2]
    chips = lax.axis_size("chip")
    row_total = ROWS_DEV * lax.axis_size(EVERYONE)
    channels = two_fine // 2 * lax.axis_size("role") * lax.axis_size("band")
    frames = width // two_fine - taps + 1
    scale_factor = 4.0 / math.sqrt(channels * sub_u * sub_v) / frames
    each = frames // chips
    count = cell_index.shape[1]
    sub_rows = sub_u + sub_v

    swap = [(core, 1 - core) for core in range(CORES)]
    other = lax.ppermute(voltages, "core", swap)
    tables = call(
        tables_kernel,
        (
            jax.ShapeDtypeStruct((2 * row_total, 6 * sub_u), jnp.bfloat16),
            jax.ShapeDtypeStruct((2 * MW, 6 * sub_v), jnp.bfloat16),
        ),
        (),
        flops=2 * voltages.size * two_fine * taps,
    )
    packed = call(
        pack_kernel,
        jax.ShapeDtypeStruct((8, -(-max(station_rows, count) // 128) * 128), jnp.int32),
        (station_flags.reshape(1, -1), cell_index.reshape(2, -1), tables[0]),
    )
    other_packed = lax.ppermute(packed, "core", swap)
    fixed = (filter_taps, kernel_rows, kernel_cols, packed)
    flops = 2 * station_rows * taps * two_fine * two_fine
    part = call(
        own_kernel,
        jax.ShapeDtypeStruct((frames * sub_rows, two_fine), jnp.float32),
        (voltages, *fixed),
        flops=frames * flops,
    )

    after = ()
    got = []
    for step in [*range(1, chips), 0]:
        made = call(
            functools.partial(sum_kernel, step, each, count),
            jax.ShapeDtypeStruct((each * sub_rows + PAD_ROWS, two_fine), jnp.bfloat16),
            (other, *fixed, other_packed, part, *after),
            flops=each * flops,
        )
        after = (made,)
        if step:
            made = lax.ppermute(made, "chip", [(source, source ^ step) for source in range(chips)])
        got.append(made)
    image = call(
        functools.partial(image_kernel, each),
        jax.ShapeDtypeStruct((row_total, MW), jnp.float32),
        (*got, *tables),
    )
    rows = lax.all_to_all(image, EVERYONE, split_axis=0, concat_axis=0, tiled=True)
    return call(
        functools.partial(final_kernel, scale_factor),
        jax.ShapeDtypeStruct((ROWS_DEV, MW), jnp.float32),
        (rows.reshape(-1, ROWS_DEV, MW),),
    )


def solution(mesh):
    roles, bands, turns = (mesh.shape[name] for name in ("role", "band", "turn"))
    split = Mesh(mesh.devices.reshape(roles, bands, turns // CORES, CORES), EVERYONE)
    in_specs = (
        P(("role", "band"), None, TURN, None),
        P(TURN),
        P(),
        P(("role", "band"), None, None, None),
        P(("role", "band"), None, None, None),
        P(None, EVERYONE, None),
    )
    out_specs = P(EVERYONE, None)
    return jax.shard_map(local, mesh=split, in_specs=in_specs, out_specs=out_specs, check_vma=False)
```

```python
import functools
import math

import jax
import jax.numpy as jnp
from jax import lax
from jax.experimental import pallas as pl
from jax.experimental.pallas import tpu as pltpu
from jax.sharding import Mesh
from jax.sharding import PartitionSpec as P

NGRID = 4096
MW = 128
ROWS_DEV = 1
DIGIT = 64
PAD_ROWS = 16
CORES = 2
TURN = ("chip", "core")
EVERYONE = ("role", "band", *TURN)
VMEM_BYTES = 24 * 1024 * 1024


def split_terms(value):
    high = value.astype(jnp.bfloat16)
    return high, (value - high.astype(jnp.float32)).astype(jnp.bfloat16)


def phase(cell, pixel):
    quarter = NGRID // 4
    turned = (cell * pixel) & (NGRID - 1)
    quadrant = (turned + quarter // 2) // quarter
    angle = (turned - quadrant * quarter).astype(jnp.float32) * (2.0 * math.pi / NGRID)
    square = angle * angle
    sine = angle * (1 + square * (-1 / 6 + square * (1 / 120 + square * (-1 / 5040 + square * (1 / 362880)))))
    cosine = 1 + square * (-1 / 2 + square * (1 / 24 + square * (-1 / 720 + square * (1 / 40320))))
    odd = (quadrant & 1) == 1
    real = jnp.where(odd, sine, cosine)
    imag = jnp.where(odd, cosine, sine)
    return (
        jnp.where(((quadrant + 1) & 2) == 2, -real, real),
        jnp.where((quadrant & 2) == 2, -imag, imag),
    )


def first_kernel(flags_ref, cells_ref, row_ref, col_ref, packed_ref):
    packed_ref[...] = jnp.zeros_like(packed_ref)
    packed_ref[0:2, : cells_ref.shape[1]] = cells_ref[...]
    packed_ref[2:3, : flags_ref.shape[1]] = flags_ref[...]
    for out_ref, sign in ((row_ref, 1), (col_ref, -1)):
        pixels, cells = out_ref.shape[0] // 2, out_ref.shape[1] // 6
        place = lax.broadcasted_iota(jnp.int32, (2 * pixels, 2 * cells), 0)
        lane = lax.broadcasted_iota(jnp.int32, (2 * pixels, 2 * cells), 1)
        lower, right = place >= pixels, lane >= cells
        pixel = jnp.where(lower, place - pixels, place) - pixels // 2
        cos, sin = phase(jnp.where(right, lane - cells, lane), pixel)
        value = jnp.where(lower == right, cos, sin)
        value = jnp.where(right & (lower == (sign < 0)), -value, value)
        high, low = split_terms(value)
        out_ref[...] = jnp.concatenate([high, low, high], axis=1)


def gridding_weights(rows_ref, cols_ref, packed_ref, turn, stations):
    both = jnp.concatenate([rows_ref[0, 0], cols_ref[0, 0]], axis=0).astype(jnp.float32)
    weights = jnp.zeros((both.shape[0], stations), jnp.float32)
    for group in range(lax.axis_size(TURN)):
        weights = jnp.where(turn == group, both[:, group * stations : (group + 1) * stations], weights)
    return (weights * packed_ref[2:3, :stations].astype(jnp.float32)).astype(jnp.bfloat16)


def cell_digits(packed_refs, count, lanes):
    turn = lax.axis_index(TURN)
    digits = jnp.zeros((4, lanes), jnp.float32)
    for index, packed in enumerate(packed_refs):
        place = turn ^ index
        wide = jnp.concatenate([packed[0:2, :count]] * (lanes // count), axis=1)
        lane = lax.broadcasted_iota(jnp.int32, wide.shape, 1)
        wide = jnp.where((lane >= place * count) & (lane < (place + 1) * count), wide, 0)
        digits = digits + jnp.concatenate([wide // DIGIT, wide % DIGIT], axis=0).astype(jnp.float32)
    digits = jnp.concatenate([digits, jnp.zeros((PAD_ROWS - 4, lanes), jnp.float32)], axis=0)
    return digits.astype(jnp.bfloat16)


def channelized(grid_ref, taps_ref, first, digits, out_ref):
    taps, two_fine, _ = taps_ref.shape
    each = (out_ref.shape[0] - PAD_ROWS) // grid_ref.shape[0]
    lhs = jnp.concatenate(
        [
            grid_ref[:, pl.ds(pl.multiple_of((first + frame) * two_fine, two_fine), taps * two_fine)]
            for frame in range(each)
        ],
        axis=0,
    )
    made = jnp.dot(lhs, taps_ref[...].reshape(taps * two_fine, two_fine), preferred_element_type=jnp.float32)
    out_ref[: out_ref.shape[0] - PAD_ROWS] = made.astype(jnp.bfloat16)
    out_ref[out_ref.shape[0] - PAD_ROWS :] = digits


def grid_kernel(own_ref, other_ref, taps_ref, rows_ref, cols_ref, packed_ref, other_packed_ref, *refs, count):
    grid_ref, digits_ref, *outs = refs
    turn, core, stations = lax.axis_index(TURN), lax.axis_index("core"), own_ref.shape[2]
    weights = [
        gridding_weights(rows_ref, cols_ref, packed, turn ^ index, stations)
        for index, packed in enumerate((packed_ref, other_packed_ref))
    ]
    held = jnp.concatenate([own_ref[0, core], other_ref[0, core]], axis=0)
    gridded = jnp.dot(jnp.concatenate(weights, axis=1), held, preferred_element_type=jnp.float32)
    grid_ref[...] = gridded.astype(jnp.bfloat16)
    digits_ref[...] = cell_digits((packed_ref, other_packed_ref), count, digits_ref.shape[1])
    each = (outs[0].shape[0] - PAD_ROWS) // grid_ref.shape[0]
    for step, out_ref in enumerate(outs, 1):
        channelized(grid_ref, taps_ref, (lax.axis_index("chip") ^ step) * each, digits_ref[...], out_ref)


def near_kernel(grid_ref, taps_ref, digits_ref, out_ref):
    each = (out_ref.shape[0] - PAD_ROWS) // grid_ref.shape[0]
    channelized(grid_ref, taps_ref, lax.axis_index("chip") * each, digits_ref[...], out_ref)


def image_kernel(pairs_each, *refs):
    *got, row_dft_ref, col_dft_ref, out_ref = refs
    fine = got[0].shape[1] // 2
    sub = row_dft_ref.shape[1] // 6
    row_total = out_ref.shape[0]
    total = got[0][...].astype(jnp.float32)
    for source in got[1:]:
        total = total + source[...].astype(jnp.float32)
    digits = total[pairs_each * 2 * sub :]
    cell_u = (digits[0:1, :fine] * DIGIT + digits[2:3, :fine]).astype(jnp.int32)
    cell_v = (digits[1:2, :fine] * DIGIT + digits[3:4, :fine]).astype(jnp.int32)

    def transform(dft_ref, first, cos, sin):
        held = jnp.concatenate(
            [
                jnp.concatenate(
                    [
                        total[index * 2 * sub + first : index * 2 * sub + first + sub, :fine],
                        total[index * 2 * sub + first : index * 2 * sub + first + sub, fine:],
                    ],
                    axis=0,
                )
                for index in range(pairs_each)
            ],
            axis=1,
        )
        high, low = split_terms(held)
        plain = jnp.dot(
            dft_ref[...], jnp.concatenate([high, high, low], axis=0), preferred_element_type=jnp.float32
        )
        half = plain.shape[0] // 2
        real, imag = plain[:half], plain[half:]
        cos = jnp.concatenate([cos] * pairs_each, axis=1)
        sin = jnp.concatenate([sin] * pairs_each, axis=1)
        return real * cos - imag * sin, real * sin + imag * cos

    row = lax.broadcasted_iota(jnp.int32, (row_total, fine), 0)
    row_real, row_imag = transform(row_dft_ref, 0, *phase(cell_u, row - row_total // 2))
    col = lax.broadcasted_iota(jnp.int32, (MW, fine), 0)
    col_real, col_imag = transform(col_dft_ref, sub, *phase(cell_v, col - MW // 2))
    left = jnp.concatenate([row_real, -row_imag], axis=1).astype(jnp.bfloat16)
    right = jnp.concatenate([col_real, col_imag], axis=1).astype(jnp.bfloat16)
    out_ref[...] = lax.dot_general(left, right, (((1,), (1,)), ((), ())), preferred_element_type=jnp.float32)


def final_kernel(scale_factor, in_ref, out_ref):
    out_ref[...] = jnp.sum(in_ref[...], axis=0) * scale_factor


def call(kernel, shape, args, flops=0):
    moved = sum(math.prod(leaf.shape) * leaf.dtype.itemsize for leaf in [*jax.tree.leaves(shape), *args])
    return pl.pallas_call(
        kernel,
        out_shape=shape,
        in_specs=[pl.BlockSpec(memory_space=pltpu.VMEM)] * len(args),
        out_specs=jax.tree.map(lambda _: pl.BlockSpec(memory_space=pltpu.VMEM), shape),
        compiler_params=pltpu.CompilerParams(vmem_limit_bytes=VMEM_BYTES),
        cost_estimate=pl.CostEstimate(flops=flops, bytes_accessed=moved, transcendentals=0),
    )(*args)


def local(voltages, station_flags, filter_taps, kernel_rows, kernel_cols, cell_index):
    station_rows, width = voltages.shape[2:]
    taps, two_fine, _ = filter_taps.shape
    sub_u, sub_v = kernel_rows.shape[2], kernel_cols.shape[2]
    chips = lax.axis_size("chip")
    row_total = ROWS_DEV * lax.axis_size(EVERYONE)
    channels = two_fine // 2 * lax.axis_size("role") * lax.axis_size("band")
    frames = width // two_fine - taps + 1
    scale_factor = 4.0 / math.sqrt(channels * sub_u * sub_v) / frames
    each = frames // chips
    count = cell_index.shape[1]
    sub_rows = sub_u + sub_v

    swap = [(core, 1 - core) for core in range(CORES)]
    other = lax.ppermute(voltages, "core", swap)
    *tables, packed = call(
        first_kernel,
        (
            jax.ShapeDtypeStruct((2 * row_total, 6 * sub_u), jnp.bfloat16),
            jax.ShapeDtypeStruct((2 * MW, 6 * sub_v), jnp.bfloat16),
            jax.ShapeDtypeStruct((8, -(-max(station_rows, count) // 128) * 128), jnp.int32),
        ),
        (station_flags.reshape(1, -1), cell_index.reshape(2, -1)),
        flops=2 * voltages.size * two_fine * taps,
    )
    other_packed = lax.ppermute(packed, "core", swap)

    piece = jax.ShapeDtypeStruct((each * sub_rows + PAD_ROWS, two_fine), jnp.bfloat16)
    flops = 2 * each * sub_rows * taps * two_fine * two_fine
    grid, digits, *far = call(
        functools.partial(grid_kernel, count=count),
        (
            jax.ShapeDtypeStruct((sub_rows, width), jnp.bfloat16),
            jax.ShapeDtypeStruct((PAD_ROWS, two_fine), jnp.bfloat16),
            *[piece] * (chips - 1),
        ),
        (voltages, other, filter_taps, kernel_rows, kernel_cols, packed, other_packed),
        flops=4 * sub_rows * station_rows * width + (chips - 1) * flops,
    )
    got = [call(near_kernel, piece, (grid, filter_taps, digits), flops=flops)]
    for step, part in enumerate(far, 1):
        got.append(lax.ppermute(part, "chip", [(source, source ^ step) for source in range(chips)]))
    image = call(
        functools.partial(image_kernel, each),
        jax.ShapeDtypeStruct((row_total, MW), jnp.float32),
        (*got, *tables),
    )
    rows = lax.all_to_all(image, EVERYONE, split_axis=0, concat_axis=0, tiled=True)
    return call(
        functools.partial(final_kernel, scale_factor),
        jax.ShapeDtypeStruct((ROWS_DEV, MW), jnp.float32),
        (rows.reshape(-1, ROWS_DEV, MW),),
    )


def solution(mesh):
    roles, bands, turns = (mesh.shape[name] for name in ("role", "band", "turn"))
    split = Mesh(mesh.devices.reshape(roles, bands, turns // CORES, CORES), EVERYONE)
    in_specs = (
        P(("role", "band"), None, TURN, None),
        P(TURN),
        P(),
        P(("role", "band"), None, None, None),
        P(("role", "band"), None, None, None),
        P(None, EVERYONE, None),
    )
    out_specs = P(EVERYONE, None)
    return jax.shard_map(local, mesh=split, in_specs=in_specs, out_specs=out_specs, check_vma=False)
```

```python
import functools
import math

import jax
import jax.numpy as jnp
from jax import lax
from jax.experimental import pallas as pl
from jax.experimental.pallas import tpu as pltpu
from jax.sharding import Mesh
from jax.sharding import PartitionSpec as P

NGRID = 4096
MW = 128
ROWS_DEV = 1
DIGIT = 64
PAD_ROWS = 16
CORES = 2
TURN = ("chip", "core")
EVERYONE = ("role", "band", *TURN)
VMEM_BYTES = 24 * 1024 * 1024


def split_terms(value):
    high = value.astype(jnp.bfloat16)
    return high, (value - high.astype(jnp.float32)).astype(jnp.bfloat16)


def phase(cell, pixel):
    quarter = NGRID // 4
    turned = (cell * pixel) & (NGRID - 1)
    quadrant = (turned + quarter // 2) // quarter
    angle = (turned - quadrant * quarter).astype(jnp.float32) * (2.0 * math.pi / NGRID)
    square = angle * angle
    sine = angle * (1 + square * (-1 / 6 + square * (1 / 120 + square * (-1 / 5040 + square * (1 / 362880)))))
    cosine = 1 + square * (-1 / 2 + square * (1 / 24 + square * (-1 / 720 + square * (1 / 40320))))
    odd = (quadrant & 1) == 1
    real = jnp.where(odd, sine, cosine)
    imag = jnp.where(odd, cosine, sine)
    return (
        jnp.where(((quadrant + 1) & 2) == 2, -real, real),
        jnp.where((quadrant & 2) == 2, -imag, imag),
    )


def tables_kernel(row_ref, col_ref):
    for out_ref, sign in ((row_ref, 1), (col_ref, -1)):
        pixels, cells = out_ref.shape[0] // 2, out_ref.shape[1] // 6
        place = lax.broadcasted_iota(jnp.int32, (2 * pixels, 2 * cells), 0)
        lane = lax.broadcasted_iota(jnp.int32, (2 * pixels, 2 * cells), 1)
        lower, right = place >= pixels, lane >= cells
        pixel = jnp.where(lower, place - pixels, place) - pixels // 2
        cos, sin = phase(jnp.where(right, lane - cells, lane), pixel)
        value = jnp.where(lower == right, cos, sin)
        value = jnp.where(right & (lower == (sign < 0)), -value, value)
        high, low = split_terms(value)
        out_ref[...] = jnp.concatenate([high, low, high], axis=1)


def pack_kernel(flags_ref, cells_ref, _, out_ref):
    out_ref[...] = jnp.zeros_like(out_ref)
    out_ref[0:2, : cells_ref.shape[1]] = cells_ref[...]
    out_ref[2:3, : flags_ref.shape[1]] = flags_ref[...]


def gridding_weights(rows_ref, cols_ref, packed_ref, turn, stations):
    both = jnp.concatenate([rows_ref[0, 0], cols_ref[0, 0]], axis=0).astype(jnp.float32)
    weights = jnp.zeros((both.shape[0], stations), jnp.float32)
    for group in range(lax.axis_size(TURN)):
        weights = jnp.where(turn == group, both[:, group * stations : (group + 1) * stations], weights)
    return (weights * packed_ref[2:3, :stations].astype(jnp.float32)).astype(jnp.bfloat16)


def cell_digits(packed_refs, count, lanes):
    turn = lax.axis_index(TURN)
    digits = jnp.zeros((4, lanes), jnp.float32)
    for index, packed in enumerate(packed_refs):
        place = turn ^ index
        wide = jnp.concatenate([packed[0:2, :count]] * (lanes // count), axis=1)
        lane = lax.broadcasted_iota(jnp.int32, wide.shape, 1)
        wide = jnp.where((lane >= place * count) & (lane < (place + 1) * count), wide, 0)
        digits = digits + jnp.concatenate([wide // DIGIT, wide % DIGIT], axis=0).astype(jnp.float32)
    digits = jnp.concatenate([digits, jnp.zeros((PAD_ROWS - 4, lanes), jnp.float32)], axis=0)
    return digits.astype(jnp.bfloat16)


def gridded_frames(volt_ref, taps_ref, weights, firsts):
    taps, two_fine, _ = taps_ref.shape
    stations = volt_ref.shape[2]
    core = lax.axis_index("core")
    lhs = jnp.concatenate(
        [
            volt_ref[0, core, :, pl.ds(pl.multiple_of(first * two_fine, two_fine), taps * two_fine)]
            for first in firsts
        ],
        axis=0,
    )
    filt = taps_ref[...].reshape(taps * two_fine, two_fine)
    spectra = jnp.dot(lhs, filt, preferred_element_type=jnp.float32).astype(jnp.bfloat16)
    return [
        jnp.dot(weights, spectra[index * stations : (index + 1) * stations], preferred_element_type=jnp.float32)
        for index in range(len(firsts))
    ]


def own_kernel(volt_ref, taps_ref, rows_ref, cols_ref, packed_ref, out_ref):
    weights = gridding_weights(rows_ref, cols_ref, packed_ref, lax.axis_index(TURN), volt_ref.shape[2])
    rows = weights.shape[0]
    for frame, gridded in enumerate(gridded_frames(volt_ref, taps_ref, weights, range(out_ref.shape[0] // rows))):
        out_ref[frame * rows : (frame + 1) * rows] = gridded


def sum_kernel(step, each, count, volt_ref, taps_ref, rows_ref, cols_ref, own_ref, packed_ref, part_ref, *refs):
    out_ref = refs[-1]
    weights = gridding_weights(rows_ref, cols_ref, packed_ref, lax.axis_index(TURN) ^ 1, volt_ref.shape[2])
    rows = weights.shape[0]
    firsts = [(lax.axis_index("chip") ^ step) * each + frame for frame in range(each)]
    for index, gridded in enumerate(gridded_frames(volt_ref, taps_ref, weights, firsts)):
        held = part_ref[pl.ds(pl.multiple_of(firsts[index] * rows, rows), rows)]
        out_ref[index * rows : (index + 1) * rows] = (held + gridded).astype(jnp.bfloat16)
    out_ref[each * rows :] = cell_digits((own_ref, packed_ref), count, out_ref.shape[1])


def image_kernel(pairs_each, *refs):
    *got, row_dft_ref, col_dft_ref, out_ref = refs
    fine = got[0].shape[1] // 2
    sub = row_dft_ref.shape[1] // 6
    row_total = out_ref.shape[0]
    total = got[0][...].astype(jnp.float32)
    for source in got[1:]:
        total = total + source[...].astype(jnp.float32)
    digits = total[pairs_each * 2 * sub :]
    cell_u = (digits[0:1, :fine] * DIGIT + digits[2:3, :fine]).astype(jnp.int32)
    cell_v = (digits[1:2, :fine] * DIGIT + digits[3:4, :fine]).astype(jnp.int32)

    def transform(dft_ref, first, cos, sin):
        held = jnp.concatenate(
            [
                jnp.concatenate(
                    [
                        total[index * 2 * sub + first : index * 2 * sub + first + sub, :fine],
                        total[index * 2 * sub + first : index * 2 * sub + first + sub, fine:],
                    ],
                    axis=0,
                )
                for index in range(pairs_each)
            ],
            axis=1,
        )
        high, low = split_terms(held)
        plain = jnp.dot(
            dft_ref[...], jnp.concatenate([high, high, low], axis=0), preferred_element_type=jnp.float32
        )
        half = plain.shape[0] // 2
        real, imag = plain[:half], plain[half:]
        cos = jnp.concatenate([cos] * pairs_each, axis=1)
        sin = jnp.concatenate([sin] * pairs_each, axis=1)
        return real * cos - imag * sin, real * sin + imag * cos

    row = lax.broadcasted_iota(jnp.int32, (row_total, fine), 0)
    row_real, row_imag = transform(row_dft_ref, 0, *phase(cell_u, row - row_total // 2))
    col = lax.broadcasted_iota(jnp.int32, (MW, fine), 0)
    col_real, col_imag = transform(col_dft_ref, sub, *phase(cell_v, col - MW // 2))
    left = jnp.concatenate([row_real, -row_imag], axis=1).astype(jnp.bfloat16)
    right = jnp.concatenate([col_real, col_imag], axis=1).astype(jnp.bfloat16)
    out_ref[...] = lax.dot_general(left, right, (((1,), (1,)), ((), ())), preferred_element_type=jnp.float32)


def scale_kernel(scale_factor, _, out_ref):
    out_ref[...] = jnp.full(out_ref.shape, scale_factor, out_ref.dtype)


def final_kernel(in_ref, scale_ref, out_ref):
    out_ref[...] = jnp.sum(in_ref[...], axis=0) * scale_ref[...]


def call(kernel, shape, args, flops=0):
    moved = sum(math.prod(leaf.shape) * leaf.dtype.itemsize for leaf in [*jax.tree.leaves(shape), *args])
    return pl.pallas_call(
        kernel,
        out_shape=shape,
        in_specs=[pl.BlockSpec(memory_space=pltpu.VMEM)] * len(args),
        out_specs=jax.tree.map(lambda _: pl.BlockSpec(memory_space=pltpu.VMEM), shape),
        compiler_params=pltpu.CompilerParams(vmem_limit_bytes=VMEM_BYTES),
        cost_estimate=pl.CostEstimate(flops=flops, bytes_accessed=moved, transcendentals=0),
    )(*args)


def local(voltages, station_flags, filter_taps, kernel_rows, kernel_cols, cell_index):
    station_rows, width = voltages.shape[2:]
    taps, two_fine, _ = filter_taps.shape
    sub_u, sub_v = kernel_rows.shape[2], kernel_cols.shape[2]
    chips = lax.axis_size("chip")
    row_total = ROWS_DEV * lax.axis_size(EVERYONE)
    channels = two_fine // 2 * lax.axis_size("role") * lax.axis_size("band")
    frames = width // two_fine - taps + 1
    scale_factor = 4.0 / math.sqrt(channels * sub_u * sub_v) / frames
    each = frames // chips
    count = cell_index.shape[1]
    sub_rows = sub_u + sub_v

    swap = [(core, 1 - core) for core in range(CORES)]
    other = lax.ppermute(voltages, "core", swap)
    tables = call(
        tables_kernel,
        (
            jax.ShapeDtypeStruct((2 * row_total, 6 * sub_u), jnp.bfloat16),
            jax.ShapeDtypeStruct((2 * MW, 6 * sub_v), jnp.bfloat16),
        ),
        (),
        flops=2 * voltages.size * two_fine * taps,
    )
    packed = call(
        pack_kernel,
        jax.ShapeDtypeStruct((8, -(-max(station_rows, count) // 128) * 128), jnp.int32),
        (station_flags.reshape(1, -1), cell_index.reshape(2, -1), tables[0]),
    )
    other_packed = lax.ppermute(packed, "core", swap)
    fixed = (filter_taps, kernel_rows, kernel_cols, packed)
    flops = 2 * station_rows * taps * two_fine * two_fine
    part = call(
        own_kernel,
        jax.ShapeDtypeStruct((frames * sub_rows, two_fine), jnp.float32),
        (voltages, *fixed),
        flops=frames * flops,
    )

    after = ()
    got = []
    for step in [*range(1, chips), 0]:
        made = call(
            functools.partial(sum_kernel, step, each, count),
            jax.ShapeDtypeStruct((each * sub_rows + PAD_ROWS, two_fine), jnp.bfloat16),
            (other, *fixed, other_packed, part, *after),
            flops=each * flops,
        )
        after = (made,)
        if step:
            made = lax.ppermute(made, "chip", [(source, source ^ step) for source in range(chips)])
        got.append(made)
    image = call(
        functools.partial(image_kernel, each),
        jax.ShapeDtypeStruct((row_total, MW), jnp.float32),
        (*got, *tables),
    )
    rows = lax.all_to_all(image, EVERYONE, split_axis=0, concat_axis=0, tiled=True)
    row = jax.ShapeDtypeStruct((ROWS_DEV, MW), jnp.float32)
    scale = call(functools.partial(scale_kernel, scale_factor), row, (image,), flops=2 * image.size * row_total)
    return call(final_kernel, row, (rows.reshape(-1, ROWS_DEV, MW), scale))


def solution(mesh):
    roles, bands, turns = (mesh.shape[name] for name in ("role", "band", "turn"))
    split = Mesh(mesh.devices.reshape(roles, bands, turns // CORES, CORES), EVERYONE)
    in_specs = (
        P(("role", "band"), None, TURN, None),
        P(TURN),
        P(),
        P(("role", "band"), None, None, None),
        P(("role", "band"), None, None, None),
        P(None, EVERYONE, None),
    )
    out_specs = P(EVERYONE, None)
    return jax.shard_map(local, mesh=split, in_specs=in_specs, out_specs=out_specs, check_vma=False)
```

```python
import functools
import math

import jax
import jax.numpy as jnp
from jax import lax
from jax.experimental import pallas as pl
from jax.experimental.pallas import tpu as pltpu
from jax.sharding import Mesh
from jax.sharding import PartitionSpec as P

NGRID = 4096
MW = 128
ROWS_DEV = 1
DIGIT = 64
PAD_ROWS = 16
CORES = 2
TURN = ("chip", "core")
EVERYONE = ("role", "band", *TURN)
PEERS = ("role", "band", "chip")
VMEM_BYTES = 24 * 1024 * 1024


def split_terms(value):
    high = value.astype(jnp.bfloat16)
    return high, (value - high.astype(jnp.float32)).astype(jnp.bfloat16)


def phase(cell, pixel):
    quarter = NGRID // 4
    turned = (cell * pixel) & (NGRID - 1)
    quadrant = (turned + quarter // 2) // quarter
    angle = (turned - quadrant * quarter).astype(jnp.float32) * (2.0 * math.pi / NGRID)
    square = angle * angle
    sine = angle * (1 + square * (-1 / 6 + square * (1 / 120 + square * (-1 / 5040 + square * (1 / 362880)))))
    cosine = 1 + square * (-1 / 2 + square * (1 / 24 + square * (-1 / 720 + square * (1 / 40320))))
    odd = (quadrant & 1) == 1
    real = jnp.where(odd, sine, cosine)
    imag = jnp.where(odd, cosine, sine)
    return (
        jnp.where(((quadrant + 1) & 2) == 2, -real, real),
        jnp.where((quadrant & 2) == 2, -imag, imag),
    )


def tables_kernel(row_ref, col_ref):
    for out_ref, sign in ((row_ref, 1), (col_ref, -1)):
        pixels, cells = out_ref.shape[0] // 2, out_ref.shape[1] // 6
        place = lax.broadcasted_iota(jnp.int32, (2 * pixels, 2 * cells), 0)
        lane = lax.broadcasted_iota(jnp.int32, (2 * pixels, 2 * cells), 1)
        lower, right = place >= pixels, lane >= cells
        pixel = jnp.where(lower, place - pixels, place)
        pixel = (row_order(pixel, pixels) if sign > 0 else pixel) - pixels // 2
        cos, sin = phase(jnp.where(right, lane - cells, lane), pixel)
        value = jnp.where(lower == right, cos, sin)
        value = jnp.where(right & (lower == (sign < 0)), -value, value)
        high, low = split_terms(value)
        out_ref[...] = jnp.concatenate([high, low, high], axis=1)


def pack_kernel(flags_ref, cells_ref, _, out_ref):
    out_ref[...] = jnp.zeros_like(out_ref)
    out_ref[0:2, : cells_ref.shape[1]] = cells_ref[...]
    out_ref[2:3, : flags_ref.shape[1]] = flags_ref[...]


def gridding_weights(rows_ref, cols_ref, packed_ref, turn, stations):
    both = jnp.concatenate([rows_ref[0, 0], cols_ref[0, 0]], axis=0).astype(jnp.float32)
    weights = jnp.zeros((both.shape[0], stations), jnp.float32)
    for group in range(lax.axis_size(TURN)):
        weights = jnp.where(turn == group, both[:, group * stations : (group + 1) * stations], weights)
    return (weights * packed_ref[2:3, :stations].astype(jnp.float32)).astype(jnp.bfloat16)


def cell_digits(packed_refs, count, lanes):
    turn = lax.axis_index(TURN)
    digits = jnp.zeros((4, lanes), jnp.float32)
    for index, packed in enumerate(packed_refs):
        place = turn ^ index
        wide = jnp.concatenate([packed[0:2, :count]] * (lanes // count), axis=1)
        lane = lax.broadcasted_iota(jnp.int32, wide.shape, 1)
        wide = jnp.where((lane >= place * count) & (lane < (place + 1) * count), wide, 0)
        digits = digits + jnp.concatenate([wide // DIGIT, wide % DIGIT], axis=0).astype(jnp.float32)
    digits = jnp.concatenate([digits, jnp.zeros((PAD_ROWS - 4, lanes), jnp.float32)], axis=0)
    return digits.astype(jnp.bfloat16)


def gridded_frames(volt_ref, taps_ref, weights, firsts):
    taps, two_fine, _ = taps_ref.shape
    stations = volt_ref.shape[2]
    core = lax.axis_index("core")
    lhs = jnp.concatenate(
        [
            volt_ref[0, core, :, pl.ds(pl.multiple_of(first * two_fine, two_fine), taps * two_fine)]
            for first in firsts
        ],
        axis=0,
    )
    filt = taps_ref[...].reshape(taps * two_fine, two_fine)
    spectra = jnp.dot(lhs, filt, preferred_element_type=jnp.float32).astype(jnp.bfloat16)
    return [
        jnp.dot(weights, spectra[index * stations : (index + 1) * stations], preferred_element_type=jnp.float32)
        for index in range(len(firsts))
    ]


def own_kernel(volt_ref, taps_ref, rows_ref, cols_ref, packed_ref, out_ref):
    weights = gridding_weights(rows_ref, cols_ref, packed_ref, lax.axis_index(TURN), volt_ref.shape[2])
    rows = weights.shape[0]
    for frame, gridded in enumerate(gridded_frames(volt_ref, taps_ref, weights, range(out_ref.shape[0] // rows))):
        out_ref[frame * rows : (frame + 1) * rows] = gridded


def sum_kernel(step, each, count, volt_ref, taps_ref, rows_ref, cols_ref, own_ref, packed_ref, part_ref, *refs):
    out_ref = refs[-1]
    weights = gridding_weights(rows_ref, cols_ref, packed_ref, lax.axis_index(TURN) ^ 1, volt_ref.shape[2])
    rows = weights.shape[0]
    firsts = [(lax.axis_index("chip") ^ step) * each + frame for frame in range(each)]
    for index, gridded in enumerate(gridded_frames(volt_ref, taps_ref, weights, firsts)):
        held = part_ref[pl.ds(pl.multiple_of(firsts[index] * rows, rows), rows)]
        out_ref[index * rows : (index + 1) * rows] = (held + gridded).astype(jnp.bfloat16)
    out_ref[each * rows :] = cell_digits((own_ref, packed_ref), count, out_ref.shape[1])


def row_order(place, row_total):
    owners = row_total // ROWS_DEV // CORES
    owner, here = place // ROWS_DEV, place % ROWS_DEV
    return (owner % owners * CORES + owner // owners) * ROWS_DEV + here


def image_kernel(pairs_each, *refs):
    *got, row_dft_ref, col_dft_ref, kept_ref, given_ref, held_ref = refs
    fine = got[0].shape[1] // 2
    sub = row_dft_ref.shape[1] // 6
    row_total = held_ref.shape[0]
    total = got[0][...].astype(jnp.float32)
    for source in got[1:]:
        total = total + source[...].astype(jnp.float32)
    digits = total[pairs_each * 2 * sub :]
    cell_u = (digits[0:1, :fine] * DIGIT + digits[2:3, :fine]).astype(jnp.int32)
    cell_v = (digits[1:2, :fine] * DIGIT + digits[3:4, :fine]).astype(jnp.int32)

    def transform(dft_ref, first, cos, sin):
        held = jnp.concatenate(
            [
                jnp.concatenate(
                    [
                        total[index * 2 * sub + first : index * 2 * sub + first + sub, :fine],
                        total[index * 2 * sub + first : index * 2 * sub + first + sub, fine:],
                    ],
                    axis=0,
                )
                for index in range(pairs_each)
            ],
            axis=1,
        )
        high, low = split_terms(held)
        plain = jnp.dot(
            dft_ref[...], jnp.concatenate([high, high, low], axis=0), preferred_element_type=jnp.float32
        )
        half = plain.shape[0] // 2
        real, imag = plain[:half], plain[half:]
        cos = jnp.concatenate([cos] * pairs_each, axis=1)
        sin = jnp.concatenate([sin] * pairs_each, axis=1)
        return real * cos - imag * sin, real * sin + imag * cos

    row = row_order(lax.broadcasted_iota(jnp.int32, (row_total, fine), 0), row_total)
    row_real, row_imag = transform(row_dft_ref, 0, *phase(cell_u, row - row_total // 2))
    col = lax.broadcasted_iota(jnp.int32, (MW, fine), 0)
    col_real, col_imag = transform(col_dft_ref, sub, *phase(cell_v, col - MW // 2))
    left = jnp.concatenate([row_real, -row_imag], axis=1).astype(jnp.bfloat16)
    right = jnp.concatenate([col_real, col_imag], axis=1).astype(jnp.bfloat16)
    held_ref[...] = lax.dot_general(left, right, (((1,), (1,)), ((), ())), preferred_element_type=jnp.float32)
    core, half = lax.axis_index("core"), row_total // CORES
    kept_ref[...] = held_ref[pl.ds(core * half, half)]
    given_ref[...] = held_ref[pl.ds((1 - core) * half, half)]


def add_kernel(left_ref, right_ref, out_ref, first_ref):
    out_ref[...] = left_ref[...] + right_ref[...]
    first_ref[...] = out_ref[: first_ref.shape[0]]


def scale_kernel(scale_factor, _, out_ref):
    out_ref[...] = jnp.full(out_ref.shape, scale_factor, out_ref.dtype)


def final_kernel(in_ref, scale_ref, out_ref):
    out_ref[...] = jnp.sum(in_ref[...], axis=0) * scale_ref[...]


def call(kernel, shape, args, scratch=(), flops=0):
    moved = sum(math.prod(leaf.shape) * leaf.dtype.itemsize for leaf in [*jax.tree.leaves(shape), *args])
    return pl.pallas_call(
        kernel,
        out_shape=shape,
        in_specs=[pl.BlockSpec(memory_space=pltpu.VMEM)] * len(args),
        out_specs=jax.tree.map(lambda _: pl.BlockSpec(memory_space=pltpu.VMEM), shape),
        scratch_shapes=scratch,
        compiler_params=pltpu.CompilerParams(vmem_limit_bytes=VMEM_BYTES),
        cost_estimate=pl.CostEstimate(flops=flops, bytes_accessed=moved, transcendentals=0),
    )(*args)


def local(voltages, station_flags, filter_taps, kernel_rows, kernel_cols, cell_index):
    station_rows, width = voltages.shape[2:]
    taps, two_fine, _ = filter_taps.shape
    sub_u, sub_v = kernel_rows.shape[2], kernel_cols.shape[2]
    chips = lax.axis_size("chip")
    row_total = ROWS_DEV * lax.axis_size(EVERYONE)
    channels = two_fine // 2 * lax.axis_size("role") * lax.axis_size("band")
    frames = width // two_fine - taps + 1
    scale_factor = 4.0 / math.sqrt(channels * sub_u * sub_v) / frames
    each = frames // chips
    count = cell_index.shape[1]
    sub_rows = sub_u + sub_v

    swap = [(core, 1 - core) for core in range(CORES)]
    other = lax.ppermute(voltages, "core", swap)
    tables = call(
        tables_kernel,
        (
            jax.ShapeDtypeStruct((2 * row_total, 6 * sub_u), jnp.bfloat16),
            jax.ShapeDtypeStruct((2 * MW, 6 * sub_v), jnp.bfloat16),
        ),
        (),
        flops=2 * voltages.size * two_fine * taps,
    )
    packed = call(
        pack_kernel,
        jax.ShapeDtypeStruct((8, -(-max(station_rows, count) // 128) * 128), jnp.int32),
        (station_flags.reshape(1, -1), cell_index.reshape(2, -1), tables[0]),
    )
    other_packed = lax.ppermute(packed, "core", swap)
    fixed = (filter_taps, kernel_rows, kernel_cols, packed)
    flops = 2 * station_rows * taps * two_fine * two_fine
    part = call(
        own_kernel,
        jax.ShapeDtypeStruct((frames * sub_rows, two_fine), jnp.float32),
        (voltages, *fixed),
        flops=frames * flops,
    )

    after = ()
    got = []
    for step in [*range(1, chips), 0]:
        made = call(
            functools.partial(sum_kernel, step, each, count),
            jax.ShapeDtypeStruct((each * sub_rows + PAD_ROWS, two_fine), jnp.bfloat16),
            (other, *fixed, other_packed, part, *after),
            flops=each * flops,
        )
        after = (made,)
        if step:
            made = lax.ppermute(made, "chip", [(source, source ^ step) for source in range(chips)])
        got.append(made)
    half = jax.ShapeDtypeStruct((row_total // CORES, MW), jnp.float32)
    kept, given = call(
        functools.partial(image_kernel, each),
        (half, half),
        (*got, *tables),
        scratch=[pltpu.VMEM((row_total, MW), jnp.float32)],
    )
    row = jax.ShapeDtypeStruct((ROWS_DEV, MW), jnp.float32)
    image, first = call(add_kernel, (half, row), (kept, lax.ppermute(given, "core", swap)))
    rows = lax.all_to_all(image, PEERS, split_axis=0, concat_axis=0, tiled=True)
    scale = call(functools.partial(scale_kernel, scale_factor), row, (first,), flops=2 * image.size * row_total)
    return call(final_kernel, row, (rows.reshape(-1, ROWS_DEV, MW), scale))


def solution(mesh):
    roles, bands, turns = (mesh.shape[name] for name in ("role", "band", "turn"))
    split = Mesh(mesh.devices.reshape(roles, bands, turns // CORES, CORES), EVERYONE)
    in_specs = (
        P(("role", "band"), None, TURN, None),
        P(TURN),
        P(),
        P(("role", "band"), None, None, None),
        P(("role", "band"), None, None, None),
        P(None, EVERYONE, None),
    )
    out_specs = P(EVERYONE, None)
    return jax.shard_map(local, mesh=split, in_specs=in_specs, out_specs=out_specs, check_vma=False)
```

```python
import functools
import math

import jax
import jax.numpy as jnp
from jax import lax
from jax.experimental import pallas as pl
from jax.experimental.pallas import tpu as pltpu
from jax.sharding import Mesh
from jax.sharding import PartitionSpec as P

NGRID = 4096
MW = 128
ROWS_DEV = 1
DIGIT = 64
PAD_ROWS = 16
CORES = 2
TURN = ("chip", "core")
EVERYONE = ("role", "band", *TURN)
VMEM_BYTES = 24 * 1024 * 1024


def split_terms(value):
    high = value.astype(jnp.bfloat16)
    return high, (value - high.astype(jnp.float32)).astype(jnp.bfloat16)


def phase(cell, pixel):
    quarter = NGRID // 4
    turned = (cell * pixel) & (NGRID - 1)
    quadrant = (turned + quarter // 2) // quarter
    angle = (turned - quadrant * quarter).astype(jnp.float32) * (2.0 * math.pi / NGRID)
    square = angle * angle
    sine = angle * (1 + square * (-1 / 6 + square * (1 / 120 + square * (-1 / 5040 + square * (1 / 362880)))))
    cosine = 1 + square * (-1 / 2 + square * (1 / 24 + square * (-1 / 720 + square * (1 / 40320))))
    odd = (quadrant & 1) == 1
    real = jnp.where(odd, sine, cosine)
    imag = jnp.where(odd, cosine, sine)
    return (
        jnp.where(((quadrant + 1) & 2) == 2, -real, real),
        jnp.where((quadrant & 2) == 2, -imag, imag),
    )


def tables_kernel(row_ref, col_ref):
    for out_ref, sign in ((row_ref, 1), (col_ref, -1)):
        pixels, cells = out_ref.shape[0] // 2, out_ref.shape[1] // 6
        place = lax.broadcasted_iota(jnp.int32, (2 * pixels, 2 * cells), 0)
        lane = lax.broadcasted_iota(jnp.int32, (2 * pixels, 2 * cells), 1)
        lower, right = place >= pixels, lane >= cells
        pixel = jnp.where(lower, place - pixels, place) - pixels // 2
        cos, sin = phase(jnp.where(right, lane - cells, lane), pixel)
        value = jnp.where(lower == right, cos, sin)
        value = jnp.where(right & (lower == (sign < 0)), -value, value)
        high, low = split_terms(value)
        out_ref[...] = jnp.concatenate([high, low, high], axis=1)


def pack_kernel(flags_ref, cells_ref, rows_ref, cols_ref, _, packed_ref, *weights_refs):
    turn, turns = lax.axis_index(TURN), lax.axis_size(TURN)
    count, lanes = cells_ref.shape[1], packed_ref.shape[1]
    wide = jnp.concatenate([cells_ref[...]] * (lanes // count), axis=1)
    lane = lax.broadcasted_iota(jnp.int32, wide.shape, 1)
    wide = jnp.where((lane >= turn * count) & (lane < (turn + 1) * count), wide, 0)
    packed_ref[...] = jnp.zeros_like(packed_ref)
    packed_ref[0:2] = (wide // DIGIT).astype(jnp.float32)
    packed_ref[2:4] = (wide % DIGIT).astype(jnp.float32)
    packed_ref[4:5, : flags_ref.shape[1]] = flags_ref[...].astype(jnp.float32)
    both = jnp.concatenate([rows_ref[0, 0], cols_ref[0, 0]], axis=0).astype(jnp.float32)
    for index, weights_ref in enumerate(weights_refs):
        stations = weights_ref.shape[1]
        weights = jnp.zeros(weights_ref.shape, jnp.float32)
        for group in range(turns):
            piece = both[:, group * stations : (group + 1) * stations]
            weights = jnp.where(turn ^ index == group, piece, weights)
        weights_ref[...] = weights


def flagged(weights_ref, packed_ref):
    return (weights_ref[...] * packed_ref[4:5, : weights_ref.shape[1]]).astype(jnp.bfloat16)


def gridded_frames(volt_ref, taps_ref, weights, firsts):
    taps, two_fine, _ = taps_ref.shape
    stations = volt_ref.shape[2]
    core = lax.axis_index("core")
    lhs = jnp.concatenate(
        [
            volt_ref[0, core, :, pl.ds(pl.multiple_of(first * two_fine, two_fine), taps * two_fine)]
            for first in firsts
        ],
        axis=0,
    )
    filt = taps_ref[...].reshape(taps * two_fine, two_fine)
    spectra = jnp.dot(lhs, filt, preferred_element_type=jnp.float32).astype(jnp.bfloat16)
    return [
        jnp.dot(weights, spectra[index * stations : (index + 1) * stations], preferred_element_type=jnp.float32)
        for index in range(len(firsts))
    ]


def own_kernel(volt_ref, taps_ref, weights_ref, packed_ref, out_ref):
    rows = weights_ref.shape[0]
    firsts = range(out_ref.shape[0] // rows)
    for frame, gridded in enumerate(gridded_frames(volt_ref, taps_ref, flagged(weights_ref, packed_ref), firsts)):
        out_ref[frame * rows : (frame + 1) * rows] = gridded


def sum_kernel(step, each, volt_ref, taps_ref, weights_ref, own_ref, packed_ref, part_ref, *refs):
    out_ref = refs[-1]
    rows = weights_ref.shape[0]
    firsts = [(lax.axis_index("chip") ^ step) * each + frame for frame in range(each)]
    for index, gridded in enumerate(gridded_frames(volt_ref, taps_ref, flagged(weights_ref, packed_ref), firsts)):
        held = part_ref[pl.ds(pl.multiple_of(firsts[index] * rows, rows), rows)]
        out_ref[index * rows : (index + 1) * rows] = (held + gridded).astype(jnp.bfloat16)
    digits = own_ref[...] + packed_ref[...]
    digits = jnp.concatenate([digits, jnp.zeros((PAD_ROWS - digits.shape[0], digits.shape[1]), jnp.float32)], axis=0)
    out_ref[each * rows :] = digits.astype(jnp.bfloat16)


def image_kernel(pairs_each, *refs):
    *got, row_dft_ref, col_dft_ref, out_ref = refs
    fine = got[0].shape[1] // 2
    sub = row_dft_ref.shape[1] // 6
    row_total = out_ref.shape[0]
    total = got[0][...].astype(jnp.float32)
    for source in got[1:]:
        total = total + source[...].astype(jnp.float32)
    digits = total[pairs_each * 2 * sub :]
    cell_u = (digits[0:1, :fine] * DIGIT + digits[2:3, :fine]).astype(jnp.int32)
    cell_v = (digits[1:2, :fine] * DIGIT + digits[3:4, :fine]).astype(jnp.int32)

    def transform(dft_ref, first, cos, sin):
        held = jnp.concatenate(
            [
                jnp.concatenate(
                    [
                        total[index * 2 * sub + first : index * 2 * sub + first + sub, :fine],
                        total[index * 2 * sub + first : index * 2 * sub + first + sub, fine:],
                    ],
                    axis=0,
                )
                for index in range(pairs_each)
            ],
            axis=1,
        )
        high, low = split_terms(held)
        plain = jnp.dot(
            dft_ref[...], jnp.concatenate([high, high, low], axis=0), preferred_element_type=jnp.float32
        )
        half = plain.shape[0] // 2
        real, imag = plain[:half], plain[half:]
        cos = jnp.concatenate([cos] * pairs_each, axis=1)
        sin = jnp.concatenate([sin] * pairs_each, axis=1)
        return real * cos - imag * sin, real * sin + imag * cos

    row = lax.broadcasted_iota(jnp.int32, (row_total, fine), 0)
    row_real, row_imag = transform(row_dft_ref, 0, *phase(cell_u, row - row_total // 2))
    col = lax.broadcasted_iota(jnp.int32, (MW, fine), 0)
    col_real, col_imag = transform(col_dft_ref, sub, *phase(cell_v, col - MW // 2))
    left = jnp.concatenate([row_real, -row_imag], axis=1).astype(jnp.bfloat16)
    right = jnp.concatenate([col_real, col_imag], axis=1).astype(jnp.bfloat16)
    out_ref[...] = lax.dot_general(left, right, (((1,), (1,)), ((), ())), preferred_element_type=jnp.float32)


def final_kernel(scale_factor, in_ref, out_ref):
    out_ref[...] = jnp.sum(in_ref[...], axis=0) * scale_factor


def call(kernel, shape, args, flops=0):
    moved = sum(math.prod(leaf.shape) * leaf.dtype.itemsize for leaf in [*jax.tree.leaves(shape), *args])
    return pl.pallas_call(
        kernel,
        out_shape=shape,
        in_specs=[pl.BlockSpec(memory_space=pltpu.VMEM)] * len(args),
        out_specs=jax.tree.map(lambda _: pl.BlockSpec(memory_space=pltpu.VMEM), shape),
        compiler_params=pltpu.CompilerParams(vmem_limit_bytes=VMEM_BYTES),
        cost_estimate=pl.CostEstimate(flops=flops, bytes_accessed=moved, transcendentals=0),
    )(*args)


def local(voltages, station_flags, filter_taps, kernel_rows, kernel_cols, cell_index):
    station_rows, width = voltages.shape[2:]
    taps, two_fine, _ = filter_taps.shape
    sub_u, sub_v = kernel_rows.shape[2], kernel_cols.shape[2]
    chips = lax.axis_size("chip")
    row_total = ROWS_DEV * lax.axis_size(EVERYONE)
    channels = two_fine // 2 * lax.axis_size("role") * lax.axis_size("band")
    frames = width // two_fine - taps + 1
    scale_factor = 4.0 / math.sqrt(channels * sub_u * sub_v) / frames
    each = frames // chips
    sub_rows = sub_u + sub_v

    swap = [(core, 1 - core) for core in range(CORES)]
    other = lax.ppermute(voltages, "core", swap)
    tables = call(
        tables_kernel,
        (
            jax.ShapeDtypeStruct((2 * row_total, 6 * sub_u), jnp.bfloat16),
            jax.ShapeDtypeStruct((2 * MW, 6 * sub_v), jnp.bfloat16),
        ),
        (),
        flops=2 * voltages.size * two_fine * taps,
    )
    weights = jax.ShapeDtypeStruct((sub_rows, station_rows), jnp.float32)
    packed, own_weights, other_weights = call(
        pack_kernel,
        (jax.ShapeDtypeStruct((8, two_fine), jnp.float32), weights, weights),
        (station_flags.reshape(1, -1), cell_index.reshape(2, -1), kernel_rows, kernel_cols, tables[0]),
    )
    other_packed = lax.ppermute(packed, "core", swap)
    flops = 2 * station_rows * taps * two_fine * two_fine
    part = call(
        own_kernel,
        jax.ShapeDtypeStruct((frames * sub_rows, two_fine), jnp.float32),
        (voltages, filter_taps, own_weights, packed),
        flops=frames * flops,
    )

    after = ()
    got = []
    for step in [*range(1, chips), 0]:
        made = call(
            functools.partial(sum_kernel, step, each),
            jax.ShapeDtypeStruct((each * sub_rows + PAD_ROWS, two_fine), jnp.bfloat16),
            (other, filter_taps, other_weights, packed, other_packed, part, *after),
            flops=each * flops,
        )
        after = (made,)
        if step:
            made = lax.ppermute(made, "chip", [(source, source ^ step) for source in range(chips)])
        got.append(made)
    image = call(
        functools.partial(image_kernel, each),
        jax.ShapeDtypeStruct((row_total, MW), jnp.float32),
        (*got, *tables),
    )
    rows = lax.all_to_all(image, EVERYONE, split_axis=0, concat_axis=0, tiled=True)
    return call(
        functools.partial(final_kernel, scale_factor),
        jax.ShapeDtypeStruct((ROWS_DEV, MW), jnp.float32),
        (rows.reshape(-1, ROWS_DEV, MW),),
    )


def solution(mesh):
    roles, bands, turns = (mesh.shape[name] for name in ("role", "band", "turn"))
    split = Mesh(mesh.devices.reshape(roles, bands, turns // CORES, CORES), EVERYONE)
    in_specs = (
        P(("role", "band"), None, TURN, None),
        P(TURN),
        P(),
        P(("role", "band"), None, None, None),
        P(("role", "band"), None, None, None),
        P(None, EVERYONE, None),
    )
    out_specs = P(EVERYONE, None)
    return jax.shard_map(local, mesh=split, in_specs=in_specs, out_specs=out_specs, check_vma=False)
```

```python
import functools
import math

import jax
import jax.numpy as jnp
from jax import lax
from jax.experimental import pallas as pl
from jax.experimental.pallas import tpu as pltpu
from jax.sharding import Mesh
from jax.sharding import PartitionSpec as P

NGRID = 4096
MW = 128
ROWS_DEV = 1
DIGIT = 64
PAD_ROWS = 16
CORES = 2
TURN = ("chip", "core")
EVERYONE = ("role", "band", *TURN)
VMEM_BYTES = 24 * 1024 * 1024


def split_terms(value):
    high = value.astype(jnp.bfloat16)
    return high, (value - high.astype(jnp.float32)).astype(jnp.bfloat16)


def phase(cell, pixel):
    quarter = NGRID // 4
    turned = (cell * pixel) & (NGRID - 1)
    quadrant = (turned + quarter // 2) // quarter
    angle = (turned - quadrant * quarter).astype(jnp.float32) * (2.0 * math.pi / NGRID)
    square = angle * angle
    sine = angle * (1 + square * (-1 / 6 + square * (1 / 120 + square * (-1 / 5040 + square * (1 / 362880)))))
    cosine = 1 + square * (-1 / 2 + square * (1 / 24 + square * (-1 / 720 + square * (1 / 40320))))
    odd = (quadrant & 1) == 1
    real = jnp.where(odd, sine, cosine)
    imag = jnp.where(odd, cosine, sine)
    return (
        jnp.where(((quadrant + 1) & 2) == 2, -real, real),
        jnp.where((quadrant & 2) == 2, -imag, imag),
    )


def tables_kernel(row_ref, col_ref):
    for out_ref, sign in ((row_ref, 1), (col_ref, -1)):
        pixels, cells = out_ref.shape[0] // 2, out_ref.shape[1] // 6
        place = lax.broadcasted_iota(jnp.int32, (2 * pixels, 2 * cells), 0)
        lane = lax.broadcasted_iota(jnp.int32, (2 * pixels, 2 * cells), 1)
        lower, right = place >= pixels, lane >= cells
        pixel = jnp.where(lower, place - pixels, place) - pixels // 2
        cos, sin = phase(jnp.where(right, lane - cells, lane), pixel)
        value = jnp.where(lower == right, cos, sin)
        value = jnp.where(right & (lower == (sign < 0)), -value, value)
        high, low = split_terms(value)
        out_ref[...] = jnp.concatenate([high, low, high], axis=1)


def pack_kernel(flags_ref, cells_ref, _rows_ref, _cols_ref, _table_ref, packed_ref):
    turn = lax.axis_index(TURN)
    count, lanes = cells_ref.shape[1], packed_ref.shape[1]
    wide = jnp.concatenate([cells_ref[...]] * (lanes // count), axis=1)
    lane = lax.broadcasted_iota(jnp.int32, wide.shape, 1)
    wide = jnp.where((lane >= turn * count) & (lane < (turn + 1) * count), wide, 0)
    packed_ref[...] = jnp.zeros_like(packed_ref)
    packed_ref[0:2] = (wide // DIGIT).astype(jnp.float32)
    packed_ref[2:4] = (wide % DIGIT).astype(jnp.float32)
    packed_ref[4:5, : flags_ref.shape[1]] = flags_ref[...].astype(jnp.float32)


def gridding_weights(rows_ref, cols_ref, packed_ref, turn, stations):
    both = jnp.concatenate([rows_ref[0, 0], cols_ref[0, 0]], axis=0).astype(jnp.float32)
    weights = jnp.zeros((both.shape[0], stations), jnp.float32)
    for group in range(lax.axis_size(TURN)):
        weights = jnp.where(turn == group, both[:, group * stations : (group + 1) * stations], weights)
    return (weights * packed_ref[4:5, :stations]).astype(jnp.bfloat16)


def gridded_frames(volt_ref, taps_ref, weights, firsts):
    taps, two_fine, _ = taps_ref.shape
    stations = volt_ref.shape[2]
    core = lax.axis_index("core")
    lhs = jnp.concatenate(
        [
            volt_ref[0, core, :, pl.ds(pl.multiple_of(first * two_fine, two_fine), taps * two_fine)]
            for first in firsts
        ],
        axis=0,
    )
    filt = taps_ref[...].reshape(taps * two_fine, two_fine)
    spectra = jnp.dot(lhs, filt, preferred_element_type=jnp.float32).astype(jnp.bfloat16)
    beside = jnp.concatenate(
        [spectra[index * stations : (index + 1) * stations] for index in range(len(firsts))], axis=1
    )
    gridded = jnp.dot(weights, beside, preferred_element_type=jnp.float32)
    return [gridded[:, index * two_fine : (index + 1) * two_fine] for index in range(len(firsts))]


def own_kernel(volt_ref, taps_ref, rows_ref, cols_ref, packed_ref, out_ref):
    weights = gridding_weights(rows_ref, cols_ref, packed_ref, lax.axis_index(TURN), volt_ref.shape[2])
    rows = weights.shape[0]
    for frame, gridded in enumerate(gridded_frames(volt_ref, taps_ref, weights, range(out_ref.shape[0] // rows))):
        out_ref[frame * rows : (frame + 1) * rows] = gridded


def sum_kernel(step, each, volt_ref, taps_ref, rows_ref, cols_ref, own_ref, packed_ref, part_ref, *refs):
    out_ref = refs[-1]
    weights = gridding_weights(rows_ref, cols_ref, packed_ref, lax.axis_index(TURN) ^ 1, volt_ref.shape[2])
    rows = weights.shape[0]
    firsts = [(lax.axis_index("chip") ^ step) * each + frame for frame in range(each)]
    for index, gridded in enumerate(gridded_frames(volt_ref, taps_ref, weights, firsts)):
        held = part_ref[pl.ds(pl.multiple_of(firsts[index] * rows, rows), rows)]
        out_ref[index * rows : (index + 1) * rows] = (held + gridded).astype(jnp.bfloat16)
    digits = own_ref[...] + packed_ref[...]
    digits = jnp.concatenate([digits, jnp.zeros((PAD_ROWS - digits.shape[0], digits.shape[1]), jnp.float32)], axis=0)
    out_ref[each * rows :] = digits.astype(jnp.bfloat16)


def image_kernel(pairs_each, *refs):
    *got, row_dft_ref, col_dft_ref, out_ref = refs
    fine = got[0].shape[1] // 2
    sub = row_dft_ref.shape[1] // 6
    row_total = out_ref.shape[0]
    total = got[0][...].astype(jnp.float32)
    for source in got[1:]:
        total = total + source[...].astype(jnp.float32)
    digits = total[pairs_each * 2 * sub :]
    cell_u = (digits[0:1, :fine] * DIGIT + digits[2:3, :fine]).astype(jnp.int32)
    cell_v = (digits[1:2, :fine] * DIGIT + digits[3:4, :fine]).astype(jnp.int32)

    def transform(dft_ref, first, cos, sin):
        held = jnp.concatenate(
            [
                jnp.concatenate(
                    [
                        total[index * 2 * sub + first : index * 2 * sub + first + sub, :fine],
                        total[index * 2 * sub + first : index * 2 * sub + first + sub, fine:],
                    ],
                    axis=0,
                )
                for index in range(pairs_each)
            ],
            axis=1,
        )
        high, low = split_terms(held)
        plain = jnp.dot(
            dft_ref[...], jnp.concatenate([high, high, low], axis=0), preferred_element_type=jnp.float32
        )
        half = plain.shape[0] // 2
        real, imag = plain[:half], plain[half:]
        cos = jnp.concatenate([cos] * pairs_each, axis=1)
        sin = jnp.concatenate([sin] * pairs_each, axis=1)
        return real * cos - imag * sin, real * sin + imag * cos

    row = lax.broadcasted_iota(jnp.int32, (row_total, fine), 0)
    row_real, row_imag = transform(row_dft_ref, 0, *phase(cell_u, row - row_total // 2))
    col = lax.broadcasted_iota(jnp.int32, (MW, fine), 0)
    col_real, col_imag = transform(col_dft_ref, sub, *phase(cell_v, col - MW // 2))
    left = jnp.concatenate([row_real, -row_imag], axis=1).astype(jnp.bfloat16)
    right = jnp.concatenate([col_real, col_imag], axis=1).astype(jnp.bfloat16)
    out_ref[...] = lax.dot_general(left, right, (((1,), (1,)), ((), ())), preferred_element_type=jnp.float32)


def final_kernel(scale_factor, in_ref, out_ref):
    out_ref[...] = jnp.sum(in_ref[...], axis=0) * scale_factor


def call(kernel, shape, args, flops=0):
    moved = sum(math.prod(leaf.shape) * leaf.dtype.itemsize for leaf in [*jax.tree.leaves(shape), *args])
    return pl.pallas_call(
        kernel,
        out_shape=shape,
        in_specs=[pl.BlockSpec(memory_space=pltpu.VMEM)] * len(args),
        out_specs=jax.tree.map(lambda _: pl.BlockSpec(memory_space=pltpu.VMEM), shape),
        compiler_params=pltpu.CompilerParams(vmem_limit_bytes=VMEM_BYTES),
        cost_estimate=pl.CostEstimate(flops=flops, bytes_accessed=moved, transcendentals=0),
    )(*args)


def local(voltages, station_flags, filter_taps, kernel_rows, kernel_cols, cell_index):
    station_rows, width = voltages.shape[2:]
    taps, two_fine, _ = filter_taps.shape
    sub_u, sub_v = kernel_rows.shape[2], kernel_cols.shape[2]
    chips = lax.axis_size("chip")
    row_total = ROWS_DEV * lax.axis_size(EVERYONE)
    channels = two_fine // 2 * lax.axis_size("role") * lax.axis_size("band")
    frames = width // two_fine - taps + 1
    scale_factor = 4.0 / math.sqrt(channels * sub_u * sub_v) / frames
    each = frames // chips
    sub_rows = sub_u + sub_v

    swap = [(core, 1 - core) for core in range(CORES)]
    other = lax.ppermute(voltages, "core", swap)
    tables = call(
        tables_kernel,
        (
            jax.ShapeDtypeStruct((2 * row_total, 6 * sub_u), jnp.bfloat16),
            jax.ShapeDtypeStruct((2 * MW, 6 * sub_v), jnp.bfloat16),
        ),
        (),
        flops=2 * voltages.size * two_fine * taps,
    )
    packed = call(
        pack_kernel,
        jax.ShapeDtypeStruct((8, two_fine), jnp.float32),
        (station_flags.reshape(1, -1), cell_index.reshape(2, -1), kernel_rows, kernel_cols, tables[0]),
    )
    other_packed = lax.ppermute(packed, "core", swap)
    flops = 2 * station_rows * taps * two_fine * two_fine
    part = call(
        own_kernel,
        jax.ShapeDtypeStruct((frames * sub_rows, two_fine), jnp.float32),
        (voltages, filter_taps, kernel_rows, kernel_cols, packed),
        flops=frames * flops,
    )

    after = ()
    got = []
    for step in [*range(1, chips), 0]:
        made = call(
            functools.partial(sum_kernel, step, each),
            jax.ShapeDtypeStruct((each * sub_rows + PAD_ROWS, two_fine), jnp.bfloat16),
            (other, filter_taps, kernel_rows, kernel_cols, packed, other_packed, part, *after),
            flops=each * flops,
        )
        after = (made,)
        if step:
            made = lax.ppermute(made, "chip", [(source, source ^ step) for source in range(chips)])
        got.append(made)
    image = call(
        functools.partial(image_kernel, each),
        jax.ShapeDtypeStruct((row_total, MW), jnp.float32),
        (*got, *tables),
    )
    rows = lax.all_to_all(image, EVERYONE, split_axis=0, concat_axis=0, tiled=True)
    return call(
        functools.partial(final_kernel, scale_factor),
        jax.ShapeDtypeStruct((ROWS_DEV, MW), jnp.float32),
        (rows.reshape(-1, ROWS_DEV, MW),),
    )


def solution(mesh):
    roles, bands, turns = (mesh.shape[name] for name in ("role", "band", "turn"))
    split = Mesh(mesh.devices.reshape(roles, bands, turns // CORES, CORES), EVERYONE)
    in_specs = (
        P(("role", "band"), None, TURN, None),
        P(TURN),
        P(),
        P(("role", "band"), None, None, None),
        P(("role", "band"), None, None, None),
        P(None, EVERYONE, None),
    )
    out_specs = P(EVERYONE, None)
    return jax.shard_map(local, mesh=split, in_specs=in_specs, out_specs=out_specs, check_vma=False)
```

```python
import functools
import math

import jax
import jax.numpy as jnp
from jax import lax
from jax.experimental import pallas as pl
from jax.experimental.pallas import tpu as pltpu
from jax.sharding import Mesh
from jax.sharding import PartitionSpec as P

NGRID = 4096
MW = 128
ROWS_DEV = 1
DIGIT = 64
PAD_ROWS = 16
CORES = 2
TURN = ("chip", "core")
EVERYONE = ("role", "band", *TURN)
VMEM_BYTES = 24 * 1024 * 1024


def split_terms(value):
    high = value.astype(jnp.bfloat16)
    return high, (value - high.astype(jnp.float32)).astype(jnp.bfloat16)


def phase(cell, pixel):
    quarter = NGRID // 4
    turned = (cell * pixel) & (NGRID - 1)
    quadrant = (turned + quarter // 2) // quarter
    angle = (turned - quadrant * quarter).astype(jnp.float32) * (2.0 * math.pi / NGRID)
    square = angle * angle
    sine = angle * (1 + square * (-1 / 6 + square * (1 / 120 + square * (-1 / 5040 + square * (1 / 362880)))))
    cosine = 1 + square * (-1 / 2 + square * (1 / 24 + square * (-1 / 720 + square * (1 / 40320))))
    odd = (quadrant & 1) == 1
    real = jnp.where(odd, sine, cosine)
    imag = jnp.where(odd, cosine, sine)
    return (
        jnp.where(((quadrant + 1) & 2) == 2, -real, real),
        jnp.where((quadrant & 2) == 2, -imag, imag),
    )


def tables_kernel(row_ref, col_ref):
    for out_ref, sign in ((row_ref, 1), (col_ref, -1)):
        pixels, cells = out_ref.shape[0] // 2, out_ref.shape[1] // 6
        place = lax.broadcasted_iota(jnp.int32, (2 * pixels, 2 * cells), 0)
        lane = lax.broadcasted_iota(jnp.int32, (2 * pixels, 2 * cells), 1)
        lower, right = place >= pixels, lane >= cells
        pixel = jnp.where(lower, place - pixels, place) - pixels // 2
        cos, sin = phase(jnp.where(right, lane - cells, lane), pixel)
        value = jnp.where(lower == right, cos, sin)
        value = jnp.where(right & (lower == (sign < 0)), -value, value)
        high, low = split_terms(value)
        out_ref[...] = jnp.concatenate([high, low, high], axis=1)


def pack_kernel(flags_ref, cells_ref, _rows_ref, _cols_ref, _table_ref, packed_ref):
    turn = lax.axis_index(TURN)
    count, lanes = cells_ref.shape[1], packed_ref.shape[1]
    wide = jnp.concatenate([cells_ref[...]] * (lanes // count), axis=1)
    lane = lax.broadcasted_iota(jnp.int32, wide.shape, 1)
    wide = jnp.where((lane >= turn * count) & (lane < (turn + 1) * count), wide, 0)
    packed_ref[...] = jnp.zeros_like(packed_ref)
    packed_ref[0:2] = (wide // DIGIT).astype(jnp.float32)
    packed_ref[2:4] = (wide % DIGIT).astype(jnp.float32)
    packed_ref[4:5, : flags_ref.shape[1]] = flags_ref[...].astype(jnp.float32)


def gridding_weights(rows_ref, cols_ref, packed_ref, turn, stations):
    both = jnp.concatenate([rows_ref[0, 0], cols_ref[0, 0]], axis=0).astype(jnp.float32)
    weights = jnp.zeros((both.shape[0], stations), jnp.float32)
    for group in range(lax.axis_size(TURN)):
        weights = jnp.where(turn == group, both[:, group * stations : (group + 1) * stations], weights)
    return (weights * packed_ref[4:5, :stations]).astype(jnp.bfloat16)


def gridded_frames(volt_ref, taps_ref, weights, firsts):
    taps, two_fine, _ = taps_ref.shape
    stations = volt_ref.shape[2]
    core = lax.axis_index("core")
    spectra = jnp.zeros((len(firsts) * stations, two_fine), jnp.float32)
    for tap in range(taps):
        block = jnp.concatenate(
            [
                volt_ref[0, core, :, pl.ds(pl.multiple_of((first + tap) * two_fine, two_fine), two_fine)]
                for first in firsts
            ],
            axis=0,
        )
        spectra = spectra + jnp.dot(block, taps_ref[tap], preferred_element_type=jnp.float32)
    spectra = spectra.astype(jnp.bfloat16)
    beside = jnp.concatenate(
        [spectra[index * stations : (index + 1) * stations] for index in range(len(firsts))], axis=1
    )
    gridded = jnp.dot(weights, beside, preferred_element_type=jnp.float32)
    return [gridded[:, index * two_fine : (index + 1) * two_fine] for index in range(len(firsts))]


def own_kernel(volt_ref, taps_ref, rows_ref, cols_ref, packed_ref, out_ref):
    weights = gridding_weights(rows_ref, cols_ref, packed_ref, lax.axis_index(TURN), volt_ref.shape[2])
    rows = weights.shape[0]
    for frame, gridded in enumerate(gridded_frames(volt_ref, taps_ref, weights, range(out_ref.shape[0] // rows))):
        out_ref[frame * rows : (frame + 1) * rows] = gridded


def sum_kernel(step, each, volt_ref, taps_ref, rows_ref, cols_ref, own_ref, packed_ref, part_ref, *refs):
    out_ref = refs[-1]
    weights = gridding_weights(rows_ref, cols_ref, packed_ref, lax.axis_index(TURN) ^ 1, volt_ref.shape[2])
    rows = weights.shape[0]
    firsts = [(lax.axis_index("chip") ^ step) * each + frame for frame in range(each)]
    for index, gridded in enumerate(gridded_frames(volt_ref, taps_ref, weights, firsts)):
        held = part_ref[pl.ds(pl.multiple_of(firsts[index] * rows, rows), rows)]
        out_ref[index * rows : (index + 1) * rows] = (held + gridded).astype(jnp.bfloat16)
    digits = own_ref[...] + packed_ref[...]
    digits = jnp.concatenate([digits, jnp.zeros((PAD_ROWS - digits.shape[0], digits.shape[1]), jnp.float32)], axis=0)
    out_ref[each * rows :] = digits.astype(jnp.bfloat16)


def image_kernel(pairs_each, *refs):
    *got, row_dft_ref, col_dft_ref, out_ref = refs
    fine = got[0].shape[1] // 2
    sub = row_dft_ref.shape[1] // 6
    row_total = out_ref.shape[0]
    total = got[0][...].astype(jnp.float32)
    for source in got[1:]:
        total = total + source[...].astype(jnp.float32)
    digits = total[pairs_each * 2 * sub :]
    cell_u = (digits[0:1, :fine] * DIGIT + digits[2:3, :fine]).astype(jnp.int32)
    cell_v = (digits[1:2, :fine] * DIGIT + digits[3:4, :fine]).astype(jnp.int32)

    def transform(dft_ref, first, cos, sin):
        held = jnp.concatenate(
            [
                jnp.concatenate(
                    [
                        total[index * 2 * sub + first : index * 2 * sub + first + sub, :fine],
                        total[index * 2 * sub + first : index * 2 * sub + first + sub, fine:],
                    ],
                    axis=0,
                )
                for index in range(pairs_each)
            ],
            axis=1,
        )
        high, low = split_terms(held)
        plain = jnp.dot(
            dft_ref[...], jnp.concatenate([high, high, low], axis=0), preferred_element_type=jnp.float32
        )
        half = plain.shape[0] // 2
        real, imag = plain[:half], plain[half:]
        cos = jnp.concatenate([cos] * pairs_each, axis=1)
        sin = jnp.concatenate([sin] * pairs_each, axis=1)
        return real * cos - imag * sin, real * sin + imag * cos

    row = lax.broadcasted_iota(jnp.int32, (row_total, fine), 0)
    row_real, row_imag = transform(row_dft_ref, 0, *phase(cell_u, row - row_total // 2))
    col = lax.broadcasted_iota(jnp.int32, (MW, fine), 0)
    col_real, col_imag = transform(col_dft_ref, sub, *phase(cell_v, col - MW // 2))
    left = jnp.concatenate([row_real, -row_imag], axis=1).astype(jnp.bfloat16)
    right = jnp.concatenate([col_real, col_imag], axis=1).astype(jnp.bfloat16)
    out_ref[...] = lax.dot_general(right, left, (((1,), (1,)), ((), ())), preferred_element_type=jnp.float32).T


def final_kernel(scale_factor, in_ref, out_ref):
    out_ref[...] = jnp.sum(in_ref[...], axis=0) * scale_factor


def call(kernel, shape, args, flops=0):
    moved = sum(math.prod(leaf.shape) * leaf.dtype.itemsize for leaf in [*jax.tree.leaves(shape), *args])
    return pl.pallas_call(
        kernel,
        out_shape=shape,
        in_specs=[pl.BlockSpec(memory_space=pltpu.VMEM)] * len(args),
        out_specs=jax.tree.map(lambda _: pl.BlockSpec(memory_space=pltpu.VMEM), shape),
        compiler_params=pltpu.CompilerParams(vmem_limit_bytes=VMEM_BYTES),
        cost_estimate=pl.CostEstimate(flops=flops, bytes_accessed=moved, transcendentals=0),
    )(*args)


def local(voltages, station_flags, filter_taps, kernel_rows, kernel_cols, cell_index):
    station_rows, width = voltages.shape[2:]
    taps, two_fine, _ = filter_taps.shape
    sub_u, sub_v = kernel_rows.shape[2], kernel_cols.shape[2]
    chips = lax.axis_size("chip")
    row_total = ROWS_DEV * lax.axis_size(EVERYONE)
    channels = two_fine // 2 * lax.axis_size("role") * lax.axis_size("band")
    frames = width // two_fine - taps + 1
    scale_factor = 4.0 / math.sqrt(channels * sub_u * sub_v) / frames
    each = frames // chips
    sub_rows = sub_u + sub_v

    swap = [(core, 1 - core) for core in range(CORES)]
    other = lax.ppermute(voltages, "core", swap)
    tables = call(
        tables_kernel,
        (
            jax.ShapeDtypeStruct((2 * row_total, 6 * sub_u), jnp.bfloat16),
            jax.ShapeDtypeStruct((2 * MW, 6 * sub_v), jnp.bfloat16),
        ),
        (),
        flops=2 * voltages.size * two_fine * taps,
    )
    packed = call(
        pack_kernel,
        jax.ShapeDtypeStruct((8, two_fine), jnp.float32),
        (station_flags.reshape(1, -1), cell_index.reshape(2, -1), kernel_rows, kernel_cols, tables[0]),
    )
    other_packed = lax.ppermute(packed, "core", swap)
    flops = 2 * station_rows * taps * two_fine * two_fine
    part = call(
        own_kernel,
        jax.ShapeDtypeStruct((frames * sub_rows, two_fine), jnp.float32),
        (voltages, filter_taps, kernel_rows, kernel_cols, packed),
        flops=frames * flops,
    )

    after = ()
    got = []
    for step in [*range(1, chips), 0]:
        made = call(
            functools.partial(sum_kernel, step, each),
            jax.ShapeDtypeStruct((each * sub_rows + PAD_ROWS, two_fine), jnp.bfloat16),
            (other, filter_taps, kernel_rows, kernel_cols, packed, other_packed, part, *after),
            flops=each * flops,
        )
        after = (made,)
        if step:
            made = lax.ppermute(made, "chip", [(source, source ^ step) for source in range(chips)])
        got.append(made)
    image = call(
        functools.partial(image_kernel, each),
        jax.ShapeDtypeStruct((row_total, MW), jnp.float32),
        (*got, *tables),
    )
    rows = lax.all_to_all(image, EVERYONE, split_axis=0, concat_axis=0, tiled=True)
    return call(
        functools.partial(final_kernel, scale_factor),
        jax.ShapeDtypeStruct((ROWS_DEV, MW), jnp.float32),
        (rows.reshape(-1, ROWS_DEV, MW),),
    )


def solution(mesh):
    roles, bands, turns = (mesh.shape[name] for name in ("role", "band", "turn"))
    split = Mesh(mesh.devices.reshape(roles, bands, turns // CORES, CORES), EVERYONE)
    in_specs = (
        P(("role", "band"), None, TURN, None),
        P(TURN),
        P(),
        P(("role", "band"), None, None, None),
        P(("role", "band"), None, None, None),
        P(None, EVERYONE, None),
    )
    out_specs = P(EVERYONE, None)
    return jax.shard_map(local, mesh=split, in_specs=in_specs, out_specs=out_specs, check_vma=False)
```

```python
import functools
import math

import jax
import jax.numpy as jnp
from jax import lax
from jax.experimental import pallas as pl
from jax.experimental.pallas import tpu as pltpu
from jax.sharding import Mesh
from jax.sharding import PartitionSpec as P

NGRID = 4096
MW = 128
ROWS_DEV = 1
DIGIT = 64
CORES = 2
TURN = ("chip", "core")
EVERYONE = ("role", "band", *TURN)
VMEM_BYTES = 24 * 1024 * 1024


def split_terms(value):
    high = value.astype(jnp.bfloat16)
    return high, (value - high.astype(jnp.float32)).astype(jnp.bfloat16)


def phase(cell, pixel):
    quarter = NGRID // 4
    turned = (cell * pixel) & (NGRID - 1)
    quadrant = (turned + quarter // 2) // quarter
    angle = (turned - quadrant * quarter).astype(jnp.float32) * (2.0 * math.pi / NGRID)
    square = angle * angle
    sine = angle * (1 + square * (-1 / 6 + square * (1 / 120 + square * (-1 / 5040 + square * (1 / 362880)))))
    cosine = 1 + square * (-1 / 2 + square * (1 / 24 + square * (-1 / 720 + square * (1 / 40320))))
    odd = (quadrant & 1) == 1
    real = jnp.where(odd, sine, cosine)
    imag = jnp.where(odd, cosine, sine)
    return (
        jnp.where(((quadrant + 1) & 2) == 2, -real, real),
        jnp.where((quadrant & 2) == 2, -imag, imag),
    )


def tables_kernel(row_ref, col_ref):
    for out_ref, sign in ((row_ref, 1), (col_ref, -1)):
        pixels, cells = out_ref.shape[0] // 2, out_ref.shape[1] // 6
        place = lax.broadcasted_iota(jnp.int32, (2 * pixels, 2 * cells), 0)
        lane = lax.broadcasted_iota(jnp.int32, (2 * pixels, 2 * cells), 1)
        lower, right = place >= pixels, lane >= cells
        pixel = jnp.where(lower, place - pixels, place) - pixels // 2
        cos, sin = phase(jnp.where(right, lane - cells, lane), pixel)
        value = jnp.where(lower == right, cos, sin)
        value = jnp.where(right & (lower == (sign < 0)), -value, value)
        high, low = split_terms(value)
        out_ref[...] = jnp.concatenate([high, low, high], axis=1)


def pack_kernel(flags_ref, cells_ref, _rows_ref, _cols_ref, _table_ref, packed_ref):
    turn = lax.axis_index(TURN)
    count, lanes = cells_ref.shape[1], packed_ref.shape[1]
    wide = jnp.concatenate([cells_ref[...]] * (lanes // count), axis=1)
    lane = lax.broadcasted_iota(jnp.int32, wide.shape, 1)
    wide = jnp.where((lane >= turn * count) & (lane < (turn + 1) * count), wide, 0)
    packed_ref[...] = jnp.zeros_like(packed_ref)
    packed_ref[0:2] = (wide // DIGIT).astype(jnp.float32)
    packed_ref[2:4] = (wide % DIGIT).astype(jnp.float32)
    packed_ref[4:5, : flags_ref.shape[1]] = flags_ref[...].astype(jnp.float32)


def gridding_weights(rows_ref, cols_ref, packed_ref, turn, stations):
    both = jnp.concatenate([rows_ref[0, 0], cols_ref[0, 0]], axis=0).astype(jnp.float32)
    weights = jnp.zeros((both.shape[0], stations), jnp.float32)
    for group in range(lax.axis_size(TURN)):
        weights = jnp.where(turn == group, both[:, group * stations : (group + 1) * stations], weights)
    return (weights * packed_ref[4:5, :stations]).astype(jnp.bfloat16)


def gridded_frames(volt_ref, taps_ref, weights, firsts):
    taps, two_fine, _ = taps_ref.shape
    stations = volt_ref.shape[2]
    core = lax.axis_index("core")
    lhs = jnp.concatenate(
        [
            volt_ref[0, core, :, pl.ds(pl.multiple_of(first * two_fine, two_fine), taps * two_fine)]
            for first in firsts
        ],
        axis=0,
    )
    filt = taps_ref[...].reshape(taps * two_fine, two_fine)
    spectra = jnp.dot(lhs, filt, preferred_element_type=jnp.float32).astype(jnp.bfloat16)
    beside = jnp.concatenate(
        [spectra[index * stations : (index + 1) * stations] for index in range(len(firsts))], axis=1
    )
    gridded = jnp.dot(weights, beside, preferred_element_type=jnp.float32)
    return [gridded[:, index * two_fine : (index + 1) * two_fine] for index in range(len(firsts))]


def own_kernel(volt_ref, taps_ref, rows_ref, cols_ref, packed_ref, out_ref):
    weights = gridding_weights(rows_ref, cols_ref, packed_ref, lax.axis_index(TURN), volt_ref.shape[2])
    rows = weights.shape[0]
    for frame, gridded in enumerate(gridded_frames(volt_ref, taps_ref, weights, range(out_ref.shape[0] // rows))):
        out_ref[frame * rows : (frame + 1) * rows] = gridded


def sum_kernel(step, each, volt_ref, taps_ref, rows_ref, cols_ref, packed_ref, part_ref, *refs):
    out_ref = refs[-1]
    weights = gridding_weights(rows_ref, cols_ref, packed_ref, lax.axis_index(TURN) ^ 1, volt_ref.shape[2])
    rows = weights.shape[0]
    firsts = [(lax.axis_index("chip") ^ step) * each + frame for frame in range(each)]
    for index, gridded in enumerate(gridded_frames(volt_ref, taps_ref, weights, firsts)):
        held = part_ref[pl.ds(pl.multiple_of(firsts[index] * rows, rows), rows)]
        out_ref[index * rows : (index + 1) * rows] = (held + gridded).astype(jnp.bfloat16)


def add_kernel(left_ref, right_ref, _, out_ref):
    out_ref[...] = left_ref[...] + right_ref[...]


def phases_kernel(*refs):
    *tiles, _, row_cos, row_sin, col_cos, col_sin = refs
    digits = tiles[0][...]
    for tile in tiles[1:]:
        digits = digits + tile[...]
    for index, (cos_ref, sin_ref) in enumerate(((row_cos, row_sin), (col_cos, col_sin))):
        cell = (digits[index : index + 1] * DIGIT + digits[index + 2 : index + 3]).astype(jnp.int32)
        pixel = lax.broadcasted_iota(jnp.int32, cos_ref.shape, 0) - cos_ref.shape[0] // 2
        cos_ref[...], sin_ref[...] = phase(cell, pixel)


def image_kernel(pairs_each, *refs):
    *got, row_dft_ref, col_dft_ref, row_cos, row_sin, col_cos, col_sin, out_ref = refs
    fine = got[0].shape[1] // 2
    sub = row_dft_ref.shape[1] // 6
    total = got[0][...].astype(jnp.float32)
    for source in got[1:]:
        total = total + source[...].astype(jnp.float32)
    def transform(dft_ref, first, cos, sin):
        held = jnp.concatenate(
            [
                jnp.concatenate(
                    [
                        total[index * 2 * sub + first : index * 2 * sub + first + sub, :fine],
                        total[index * 2 * sub + first : index * 2 * sub + first + sub, fine:],
                    ],
                    axis=0,
                )
                for index in range(pairs_each)
            ],
            axis=1,
        )
        high, low = split_terms(held)
        plain = jnp.dot(
            dft_ref[...], jnp.concatenate([high, high, low], axis=0), preferred_element_type=jnp.float32
        )
        half = plain.shape[0] // 2
        real, imag = plain[:half], plain[half:]
        cos = jnp.concatenate([cos] * pairs_each, axis=1)
        sin = jnp.concatenate([sin] * pairs_each, axis=1)
        return real * cos - imag * sin, real * sin + imag * cos

    row_real, row_imag = transform(row_dft_ref, 0, row_cos[...], row_sin[...])
    col_real, col_imag = transform(col_dft_ref, sub, col_cos[...], col_sin[...])
    left = jnp.concatenate([row_real, -row_imag], axis=1).astype(jnp.bfloat16)
    right = jnp.concatenate([col_real, col_imag], axis=1).astype(jnp.bfloat16)
    out_ref[...] = lax.dot_general(left, right, (((1,), (1,)), ((), ())), preferred_element_type=jnp.float32)


def final_kernel(scale_factor, in_ref, out_ref):
    out_ref[...] = jnp.sum(in_ref[...], axis=0) * scale_factor


def call(kernel, shape, args, flops=0):
    moved = sum(math.prod(leaf.shape) * leaf.dtype.itemsize for leaf in [*jax.tree.leaves(shape), *args])
    return pl.pallas_call(
        kernel,
        out_shape=shape,
        in_specs=[pl.BlockSpec(memory_space=pltpu.VMEM)] * len(args),
        out_specs=jax.tree.map(lambda _: pl.BlockSpec(memory_space=pltpu.VMEM), shape),
        compiler_params=pltpu.CompilerParams(vmem_limit_bytes=VMEM_BYTES),
        cost_estimate=pl.CostEstimate(flops=flops, bytes_accessed=moved, transcendentals=0),
    )(*args)


def local(voltages, station_flags, filter_taps, kernel_rows, kernel_cols, cell_index):
    station_rows, width = voltages.shape[2:]
    taps, two_fine, _ = filter_taps.shape
    sub_u, sub_v = kernel_rows.shape[2], kernel_cols.shape[2]
    chips = lax.axis_size("chip")
    row_total = ROWS_DEV * lax.axis_size(EVERYONE)
    channels = two_fine // 2 * lax.axis_size("role") * lax.axis_size("band")
    frames = width // two_fine - taps + 1
    scale_factor = 4.0 / math.sqrt(channels * sub_u * sub_v) / frames
    each = frames // chips
    sub_rows = sub_u + sub_v

    swap = [(core, 1 - core) for core in range(CORES)]
    other = lax.ppermute(voltages, "core", swap)
    tables = call(
        tables_kernel,
        (
            jax.ShapeDtypeStruct((2 * row_total, 6 * sub_u), jnp.bfloat16),
            jax.ShapeDtypeStruct((2 * MW, 6 * sub_v), jnp.bfloat16),
        ),
        (),
        flops=2 * voltages.size * two_fine * taps,
    )
    packed = call(
        pack_kernel,
        jax.ShapeDtypeStruct((8, two_fine // 2), jnp.float32),
        (station_flags.reshape(1, -1), cell_index.reshape(2, -1), kernel_rows, kernel_cols, tables[0]),
    )
    other_packed = lax.ppermute(packed, "core", swap)
    flops = 2 * station_rows * taps * two_fine * two_fine
    part = call(
        own_kernel,
        jax.ShapeDtypeStruct((frames * sub_rows, two_fine), jnp.float32),
        (voltages, filter_taps, kernel_rows, kernel_cols, packed),
        flops=frames * flops,
    )

    def beside(value, step):
        return lax.ppermute(value, "chip", [(source, source ^ step) for source in range(chips)])

    def summed(step, after):
        return call(
            functools.partial(sum_kernel, step, each),
            jax.ShapeDtypeStruct((each * sub_rows, two_fine), jnp.bfloat16),
            (other, filter_taps, kernel_rows, kernel_cols, other_packed, part, *after),
            flops=each * flops,
        )

    after = ()
    got = []
    for step in range(1, chips):
        made = summed(step, after)
        after = (made,)
        got.append(beside(made, step))
    tile = call(add_kernel, packed, (packed, other_packed, *after))
    tiles = [tile] + [beside(tile, step) for step in range(1, chips)]
    made = summed(0, (tile,))
    got.append(made)
    by_row = jax.ShapeDtypeStruct((row_total, two_fine // 2), jnp.float32)
    by_col = jax.ShapeDtypeStruct((MW, two_fine // 2), jnp.float32)
    phases = call(phases_kernel, (by_row, by_row, by_col, by_col), (*tiles, made))
    image = call(
        functools.partial(image_kernel, each),
        jax.ShapeDtypeStruct((row_total, MW), jnp.float32),
        (*got, *tables, *phases),
    )
    rows = lax.all_to_all(image, EVERYONE, split_axis=0, concat_axis=0, tiled=True)
    return call(
        functools.partial(final_kernel, scale_factor),
        jax.ShapeDtypeStruct((ROWS_DEV, MW), jnp.float32),
        (rows.reshape(-1, ROWS_DEV, MW),),
    )


def solution(mesh):
    roles, bands, turns = (mesh.shape[name] for name in ("role", "band", "turn"))
    split = Mesh(mesh.devices.reshape(roles, bands, turns // CORES, CORES), EVERYONE)
    in_specs = (
        P(("role", "band"), None, TURN, None),
        P(TURN),
        P(),
        P(("role", "band"), None, None, None),
        P(("role", "band"), None, None, None),
        P(None, EVERYONE, None),
    )
    out_specs = P(EVERYONE, None)
    return jax.shard_map(local, mesh=split, in_specs=in_specs, out_specs=out_specs, check_vma=False)
```

```python
import functools
import math

import jax
import jax.numpy as jnp
from jax import lax
from jax.experimental import pallas as pl
from jax.experimental.pallas import tpu as pltpu
from jax.sharding import Mesh
from jax.sharding import PartitionSpec as P

NGRID = 4096
MW = 128
ROWS_DEV = 1
DIGIT = 64
PAD_ROWS = 16
CORES = 2
TURN = ("chip", "core")
EVERYONE = ("role", "band", *TURN)
VMEM_BYTES = 24 * 1024 * 1024


def split_terms(value):
    high = value.astype(jnp.bfloat16)
    return high, (value - high.astype(jnp.float32)).astype(jnp.bfloat16)


def phase(cell, pixel):
    quarter = NGRID // 4
    turned = (cell * pixel) & (NGRID - 1)
    quadrant = (turned + quarter // 2) // quarter
    angle = (turned - quadrant * quarter).astype(jnp.float32) * (2.0 * math.pi / NGRID)
    square = angle * angle
    sine = angle * (1 + square * (-1 / 6 + square * (1 / 120 + square * (-1 / 5040 + square * (1 / 362880)))))
    cosine = 1 + square * (-1 / 2 + square * (1 / 24 + square * (-1 / 720 + square * (1 / 40320))))
    odd = (quadrant & 1) == 1
    real = jnp.where(odd, sine, cosine)
    imag = jnp.where(odd, cosine, sine)
    return (
        jnp.where(((quadrant + 1) & 2) == 2, -real, real),
        jnp.where((quadrant & 2) == 2, -imag, imag),
    )


def tables_kernel(row_ref, col_ref):
    for out_ref, sign in ((row_ref, 1), (col_ref, -1)):
        pixels, cells = out_ref.shape[0] // 2, out_ref.shape[1] // 6
        place = lax.broadcasted_iota(jnp.int32, (2 * pixels, 2 * cells), 0)
        lane = lax.broadcasted_iota(jnp.int32, (2 * pixels, 2 * cells), 1)
        lower, right = place >= pixels, lane >= cells
        pixel = jnp.where(lower, place - pixels, place) - pixels // 2
        cos, sin = phase(jnp.where(right, lane - cells, lane), pixel)
        value = jnp.where(lower == right, cos, sin)
        value = jnp.where(right & (lower == (sign < 0)), -value, value)
        high, low = split_terms(value)
        out_ref[...] = jnp.concatenate([high, low, high], axis=1)


def pack_kernel(flags_ref, cells_ref, _rows_ref, _cols_ref, _table_ref, packed_ref):
    turn = lax.axis_index(TURN)
    count, lanes = cells_ref.shape[1], packed_ref.shape[1]
    wide = jnp.concatenate([cells_ref[...]] * (lanes // count), axis=1)
    lane = lax.broadcasted_iota(jnp.int32, wide.shape, 1)
    wide = jnp.where((lane >= turn * count) & (lane < (turn + 1) * count), wide, 0)
    packed_ref[...] = jnp.zeros_like(packed_ref)
    packed_ref[0:2] = (wide // DIGIT).astype(jnp.float32)
    packed_ref[2:4] = (wide % DIGIT).astype(jnp.float32)
    packed_ref[4:5, : flags_ref.shape[1]] = flags_ref[...].astype(jnp.float32)


def gridding_weights(rows_ref, cols_ref, packed_ref, turn, stations):
    both = jnp.concatenate([rows_ref[0, 0], cols_ref[0, 0]], axis=0).astype(jnp.float32)
    weights = jnp.zeros((both.shape[0], stations), jnp.float32)
    for group in range(lax.axis_size(TURN)):
        weights = jnp.where(turn == group, both[:, group * stations : (group + 1) * stations], weights)
    return (weights * packed_ref[4:5, :stations]).astype(jnp.bfloat16)


def gridded_frames(volt_ref, taps_ref, weights, firsts):
    taps, two_fine, _ = taps_ref.shape
    stations = volt_ref.shape[2]
    lhs = jnp.concatenate(
        [
            volt_ref[0, 0, :, pl.ds(pl.multiple_of(first * two_fine, two_fine), taps * two_fine)]
            for first in firsts
        ],
        axis=0,
    )
    filt = taps_ref[...].reshape(taps * two_fine, two_fine)
    spectra = jnp.dot(lhs, filt, preferred_element_type=jnp.float32).astype(jnp.bfloat16)
    beside = jnp.concatenate(
        [spectra[index * stations : (index + 1) * stations] for index in range(len(firsts))], axis=1
    )
    gridded = jnp.dot(weights, beside, preferred_element_type=jnp.float32)
    return [gridded[:, index * two_fine : (index + 1) * two_fine] for index in range(len(firsts))]


def own_kernel(first_ref, second_ref, taps_ref, rows_ref, cols_ref, packed_ref, out_ref):
    weights = gridding_weights(rows_ref, cols_ref, packed_ref, lax.axis_index(TURN), first_ref.shape[2])
    rows = weights.shape[0]

    def fill(volt_ref):
        for frame, gridded in enumerate(gridded_frames(volt_ref, taps_ref, weights, range(out_ref.shape[0] // rows))):
            out_ref[frame * rows : (frame + 1) * rows] = gridded

    for core, volt_ref in enumerate((first_ref, second_ref)):
        pl.when(lax.axis_index("core") == core)(functools.partial(fill, volt_ref))


def sum_kernel(step, each, first_ref, second_ref, taps_ref, rows_ref, cols_ref, own_ref, packed_ref, part_ref, *refs):
    out_ref = refs[-1]
    weights = gridding_weights(rows_ref, cols_ref, packed_ref, lax.axis_index(TURN) ^ 1, first_ref.shape[2])
    rows = weights.shape[0]
    firsts = [(lax.axis_index("chip") ^ step) * each + frame for frame in range(each)]

    def add(volt_ref):
        for index, gridded in enumerate(gridded_frames(volt_ref, taps_ref, weights, firsts)):
            held = part_ref[pl.ds(pl.multiple_of(firsts[index] * rows, rows), rows)]
            out_ref[index * rows : (index + 1) * rows] = (held + gridded).astype(jnp.bfloat16)

    for core, volt_ref in enumerate((first_ref, second_ref)):
        pl.when(lax.axis_index("core") == core)(functools.partial(add, volt_ref))
    digits = own_ref[...] + packed_ref[...]
    digits = jnp.concatenate([digits, jnp.zeros((PAD_ROWS - digits.shape[0], digits.shape[1]), jnp.float32)], axis=0)
    out_ref[each * rows :] = digits.astype(jnp.bfloat16)


def image_kernel(pairs_each, *refs):
    *got, row_dft_ref, col_dft_ref, out_ref = refs
    fine = got[0].shape[1] // 2
    sub = row_dft_ref.shape[1] // 6
    row_total = out_ref.shape[0]
    total = got[0][...].astype(jnp.float32)
    for source in got[1:]:
        total = total + source[...].astype(jnp.float32)
    digits = total[pairs_each * 2 * sub :]
    cell_u = (digits[0:1, :fine] * DIGIT + digits[2:3, :fine]).astype(jnp.int32)
    cell_v = (digits[1:2, :fine] * DIGIT + digits[3:4, :fine]).astype(jnp.int32)

    def transform(dft_ref, first, cos, sin):
        held = jnp.concatenate(
            [
                jnp.concatenate(
                    [
                        total[index * 2 * sub + first : index * 2 * sub + first + sub, :fine],
                        total[index * 2 * sub + first : index * 2 * sub + first + sub, fine:],
                    ],
                    axis=0,
                )
                for index in range(pairs_each)
            ],
            axis=1,
        )
        high, low = split_terms(held)
        plain = jnp.dot(
            dft_ref[...], jnp.concatenate([high, high, low], axis=0), preferred_element_type=jnp.float32
        )
        half = plain.shape[0] // 2
        real, imag = plain[:half], plain[half:]
        cos = jnp.concatenate([cos] * pairs_each, axis=1)
        sin = jnp.concatenate([sin] * pairs_each, axis=1)
        return real * cos - imag * sin, real * sin + imag * cos

    row = lax.broadcasted_iota(jnp.int32, (row_total, fine), 0)
    row_real, row_imag = transform(row_dft_ref, 0, *phase(cell_u, row - row_total // 2))
    col = lax.broadcasted_iota(jnp.int32, (MW, fine), 0)
    col_real, col_imag = transform(col_dft_ref, sub, *phase(cell_v, col - MW // 2))
    left = jnp.concatenate([row_real, -row_imag], axis=1).astype(jnp.bfloat16)
    right = jnp.concatenate([col_real, col_imag], axis=1).astype(jnp.bfloat16)
    out_ref[...] = lax.dot_general(left, right, (((1,), (1,)), ((), ())), preferred_element_type=jnp.float32)


def final_kernel(scale_factor, in_ref, out_ref):
    out_ref[...] = jnp.sum(in_ref[...], axis=0) * scale_factor


def call(kernel, shape, args, flops=0):
    moved = sum(math.prod(leaf.shape) * leaf.dtype.itemsize for leaf in [*jax.tree.leaves(shape), *args])
    return pl.pallas_call(
        kernel,
        out_shape=shape,
        in_specs=[pl.BlockSpec(memory_space=pltpu.VMEM)] * len(args),
        out_specs=jax.tree.map(lambda _: pl.BlockSpec(memory_space=pltpu.VMEM), shape),
        compiler_params=pltpu.CompilerParams(vmem_limit_bytes=VMEM_BYTES),
        cost_estimate=pl.CostEstimate(flops=flops, bytes_accessed=moved, transcendentals=0),
    )(*args)


def local(voltages, station_flags, filter_taps, kernel_rows, kernel_cols, cell_index):
    station_rows, width = voltages.shape[2:]
    taps, two_fine, _ = filter_taps.shape
    sub_u, sub_v = kernel_rows.shape[2], kernel_cols.shape[2]
    chips = lax.axis_size("chip")
    row_total = ROWS_DEV * lax.axis_size(EVERYONE)
    channels = two_fine // 2 * lax.axis_size("role") * lax.axis_size("band")
    frames = width // two_fine - taps + 1
    scale_factor = 4.0 / math.sqrt(channels * sub_u * sub_v) / frames
    each = frames // chips
    sub_rows = sub_u + sub_v

    swap = [(core, 1 - core) for core in range(CORES)]
    own = [voltages[:, core : core + 1] for core in range(CORES)]
    other = [lax.ppermute(own[core], "core", [(1 - core, core)]) for core in range(CORES)]
    tables = call(
        tables_kernel,
        (
            jax.ShapeDtypeStruct((2 * row_total, 6 * sub_u), jnp.bfloat16),
            jax.ShapeDtypeStruct((2 * MW, 6 * sub_v), jnp.bfloat16),
        ),
        (),
        flops=2 * voltages.size * two_fine * taps,
    )
    packed = call(
        pack_kernel,
        jax.ShapeDtypeStruct((8, two_fine), jnp.float32),
        (station_flags.reshape(1, -1), cell_index.reshape(2, -1), kernel_rows, kernel_cols, tables[0]),
    )
    other_packed = lax.ppermute(packed, "core", swap)
    flops = 2 * station_rows * taps * two_fine * two_fine
    part = call(
        own_kernel,
        jax.ShapeDtypeStruct((frames * sub_rows, two_fine), jnp.float32),
        (*own, filter_taps, kernel_rows, kernel_cols, packed),
        flops=frames * flops,
    )

    after = ()
    got = []
    for step in [*range(1, chips), 0]:
        made = call(
            functools.partial(sum_kernel, step, each),
            jax.ShapeDtypeStruct((each * sub_rows + PAD_ROWS, two_fine), jnp.bfloat16),
            (*other, filter_taps, kernel_rows, kernel_cols, packed, other_packed, part, *after),
            flops=each * flops,
        )
        after = (made,)
        if step:
            made = lax.ppermute(made, "chip", [(source, source ^ step) for source in range(chips)])
        got.append(made)
    image = call(
        functools.partial(image_kernel, each),
        jax.ShapeDtypeStruct((row_total, MW), jnp.float32),
        (*got, *tables),
    )
    rows = lax.all_to_all(image, EVERYONE, split_axis=0, concat_axis=0, tiled=True)
    return call(
        functools.partial(final_kernel, scale_factor),
        jax.ShapeDtypeStruct((ROWS_DEV, MW), jnp.float32),
        (rows.reshape(-1, ROWS_DEV, MW),),
    )


def solution(mesh):
    roles, bands, turns = (mesh.shape[name] for name in ("role", "band", "turn"))
    split = Mesh(mesh.devices.reshape(roles, bands, turns // CORES, CORES), EVERYONE)
    in_specs = (
        P(("role", "band"), None, TURN, None),
        P(TURN),
        P(),
        P(("role", "band"), None, None, None),
        P(("role", "band"), None, None, None),
        P(None, EVERYONE, None),
    )
    out_specs = P(EVERYONE, None)
    return jax.shard_map(local, mesh=split, in_specs=in_specs, out_specs=out_specs, check_vma=False)
```

```python
import functools
import math

import jax
import jax.numpy as jnp
from jax import lax
from jax.experimental import pallas as pl
from jax.experimental.pallas import tpu as pltpu
from jax.sharding import Mesh
from jax.sharding import PartitionSpec as P

NGRID = 4096
MW = 128
ROWS_DEV = 1
DIGIT = 64
PAD_ROWS = 16
CORES = 2
TURN = ("chip", "core")
EVERYONE = ("role", "band", *TURN)
VMEM_BYTES = 24 * 1024 * 1024


def split_terms(value):
    high = value.astype(jnp.bfloat16)
    return high, (value - high.astype(jnp.float32)).astype(jnp.bfloat16)


def phase(cell, pixel):
    quarter = NGRID // 4
    turned = (cell * pixel) & (NGRID - 1)
    quadrant = (turned + quarter // 2) // quarter
    angle = (turned - quadrant * quarter).astype(jnp.float32) * (2.0 * math.pi / NGRID)
    square = angle * angle
    sine = angle * (1 + square * (-1 / 6 + square * (1 / 120 + square * (-1 / 5040 + square * (1 / 362880)))))
    cosine = 1 + square * (-1 / 2 + square * (1 / 24 + square * (-1 / 720 + square * (1 / 40320))))
    odd = (quadrant & 1) == 1
    real = jnp.where(odd, sine, cosine)
    imag = jnp.where(odd, cosine, sine)
    return (
        jnp.where(((quadrant + 1) & 2) == 2, -real, real),
        jnp.where((quadrant & 2) == 2, -imag, imag),
    )


def tables_kernel(row_ref, col_ref):
    for out_ref, sign in ((row_ref, 1), (col_ref, -1)):
        pixels, cells = out_ref.shape[0] // 2, out_ref.shape[1] // 6
        place = lax.broadcasted_iota(jnp.int32, (2 * pixels, 2 * cells), 0)
        lane = lax.broadcasted_iota(jnp.int32, (2 * pixels, 2 * cells), 1)
        lower, right = place >= pixels, lane >= cells
        pixel = jnp.where(lower, place - pixels, place) - pixels // 2
        cos, sin = phase(jnp.where(right, lane - cells, lane), pixel)
        value = jnp.where(lower == right, cos, sin)
        value = jnp.where(right & (lower == (sign < 0)), -value, value)
        high, low = split_terms(value)
        out_ref[...] = jnp.concatenate([high, low, high], axis=1)


def pack_kernel(flags_ref, cells_ref, _rows_ref, _cols_ref, _table_ref, packed_ref):
    turn = lax.axis_index(TURN)
    count, lanes = cells_ref.shape[1], packed_ref.shape[1]
    wide = jnp.concatenate([cells_ref[...]] * (lanes // count), axis=1)
    lane = lax.broadcasted_iota(jnp.int32, wide.shape, 1)
    wide = jnp.where((lane >= turn * count) & (lane < (turn + 1) * count), wide, 0)
    packed_ref[...] = jnp.zeros_like(packed_ref)
    packed_ref[0:2] = (wide // DIGIT).astype(jnp.float32)
    packed_ref[2:4] = (wide % DIGIT).astype(jnp.float32)
    packed_ref[4:5, : flags_ref.shape[1]] = flags_ref[...].astype(jnp.float32)


def gridding_weights(rows_ref, cols_ref, packed_ref, turn, stations):
    both = jnp.concatenate([rows_ref[0, 0], cols_ref[0, 0]], axis=0).astype(jnp.float32)
    weights = jnp.zeros((both.shape[0], stations), jnp.float32)
    for group in range(lax.axis_size(TURN)):
        weights = jnp.where(turn == group, both[:, group * stations : (group + 1) * stations], weights)
    return (weights * packed_ref[4:5, :stations]).astype(jnp.bfloat16)


def gridded_frames(volt_ref, taps_ref, weights, firsts):
    taps, two_fine, _ = taps_ref.shape
    stations = volt_ref.shape[2]
    core = lax.axis_index("core")
    lhs = jnp.concatenate(
        [
            volt_ref[0, core, :, pl.ds(pl.multiple_of(first * two_fine, two_fine), taps * two_fine)]
            for first in firsts
        ],
        axis=0,
    )
    filt = taps_ref[...].reshape(taps * two_fine, two_fine)
    spectra = jnp.dot(lhs, filt, preferred_element_type=jnp.float32).astype(jnp.bfloat16)
    beside = jnp.concatenate(
        [spectra[index * stations : (index + 1) * stations] for index in range(len(firsts))], axis=1
    )
    gridded = jnp.dot(weights, beside, preferred_element_type=jnp.float32)
    return [gridded[:, index * two_fine : (index + 1) * two_fine] for index in range(len(firsts))]


def own_kernel(volt_ref, taps_ref, rows_ref, cols_ref, packed_ref, out_ref):
    weights = gridding_weights(rows_ref, cols_ref, packed_ref, lax.axis_index(TURN), volt_ref.shape[2])
    rows = weights.shape[0]
    for frame, gridded in enumerate(gridded_frames(volt_ref, taps_ref, weights, range(out_ref.shape[0] // rows))):
        out_ref[frame * rows : (frame + 1) * rows] = gridded


def other_added(step, each, volt_ref, taps_ref, rows_ref, cols_ref, packed_ref, part_ref):
    weights = gridding_weights(rows_ref, cols_ref, packed_ref, lax.axis_index(TURN) ^ 1, volt_ref.shape[2])
    rows = weights.shape[0]
    firsts = [(lax.axis_index("chip") ^ step) * each + frame for frame in range(each)]
    return [
        part_ref[pl.ds(pl.multiple_of(first * rows, rows), rows)] + gridded
        for first, gridded in zip(firsts, gridded_frames(volt_ref, taps_ref, weights, firsts))
    ]


def far_kernel(step, each, own_ref, *refs):
    out_ref = refs[-1]
    made = other_added(step, each, *refs[:6])
    rows = made[0].shape[0]
    for index, frame in enumerate(made):
        out_ref[index * rows : (index + 1) * rows] = frame.astype(jnp.bfloat16)
    digits = own_ref[...] + refs[4][...]
    digits = jnp.concatenate([digits, jnp.zeros((PAD_ROWS - digits.shape[0], digits.shape[1]), jnp.float32)], axis=0)
    out_ref[each * rows :] = digits.astype(jnp.bfloat16)


def cells_side(frames, first, sub):
    fine = frames[0].shape[1] // 2
    return jnp.concatenate(
        [
            jnp.concatenate([frame[first : first + sub, :fine], frame[first : first + sub, fine:]], axis=0)
            for frame in frames
        ],
        axis=1,
    )


def near_kernel(each, *refs):
    row_dft_ref, col_dft_ref, _, row_ref, col_ref = refs[6:]
    made = other_added(0, each, *refs[:6])
    sub = row_dft_ref.shape[1] // 6
    for dft_ref, out_ref, first in ((row_dft_ref, row_ref, 0), (col_dft_ref, col_ref, sub)):
        high, low = split_terms(cells_side(made, first, sub))
        out_ref[...] = jnp.dot(
            dft_ref[...], jnp.concatenate([high, high, low], axis=0), preferred_element_type=jnp.float32
        )


def image_kernel(each, own_ref, packed_ref, row_ref, col_ref, row_dft_ref, col_dft_ref, *refs):
    *got, out_ref = refs
    fine = got[0].shape[1] // 2
    sub = row_dft_ref.shape[1] // 6
    digits = own_ref[...] + packed_ref[...]
    for source in got:
        digits = digits + source[each * 2 * sub :].astype(jnp.float32)[: digits.shape[0]]
    cell_u = (digits[0:1, :fine] * DIGIT + digits[2:3, :fine]).astype(jnp.int32)
    cell_v = (digits[1:2, :fine] * DIGIT + digits[3:4, :fine]).astype(jnp.int32)

    def side(plain_ref, dft_ref, first, cell):
        plain = plain_ref[...]
        half = plain.shape[0] // 2
        for source in got:
            frames = [source[index * 2 * sub : (index + 1) * 2 * sub] for index in range(each)]
            held = cells_side(frames, first, sub)
            plain = plain + jnp.dot(
                dft_ref[:, : 4 * sub], jnp.concatenate([held, held], axis=0), preferred_element_type=jnp.float32
            )
        cos, sin = phase(cell, lax.broadcasted_iota(jnp.int32, (half, fine), 0) - half // 2)
        cos = jnp.concatenate([cos] * each, axis=1)
        sin = jnp.concatenate([sin] * each, axis=1)
        real, imag = plain[:half], plain[half:]
        return real * cos - imag * sin, real * sin + imag * cos

    row_real, row_imag = side(row_ref, row_dft_ref, 0, cell_u)
    col_real, col_imag = side(col_ref, col_dft_ref, sub, cell_v)
    left = jnp.concatenate([row_real, -row_imag], axis=1).astype(jnp.bfloat16)
    right = jnp.concatenate([col_real, col_imag], axis=1).astype(jnp.bfloat16)
    out_ref[...] = lax.dot_general(left, right, (((1,), (1,)), ((), ())), preferred_element_type=jnp.float32)


def final_kernel(scale_factor, in_ref, out_ref):
    out_ref[...] = jnp.sum(in_ref[...], axis=0) * scale_factor


def call(kernel, shape, args, flops=0):
    moved = sum(math.prod(leaf.shape) * leaf.dtype.itemsize for leaf in [*jax.tree.leaves(shape), *args])
    return pl.pallas_call(
        kernel,
        out_shape=shape,
        in_specs=[pl.BlockSpec(memory_space=pltpu.VMEM)] * len(args),
        out_specs=jax.tree.map(lambda _: pl.BlockSpec(memory_space=pltpu.VMEM), shape),
        compiler_params=pltpu.CompilerParams(vmem_limit_bytes=VMEM_BYTES),
        cost_estimate=pl.CostEstimate(flops=flops, bytes_accessed=moved, transcendentals=0),
    )(*args)


def local(voltages, station_flags, filter_taps, kernel_rows, kernel_cols, cell_index):
    station_rows, width = voltages.shape[2:]
    taps, two_fine, _ = filter_taps.shape
    sub_u, sub_v = kernel_rows.shape[2], kernel_cols.shape[2]
    chips = lax.axis_size("chip")
    row_total = ROWS_DEV * lax.axis_size(EVERYONE)
    channels = two_fine // 2 * lax.axis_size("role") * lax.axis_size("band")
    frames = width // two_fine - taps + 1
    scale_factor = 4.0 / math.sqrt(channels * sub_u * sub_v) / frames
    each = frames // chips
    sub_rows = sub_u + sub_v

    swap = [(core, 1 - core) for core in range(CORES)]
    other = lax.ppermute(voltages, "core", swap)
    tables = call(
        tables_kernel,
        (
            jax.ShapeDtypeStruct((2 * row_total, 6 * sub_u), jnp.bfloat16),
            jax.ShapeDtypeStruct((2 * MW, 6 * sub_v), jnp.bfloat16),
        ),
        (),
        flops=2 * voltages.size * two_fine * taps,
    )
    packed = call(
        pack_kernel,
        jax.ShapeDtypeStruct((8, two_fine), jnp.float32),
        (station_flags.reshape(1, -1), cell_index.reshape(2, -1), kernel_rows, kernel_cols, tables[0]),
    )
    other_packed = lax.ppermute(packed, "core", swap)
    flops = 2 * station_rows * taps * two_fine * two_fine
    part = call(
        own_kernel,
        jax.ShapeDtypeStruct((frames * sub_rows, two_fine), jnp.float32),
        (voltages, filter_taps, kernel_rows, kernel_cols, packed),
        flops=frames * flops,
    )

    summed = (other, filter_taps, kernel_rows, kernel_cols, other_packed, part)
    after = ()
    got = []
    for step in range(1, chips):
        made = call(
            functools.partial(far_kernel, step, each),
            jax.ShapeDtypeStruct((each * sub_rows + PAD_ROWS, two_fine), jnp.bfloat16),
            (packed, *summed, *after),
            flops=each * flops,
        )
        after = (made,)
        got.append(lax.ppermute(made, "chip", [(source, source ^ step) for source in range(chips)]))
    lanes = each * two_fine // 2
    sides = call(
        functools.partial(near_kernel, each),
        (
            jax.ShapeDtypeStruct((2 * row_total, lanes), jnp.float32),
            jax.ShapeDtypeStruct((2 * MW, lanes), jnp.float32),
        ),
        (*summed, *tables, *after),
        flops=each * flops,
    )
    image = call(
        functools.partial(image_kernel, each),
        jax.ShapeDtypeStruct((row_total, MW), jnp.float32),
        (packed, other_packed, *sides, *tables, *got),
    )
    rows = lax.all_to_all(image, EVERYONE, split_axis=0, concat_axis=0, tiled=True)
    return call(
        functools.partial(final_kernel, scale_factor),
        jax.ShapeDtypeStruct((ROWS_DEV, MW), jnp.float32),
        (rows.reshape(-1, ROWS_DEV, MW),),
    )


def solution(mesh):
    roles, bands, turns = (mesh.shape[name] for name in ("role", "band", "turn"))
    split = Mesh(mesh.devices.reshape(roles, bands, turns // CORES, CORES), EVERYONE)
    in_specs = (
        P(("role", "band"), None, TURN, None),
        P(TURN),
        P(),
        P(("role", "band"), None, None, None),
        P(("role", "band"), None, None, None),
        P(None, EVERYONE, None),
    )
    out_specs = P(EVERYONE, None)
    return jax.shard_map(local, mesh=split, in_specs=in_specs, out_specs=out_specs, check_vma=False)
```

```python
import functools
import math

import jax
import jax.numpy as jnp
from jax import lax
from jax.experimental import pallas as pl
from jax.experimental.pallas import tpu as pltpu
from jax.sharding import Mesh
from jax.sharding import PartitionSpec as P

NGRID = 4096
MW = 128
ROWS_DEV = 1
DIGIT = 64
PAD_ROWS = 16
CORES = 2
TURN = ("chip", "core")
EVERYONE = ("role", "band", *TURN)
VMEM_BYTES = 24 * 1024 * 1024


def split_terms(value):
    high = value.astype(jnp.bfloat16)
    return high, (value - high.astype(jnp.float32)).astype(jnp.bfloat16)


def phase(cell, pixel):
    quarter = NGRID // 4
    turned = (cell * pixel) & (NGRID - 1)
    quadrant = (turned + quarter // 2) // quarter
    angle = (turned - quadrant * quarter).astype(jnp.float32) * (2.0 * math.pi / NGRID)
    square = angle * angle
    sine = angle * (1 + square * (-1 / 6 + square * (1 / 120 + square * (-1 / 5040 + square * (1 / 362880)))))
    cosine = 1 + square * (-1 / 2 + square * (1 / 24 + square * (-1 / 720 + square * (1 / 40320))))
    odd = (quadrant & 1) == 1
    real = jnp.where(odd, sine, cosine)
    imag = jnp.where(odd, cosine, sine)
    return (
        jnp.where(((quadrant + 1) & 2) == 2, -real, real),
        jnp.where((quadrant & 2) == 2, -imag, imag),
    )


def tables_kernel(row_ref, col_ref):
    for out_ref, sign in ((row_ref, 1), (col_ref, -1)):
        pixels, cells = out_ref.shape[0] // 2, out_ref.shape[1] // 6
        place = lax.broadcasted_iota(jnp.int32, (2 * pixels, 2 * cells), 0)
        lane = lax.broadcasted_iota(jnp.int32, (2 * pixels, 2 * cells), 1)
        lower, right = place >= pixels, lane >= cells
        pixel = jnp.where(lower, place - pixels, place) - pixels // 2
        cos, sin = phase(jnp.where(right, lane - cells, lane), pixel)
        value = jnp.where(lower == right, cos, sin)
        value = jnp.where(right & (lower == (sign < 0)), -value, value)
        high, low = split_terms(value)
        out_ref[...] = jnp.concatenate([high, low, high], axis=1)


def pack_kernel(flags_ref, cells_ref, _rows_ref, _cols_ref, _table_ref, packed_ref):
    turn = lax.axis_index(TURN)
    count, lanes = cells_ref.shape[1], packed_ref.shape[1]
    wide = jnp.concatenate([cells_ref[...]] * (lanes // count), axis=1)
    lane = lax.broadcasted_iota(jnp.int32, wide.shape, 1)
    wide = jnp.where((lane >= turn * count) & (lane < (turn + 1) * count), wide, 0)
    packed_ref[...] = jnp.zeros_like(packed_ref)
    packed_ref[0:2] = (wide // DIGIT).astype(jnp.float32)
    packed_ref[2:4] = (wide % DIGIT).astype(jnp.float32)
    packed_ref[4:5, : flags_ref.shape[1]] = flags_ref[...].astype(jnp.float32)


def gridding_weights(rows_ref, cols_ref, packed_ref, turn, stations):
    both = jnp.concatenate([rows_ref[0, 0], cols_ref[0, 0]], axis=0).astype(jnp.float32)
    weights = jnp.zeros((both.shape[0], stations), jnp.float32)
    for group in range(lax.axis_size(TURN)):
        weights = jnp.where(turn == group, both[:, group * stations : (group + 1) * stations], weights)
    return (weights * packed_ref[4:5, :stations]).astype(jnp.bfloat16)


def gridded_frames(volt_ref, taps_ref, weights, firsts):
    taps, two_fine, _ = taps_ref.shape
    stations = volt_ref.shape[2]
    core = lax.axis_index("core")
    lhs = jnp.concatenate(
        [
            volt_ref[0, core, :, pl.ds(pl.multiple_of(first * two_fine, two_fine), taps * two_fine)]
            for first in firsts
        ],
        axis=0,
    )
    filt = taps_ref[...].reshape(taps * two_fine, two_fine)
    spectra = jnp.dot(lhs, filt, preferred_element_type=jnp.float32).astype(jnp.bfloat16)
    beside = jnp.concatenate(
        [spectra[index * stations : (index + 1) * stations] for index in range(len(firsts))], axis=1
    )
    gridded = jnp.dot(weights, beside, preferred_element_type=jnp.float32)
    return [gridded[:, index * two_fine : (index + 1) * two_fine] for index in range(len(firsts))]


def own_kernel(volt_ref, taps_ref, rows_ref, cols_ref, packed_ref, out_ref):
    weights = gridding_weights(rows_ref, cols_ref, packed_ref, lax.axis_index(TURN), volt_ref.shape[2])
    rows = weights.shape[0]
    for frame, gridded in enumerate(gridded_frames(volt_ref, taps_ref, weights, range(out_ref.shape[0] // rows))):
        out_ref[frame * rows : (frame + 1) * rows] = gridded


def other_added(step, each, volt_ref, taps_ref, rows_ref, cols_ref, packed_ref, part_ref):
    weights = gridding_weights(rows_ref, cols_ref, packed_ref, lax.axis_index(TURN) ^ 1, volt_ref.shape[2])
    rows = weights.shape[0]
    firsts = [(lax.axis_index("chip") ^ step) * each + frame for frame in range(each)]
    return [
        part_ref[pl.ds(pl.multiple_of(first * rows, rows), rows)] + gridded
        for first, gridded in zip(firsts, gridded_frames(volt_ref, taps_ref, weights, firsts))
    ]


def far_kernel(step, each, own_ref, *refs):
    out_ref = refs[-1]
    made = other_added(step, each, *refs[:6])
    rows = made[0].shape[0]
    for index, frame in enumerate(made):
        out_ref[index * rows : (index + 1) * rows] = frame.astype(jnp.bfloat16)
    digits = own_ref[...] + refs[4][...]
    digits = jnp.concatenate([digits, jnp.zeros((PAD_ROWS - digits.shape[0], digits.shape[1]), jnp.float32)], axis=0)
    out_ref[each * rows :] = digits.astype(jnp.bfloat16)


def cells_side(frames, first, sub):
    fine = frames[0].shape[1] // 2
    return jnp.concatenate(
        [
            jnp.concatenate([frame[first : first + sub, :fine], frame[first : first + sub, fine:]], axis=0)
            for frame in frames
        ],
        axis=1,
    )


def near_kernel(each, *refs):
    row_dft_ref, col_dft_ref, _, row_ref, col_ref = refs[6:]
    made = other_added(0, each, *refs[:6])
    sub = row_dft_ref.shape[1] // 6
    for dft_ref, out_ref, first in ((row_dft_ref, row_ref, 0), (col_dft_ref, col_ref, sub)):
        high, low = split_terms(cells_side(made, first, sub))
        out_ref[...] = jnp.dot(
            dft_ref[...], jnp.concatenate([high, high, low], axis=0), preferred_element_type=jnp.float32
        )


def image_kernel(each, own_ref, packed_ref, row_ref, col_ref, row_dft_ref, col_dft_ref, *refs):
    *got, out_ref = refs
    fine = got[0].shape[1] // 2
    sub = row_dft_ref.shape[1] // 6
    digits = own_ref[...] + packed_ref[...]
    for source in got:
        digits = digits + source[each * 2 * sub :].astype(jnp.float32)[: digits.shape[0]]
    cell_u = (digits[0:1, :fine] * DIGIT + digits[2:3, :fine]).astype(jnp.int32)
    cell_v = (digits[1:2, :fine] * DIGIT + digits[3:4, :fine]).astype(jnp.int32)

    def side(plain_ref, dft_ref, first, cell):
        plain = plain_ref[...]
        half = plain.shape[0] // 2
        for source in got:
            frames = [source[index * 2 * sub : (index + 1) * 2 * sub] for index in range(each)]
            held = cells_side(frames, first, sub)
            plain = plain + jnp.dot(
                dft_ref[:, : 4 * sub], jnp.concatenate([held, held], axis=0), preferred_element_type=jnp.float32
            )
        cos, sin = phase(cell, lax.broadcasted_iota(jnp.int32, (half, fine), 0) - half // 2)
        turned = []
        for index in range(each):
            real, imag = (plain[part : part + half, index * fine : (index + 1) * fine] for part in (0, half))
            turned.append((real * cos - imag * sin, real * sin + imag * cos))
        return turned

    image = jnp.zeros(out_ref.shape, jnp.float32)
    for row, col in zip(side(row_ref, row_dft_ref, 0, cell_u), side(col_ref, col_dft_ref, sub, cell_v)):
        left = jnp.concatenate([row[0], -row[1]], axis=1).astype(jnp.bfloat16)
        right = jnp.concatenate(col, axis=1).astype(jnp.bfloat16)
        image = image + lax.dot_general(left, right, (((1,), (1,)), ((), ())), preferred_element_type=jnp.float32)
    out_ref[...] = image


def final_kernel(scale_factor, in_ref, out_ref):
    out_ref[...] = jnp.sum(in_ref[...], axis=0) * scale_factor


def call(kernel, shape, args, flops=0):
    moved = sum(math.prod(leaf.shape) * leaf.dtype.itemsize for leaf in [*jax.tree.leaves(shape), *args])
    return pl.pallas_call(
        kernel,
        out_shape=shape,
        in_specs=[pl.BlockSpec(memory_space=pltpu.VMEM)] * len(args),
        out_specs=jax.tree.map(lambda _: pl.BlockSpec(memory_space=pltpu.VMEM), shape),
        compiler_params=pltpu.CompilerParams(vmem_limit_bytes=VMEM_BYTES),
        cost_estimate=pl.CostEstimate(flops=flops, bytes_accessed=moved, transcendentals=0),
    )(*args)


def local(voltages, station_flags, filter_taps, kernel_rows, kernel_cols, cell_index):
    station_rows, width = voltages.shape[2:]
    taps, two_fine, _ = filter_taps.shape
    sub_u, sub_v = kernel_rows.shape[2], kernel_cols.shape[2]
    chips = lax.axis_size("chip")
    row_total = ROWS_DEV * lax.axis_size(EVERYONE)
    channels = two_fine // 2 * lax.axis_size("role") * lax.axis_size("band")
    frames = width // two_fine - taps + 1
    scale_factor = 4.0 / math.sqrt(channels * sub_u * sub_v) / frames
    each = frames // chips
    sub_rows = sub_u + sub_v

    swap = [(core, 1 - core) for core in range(CORES)]
    other = lax.ppermute(voltages, "core", swap)
    tables = call(
        tables_kernel,
        (
            jax.ShapeDtypeStruct((2 * row_total, 6 * sub_u), jnp.bfloat16),
            jax.ShapeDtypeStruct((2 * MW, 6 * sub_v), jnp.bfloat16),
        ),
        (),
        flops=2 * voltages.size * two_fine * taps,
    )
    packed = call(
        pack_kernel,
        jax.ShapeDtypeStruct((8, two_fine), jnp.float32),
        (station_flags.reshape(1, -1), cell_index.reshape(2, -1), kernel_rows, kernel_cols, tables[0]),
    )
    other_packed = lax.ppermute(packed, "core", swap)
    flops = 2 * station_rows * taps * two_fine * two_fine
    part = call(
        own_kernel,
        jax.ShapeDtypeStruct((frames * sub_rows, two_fine), jnp.float32),
        (voltages, filter_taps, kernel_rows, kernel_cols, packed),
        flops=frames * flops,
    )

    summed = (other, filter_taps, kernel_rows, kernel_cols, other_packed, part)
    after = ()
    got = []
    for step in range(1, chips):
        made = call(
            functools.partial(far_kernel, step, each),
            jax.ShapeDtypeStruct((each * sub_rows + PAD_ROWS, two_fine), jnp.bfloat16),
            (packed, *summed, *after),
            flops=each * flops,
        )
        after = (made,)
        got.append(lax.ppermute(made, "chip", [(source, source ^ step) for source in range(chips)]))
    lanes = each * two_fine // 2
    sides = call(
        functools.partial(near_kernel, each),
        (
            jax.ShapeDtypeStruct((2 * row_total, lanes), jnp.float32),
            jax.ShapeDtypeStruct((2 * MW, lanes), jnp.float32),
        ),
        (*summed, *tables, *after),
        flops=each * flops,
    )
    image = call(
        functools.partial(image_kernel, each),
        jax.ShapeDtypeStruct((row_total, MW), jnp.float32),
        (packed, other_packed, *sides, *tables, *got),
    )
    rows = lax.all_to_all(image, EVERYONE, split_axis=0, concat_axis=0, tiled=True)
    return call(
        functools.partial(final_kernel, scale_factor),
        jax.ShapeDtypeStruct((ROWS_DEV, MW), jnp.float32),
        (rows.reshape(-1, ROWS_DEV, MW),),
    )


def solution(mesh):
    roles, bands, turns = (mesh.shape[name] for name in ("role", "band", "turn"))
    split = Mesh(mesh.devices.reshape(roles, bands, turns // CORES, CORES), EVERYONE)
    in_specs = (
        P(("role", "band"), None, TURN, None),
        P(TURN),
        P(),
        P(("role", "band"), None, None, None),
        P(("role", "band"), None, None, None),
        P(None, EVERYONE, None),
    )
    out_specs = P(EVERYONE, None)
    return jax.shard_map(local, mesh=split, in_specs=in_specs, out_specs=out_specs, check_vma=False)
```

```python
import functools
import math

import jax
import jax.numpy as jnp
from jax import lax
from jax.experimental import pallas as pl
from jax.experimental.pallas import tpu as pltpu
from jax.sharding import Mesh
from jax.sharding import PartitionSpec as P

NGRID = 4096
MW = 128
ROWS_DEV = 1
DIGIT = 64
PAD_ROWS = 16
CORES = 2
TURN = ("chip", "core")
EVERYONE = ("role", "band", *TURN)
VMEM_BYTES = 24 * 1024 * 1024


def split_terms(value):
    high = value.astype(jnp.bfloat16)
    return high, (value - high.astype(jnp.float32)).astype(jnp.bfloat16)


def phase(cell, pixel):
    quarter = NGRID // 4
    turned = (cell * pixel) & (NGRID - 1)
    quadrant = (turned + quarter // 2) // quarter
    angle = (turned - quadrant * quarter).astype(jnp.float32) * (2.0 * math.pi / NGRID)
    square = angle * angle
    sine = angle * (1 + square * (-1 / 6 + square * (1 / 120 + square * (-1 / 5040 + square * (1 / 362880)))))
    cosine = 1 + square * (-1 / 2 + square * (1 / 24 + square * (-1 / 720 + square * (1 / 40320))))
    odd = (quadrant & 1) == 1
    real = jnp.where(odd, sine, cosine)
    imag = jnp.where(odd, cosine, sine)
    return (
        jnp.where(((quadrant + 1) & 2) == 2, -real, real),
        jnp.where((quadrant & 2) == 2, -imag, imag),
    )


def token_kernel(out_ref):
    out_ref[...] = jnp.zeros_like(out_ref)


def tables_kernel(_, row_ref, col_ref):
    for out_ref, sign in ((row_ref, 1), (col_ref, -1)):
        pixels, cells = out_ref.shape[0] // 2, out_ref.shape[1] // 6
        place = lax.broadcasted_iota(jnp.int32, (2 * pixels, 2 * cells), 0)
        lane = lax.broadcasted_iota(jnp.int32, (2 * pixels, 2 * cells), 1)
        lower, right = place >= pixels, lane >= cells
        pixel = jnp.where(lower, place - pixels, place) - pixels // 2
        cos, sin = phase(jnp.where(right, lane - cells, lane), pixel)
        value = jnp.where(lower == right, cos, sin)
        value = jnp.where(right & (lower == (sign < 0)), -value, value)
        high, low = split_terms(value)
        out_ref[...] = jnp.concatenate([high, low, high], axis=1)


def pack_kernel(flags_ref, cells_ref, _rows_ref, _cols_ref, _table_ref, packed_ref):
    turn = lax.axis_index(TURN)
    count, lanes = cells_ref.shape[1], packed_ref.shape[1]
    wide = jnp.concatenate([cells_ref[...]] * (lanes // count), axis=1)
    lane = lax.broadcasted_iota(jnp.int32, wide.shape, 1)
    wide = jnp.where((lane >= turn * count) & (lane < (turn + 1) * count), wide, 0)
    packed_ref[...] = jnp.zeros_like(packed_ref)
    packed_ref[0:2] = (wide // DIGIT).astype(jnp.float32)
    packed_ref[2:4] = (wide % DIGIT).astype(jnp.float32)
    packed_ref[4:5, : flags_ref.shape[1]] = flags_ref[...].astype(jnp.float32)


def gridding_weights(rows_ref, cols_ref, packed_ref, turn, stations):
    both = jnp.concatenate([rows_ref[0, 0], cols_ref[0, 0]], axis=0).astype(jnp.float32)
    weights = jnp.zeros((both.shape[0], stations), jnp.float32)
    for group in range(lax.axis_size(TURN)):
        weights = jnp.where(turn == group, both[:, group * stations : (group + 1) * stations], weights)
    return (weights * packed_ref[4:5, :stations]).astype(jnp.bfloat16)


def gridded_frames(volt_ref, taps_ref, weights, firsts):
    taps, two_fine, _ = taps_ref.shape
    stations = volt_ref.shape[2]
    core = lax.axis_index("core")
    lhs = jnp.concatenate(
        [
            volt_ref[0, core, :, pl.ds(pl.multiple_of(first * two_fine, two_fine), taps * two_fine)]
            for first in firsts
        ],
        axis=0,
    )
    filt = taps_ref[...].reshape(taps * two_fine, two_fine)
    spectra = jnp.dot(lhs, filt, preferred_element_type=jnp.float32).astype(jnp.bfloat16)
    beside = jnp.concatenate(
        [spectra[index * stations : (index + 1) * stations] for index in range(len(firsts))], axis=1
    )
    gridded = jnp.dot(weights, beside, preferred_element_type=jnp.float32)
    return [gridded[:, index * two_fine : (index + 1) * two_fine] for index in range(len(firsts))]


def own_kernel(volt_ref, taps_ref, rows_ref, cols_ref, packed_ref, out_ref):
    weights = gridding_weights(rows_ref, cols_ref, packed_ref, lax.axis_index(TURN), volt_ref.shape[2])
    rows = weights.shape[0]
    for frame, gridded in enumerate(gridded_frames(volt_ref, taps_ref, weights, range(out_ref.shape[0] // rows))):
        out_ref[frame * rows : (frame + 1) * rows] = gridded


def other_added(step, each, volt_ref, taps_ref, rows_ref, cols_ref, packed_ref, part_ref):
    weights = gridding_weights(rows_ref, cols_ref, packed_ref, lax.axis_index(TURN) ^ 1, volt_ref.shape[2])
    rows = weights.shape[0]
    firsts = [(lax.axis_index("chip") ^ step) * each + frame for frame in range(each)]
    return [
        part_ref[pl.ds(pl.multiple_of(first * rows, rows), rows)] + gridded
        for first, gridded in zip(firsts, gridded_frames(volt_ref, taps_ref, weights, firsts))
    ]


def far_kernel(step, each, own_ref, *refs):
    out_ref = refs[-1]
    made = other_added(step, each, *refs[:6])
    rows = made[0].shape[0]
    for index, frame in enumerate(made):
        out_ref[index * rows : (index + 1) * rows] = frame.astype(jnp.bfloat16)
    digits = own_ref[...] + refs[4][...]
    digits = jnp.concatenate([digits, jnp.zeros((PAD_ROWS - digits.shape[0], digits.shape[1]), jnp.float32)], axis=0)
    out_ref[each * rows :] = digits.astype(jnp.bfloat16)


def cells_side(frames, first, sub):
    fine = frames[0].shape[1] // 2
    return jnp.concatenate(
        [
            jnp.concatenate([frame[first : first + sub, :fine], frame[first : first + sub, fine:]], axis=0)
            for frame in frames
        ],
        axis=1,
    )


def near_kernel(each, *refs):
    row_dft_ref, col_dft_ref, _, row_ref, col_ref = refs[6:]
    made = other_added(0, each, *refs[:6])
    sub = row_dft_ref.shape[1] // 6
    for dft_ref, out_ref, first in ((row_dft_ref, row_ref, 0), (col_dft_ref, col_ref, sub)):
        high, low = split_terms(cells_side(made, first, sub))
        out_ref[...] = jnp.dot(
            dft_ref[...], jnp.concatenate([high, high, low], axis=0), preferred_element_type=jnp.float32
        )


def image_kernel(each, own_ref, packed_ref, row_ref, col_ref, row_dft_ref, col_dft_ref, *refs):
    *got, out_ref = refs
    fine = got[0].shape[1] // 2
    sub = row_dft_ref.shape[1] // 6
    digits = own_ref[...] + packed_ref[...]
    for source in got:
        digits = digits + source[each * 2 * sub :].astype(jnp.float32)[: digits.shape[0]]
    cell_u = (digits[0:1, :fine] * DIGIT + digits[2:3, :fine]).astype(jnp.int32)
    cell_v = (digits[1:2, :fine] * DIGIT + digits[3:4, :fine]).astype(jnp.int32)

    def side(plain_ref, dft_ref, first, cell):
        plain = plain_ref[...]
        half = plain.shape[0] // 2
        for source in got:
            frames = [source[index * 2 * sub : (index + 1) * 2 * sub] for index in range(each)]
            held = cells_side(frames, first, sub)
            plain = plain + jnp.dot(
                dft_ref[:, : 4 * sub], jnp.concatenate([held, held], axis=0), preferred_element_type=jnp.float32
            )
        cos, sin = phase(cell, lax.broadcasted_iota(jnp.int32, (half, fine), 0) - half // 2)
        cos = jnp.concatenate([cos] * each, axis=1)
        sin = jnp.concatenate([sin] * each, axis=1)
        real, imag = plain[:half], plain[half:]
        return real * cos - imag * sin, real * sin + imag * cos

    row_real, row_imag = side(row_ref, row_dft_ref, 0, cell_u)
    col_real, col_imag = side(col_ref, col_dft_ref, sub, cell_v)
    left = jnp.concatenate([row_real, -row_imag], axis=1).astype(jnp.bfloat16)
    right = jnp.concatenate([col_real, col_imag], axis=1).astype(jnp.bfloat16)
    out_ref[...] = lax.dot_general(left, right, (((1,), (1,)), ((), ())), preferred_element_type=jnp.float32)


def final_kernel(scale_factor, in_ref, out_ref):
    out_ref[...] = jnp.sum(in_ref[...], axis=0) * scale_factor


def call(kernel, shape, args, flops=0):
    moved = sum(math.prod(leaf.shape) * leaf.dtype.itemsize for leaf in [*jax.tree.leaves(shape), *args])
    return pl.pallas_call(
        kernel,
        out_shape=shape,
        in_specs=[pl.BlockSpec(memory_space=pltpu.VMEM)] * len(args),
        out_specs=jax.tree.map(lambda _: pl.BlockSpec(memory_space=pltpu.VMEM), shape),
        compiler_params=pltpu.CompilerParams(vmem_limit_bytes=VMEM_BYTES),
        cost_estimate=pl.CostEstimate(flops=flops, bytes_accessed=moved, transcendentals=0),
    )(*args)


def local(voltages, station_flags, filter_taps, kernel_rows, kernel_cols, cell_index):
    station_rows, width = voltages.shape[2:]
    taps, two_fine, _ = filter_taps.shape
    sub_u, sub_v = kernel_rows.shape[2], kernel_cols.shape[2]
    chips = lax.axis_size("chip")
    row_total = ROWS_DEV * lax.axis_size(EVERYONE)
    channels = two_fine // 2 * lax.axis_size("role") * lax.axis_size("band")
    frames = width // two_fine - taps + 1
    scale_factor = 4.0 / math.sqrt(channels * sub_u * sub_v) / frames
    each = frames // chips
    sub_rows = sub_u + sub_v

    swap = [(core, 1 - core) for core in range(CORES)]
    other = lax.ppermute(voltages, "core", swap)
    token = call(
        token_kernel, jax.ShapeDtypeStruct((8, MW), jnp.float32), (), flops=2 * voltages.size * two_fine * taps
    )
    packed = call(
        pack_kernel,
        jax.ShapeDtypeStruct((8, two_fine), jnp.float32),
        (station_flags.reshape(1, -1), cell_index.reshape(2, -1), kernel_rows, kernel_cols, token),
    )
    other_packed = lax.ppermute(packed, "core", swap)
    flops = 2 * station_rows * taps * two_fine * two_fine
    part = call(
        own_kernel,
        jax.ShapeDtypeStruct((frames * sub_rows, two_fine), jnp.float32),
        (voltages, filter_taps, kernel_rows, kernel_cols, packed),
        flops=frames * flops,
    )

    summed = (other, filter_taps, kernel_rows, kernel_cols, other_packed, part)
    after = ()
    got = []
    for step in range(1, chips):
        made = call(
            functools.partial(far_kernel, step, each),
            jax.ShapeDtypeStruct((each * sub_rows + PAD_ROWS, two_fine), jnp.bfloat16),
            (packed, *summed, *after),
            flops=each * flops,
        )
        after = (made,)
        got.append(lax.ppermute(made, "chip", [(source, source ^ step) for source in range(chips)]))
    tables = call(
        tables_kernel,
        (
            jax.ShapeDtypeStruct((2 * row_total, 6 * sub_u), jnp.bfloat16),
            jax.ShapeDtypeStruct((2 * MW, 6 * sub_v), jnp.bfloat16),
        ),
        after,
    )
    lanes = each * two_fine // 2
    sides = call(
        functools.partial(near_kernel, each),
        (
            jax.ShapeDtypeStruct((2 * row_total, lanes), jnp.float32),
            jax.ShapeDtypeStruct((2 * MW, lanes), jnp.float32),
        ),
        (*summed, *tables, *after),
        flops=each * flops,
    )
    image = call(
        functools.partial(image_kernel, each),
        jax.ShapeDtypeStruct((row_total, MW), jnp.float32),
        (packed, other_packed, *sides, *tables, *got),
    )
    rows = lax.all_to_all(image, EVERYONE, split_axis=0, concat_axis=0, tiled=True)
    return call(
        functools.partial(final_kernel, scale_factor),
        jax.ShapeDtypeStruct((ROWS_DEV, MW), jnp.float32),
        (rows.reshape(-1, ROWS_DEV, MW),),
    )


def solution(mesh):
    roles, bands, turns = (mesh.shape[name] for name in ("role", "band", "turn"))
    split = Mesh(mesh.devices.reshape(roles, bands, turns // CORES, CORES), EVERYONE)
    in_specs = (
        P(("role", "band"), None, TURN, None),
        P(TURN),
        P(),
        P(("role", "band"), None, None, None),
        P(("role", "band"), None, None, None),
        P(None, EVERYONE, None),
    )
    out_specs = P(EVERYONE, None)
    return jax.shard_map(local, mesh=split, in_specs=in_specs, out_specs=out_specs, check_vma=False)
```

```python
import functools
import math

import jax
import jax.numpy as jnp
from jax import lax
from jax.experimental import pallas as pl
from jax.experimental.pallas import tpu as pltpu
from jax.sharding import Mesh
from jax.sharding import PartitionSpec as P

NGRID = 4096
MW = 128
ROWS_DEV = 1
DIGIT = 64
PAD_ROWS = 16
CORES = 2
TURN = ("chip", "core")
EVERYONE = ("role", "band", *TURN)
VMEM_BYTES = 24 * 1024 * 1024


def split_terms(value):
    high = value.astype(jnp.bfloat16)
    return high, (value - high.astype(jnp.float32)).astype(jnp.bfloat16)


def phase(cell, pixel):
    quarter = NGRID // 4
    turned = (cell * pixel) & (NGRID - 1)
    quadrant = (turned + quarter // 2) // quarter
    angle = (turned - quadrant * quarter).astype(jnp.float32) * (2.0 * math.pi / NGRID)
    square = angle * angle
    sine = angle * (1 + square * (-1 / 6 + square * (1 / 120 + square * (-1 / 5040 + square * (1 / 362880)))))
    cosine = 1 + square * (-1 / 2 + square * (1 / 24 + square * (-1 / 720 + square * (1 / 40320))))
    odd = (quadrant & 1) == 1
    real = jnp.where(odd, sine, cosine)
    imag = jnp.where(odd, cosine, sine)
    return (
        jnp.where(((quadrant + 1) & 2) == 2, -real, real),
        jnp.where((quadrant & 2) == 2, -imag, imag),
    )


def tables_kernel(row_ref, col_ref):
    for out_ref, sign in ((row_ref, 1), (col_ref, -1)):
        pixels, cells = out_ref.shape[0] // 2, out_ref.shape[1] // 6
        place = lax.broadcasted_iota(jnp.int32, (2 * pixels, 2 * cells), 0)
        lane = lax.broadcasted_iota(jnp.int32, (2 * pixels, 2 * cells), 1)
        lower, right = place >= pixels, lane >= cells
        pixel = jnp.where(lower, place - pixels, place) - pixels // 2
        cos, sin = phase(jnp.where(right, lane - cells, lane), pixel)
        value = jnp.where(lower == right, cos, sin)
        value = jnp.where(right & (lower == (sign < 0)), -value, value)
        high, low = split_terms(value)
        out_ref[...] = jnp.concatenate([high, low, high], axis=1)


def pack_kernel(flags_ref, cells_ref, _rows_ref, _cols_ref, _table_ref, packed_ref):
    turn = lax.axis_index(TURN)
    count, lanes = cells_ref.shape[1], packed_ref.shape[1]
    wide = jnp.concatenate([cells_ref[...]] * (lanes // count), axis=1)
    lane = lax.broadcasted_iota(jnp.int32, wide.shape, 1)
    wide = jnp.where((lane >= turn * count) & (lane < (turn + 1) * count), wide, 0)
    packed_ref[...] = jnp.zeros_like(packed_ref)
    packed_ref[0:2] = (wide // DIGIT).astype(jnp.float32)
    packed_ref[2:4] = (wide % DIGIT).astype(jnp.float32)
    packed_ref[4:5, : flags_ref.shape[1]] = flags_ref[...].astype(jnp.float32)


def gridding_weights(rows_ref, cols_ref, packed_ref, turn, stations):
    both = jnp.concatenate([rows_ref[0, 0], cols_ref[0, 0]], axis=0).astype(jnp.float32)
    weights = jnp.zeros((both.shape[0], stations), jnp.float32)
    for group in range(lax.axis_size(TURN)):
        weights = jnp.where(turn == group, both[:, group * stations : (group + 1) * stations], weights)
    return (weights * packed_ref[4:5, :stations]).astype(jnp.bfloat16)


def gridded_frames(volt_ref, taps_ref, weights, firsts):
    taps, two_fine, _ = taps_ref.shape
    stations = volt_ref.shape[2]
    core = lax.axis_index("core")
    lhs = jnp.concatenate(
        [
            volt_ref[0, core, :, pl.ds(pl.multiple_of(first * two_fine, two_fine), taps * two_fine)]
            for first in firsts
        ],
        axis=0,
    )
    filt = taps_ref[...].reshape(taps * two_fine, two_fine)
    half = taps // 2 * two_fine
    spectra = jnp.dot(lhs[:, :half], filt[:half], preferred_element_type=jnp.float32)
    spectra = spectra + jnp.dot(lhs[:, half:], filt[half:], preferred_element_type=jnp.float32)
    spectra = spectra.astype(jnp.bfloat16)
    beside = jnp.concatenate(
        [spectra[index * stations : (index + 1) * stations] for index in range(len(firsts))], axis=1
    )
    gridded = jnp.dot(weights, beside, preferred_element_type=jnp.float32)
    return [gridded[:, index * two_fine : (index + 1) * two_fine] for index in range(len(firsts))]


def own_kernel(volt_ref, taps_ref, rows_ref, cols_ref, packed_ref, out_ref):
    weights = gridding_weights(rows_ref, cols_ref, packed_ref, lax.axis_index(TURN), volt_ref.shape[2])
    rows = weights.shape[0]
    for frame, gridded in enumerate(gridded_frames(volt_ref, taps_ref, weights, range(out_ref.shape[0] // rows))):
        out_ref[frame * rows : (frame + 1) * rows] = gridded


def other_added(step, each, volt_ref, taps_ref, rows_ref, cols_ref, packed_ref, part_ref):
    weights = gridding_weights(rows_ref, cols_ref, packed_ref, lax.axis_index(TURN) ^ 1, volt_ref.shape[2])
    rows = weights.shape[0]
    firsts = [(lax.axis_index("chip") ^ step) * each + frame for frame in range(each)]
    return [
        part_ref[pl.ds(pl.multiple_of(first * rows, rows), rows)] + gridded
        for first, gridded in zip(firsts, gridded_frames(volt_ref, taps_ref, weights, firsts))
    ]


def far_kernel(step, each, own_ref, *refs):
    out_ref = refs[-1]
    made = other_added(step, each, *refs[:6])
    rows = made[0].shape[0]
    for index, frame in enumerate(made):
        out_ref[index * rows : (index + 1) * rows] = frame.astype(jnp.bfloat16)
    digits = own_ref[...] + refs[4][...]
    digits = jnp.concatenate([digits, jnp.zeros((PAD_ROWS - digits.shape[0], digits.shape[1]), jnp.float32)], axis=0)
    out_ref[each * rows :] = digits.astype(jnp.bfloat16)


def cells_side(frames, first, sub):
    fine = frames[0].shape[1] // 2
    return jnp.concatenate(
        [
            jnp.concatenate([frame[first : first + sub, :fine], frame[first : first + sub, fine:]], axis=0)
            for frame in frames
        ],
        axis=1,
    )


def near_kernel(each, *refs):
    row_dft_ref, col_dft_ref, _, row_ref, col_ref = refs[6:]
    made = other_added(0, each, *refs[:6])
    sub = row_dft_ref.shape[1] // 6
    for dft_ref, out_ref, first in ((row_dft_ref, row_ref, 0), (col_dft_ref, col_ref, sub)):
        high, low = split_terms(cells_side(made, first, sub))
        out_ref[...] = jnp.dot(
            dft_ref[...], jnp.concatenate([high, high, low], axis=0), preferred_element_type=jnp.float32
        )


def image_kernel(each, own_ref, packed_ref, row_ref, col_ref, row_dft_ref, col_dft_ref, *refs):
    *got, out_ref = refs
    fine = got[0].shape[1] // 2
    sub = row_dft_ref.shape[1] // 6
    digits = own_ref[...] + packed_ref[...]
    for source in got:
        digits = digits + source[each * 2 * sub :].astype(jnp.float32)[: digits.shape[0]]
    cell_u = (digits[0:1, :fine] * DIGIT + digits[2:3, :fine]).astype(jnp.int32)
    cell_v = (digits[1:2, :fine] * DIGIT + digits[3:4, :fine]).astype(jnp.int32)

    def side(plain_ref, dft_ref, first, cell):
        plain = plain_ref[...]
        half = plain.shape[0] // 2
        for source in got:
            frames = [source[index * 2 * sub : (index + 1) * 2 * sub] for index in range(each)]
            held = cells_side(frames, first, sub)
            plain = plain + jnp.dot(
                dft_ref[:, : 4 * sub], jnp.concatenate([held, held], axis=0), preferred_element_type=jnp.float32
            )
        cos, sin = phase(cell, lax.broadcasted_iota(jnp.int32, (half, fine), 0) - half // 2)
        cos = jnp.concatenate([cos] * each, axis=1)
        sin = jnp.concatenate([sin] * each, axis=1)
        real, imag = plain[:half], plain[half:]
        return real * cos - imag * sin, real * sin + imag * cos

    row_real, row_imag = side(row_ref, row_dft_ref, 0, cell_u)
    col_real, col_imag = side(col_ref, col_dft_ref, sub, cell_v)
    left = jnp.concatenate([row_real, -row_imag], axis=1).astype(jnp.bfloat16)
    right = jnp.concatenate([col_real, col_imag], axis=1).astype(jnp.bfloat16)
    out_ref[...] = lax.dot_general(left, right, (((1,), (1,)), ((), ())), preferred_element_type=jnp.float32)


def final_kernel(scale_factor, in_ref, out_ref):
    out_ref[...] = jnp.sum(in_ref[...], axis=0) * scale_factor


def call(kernel, shape, args, flops=0):
    moved = sum(math.prod(leaf.shape) * leaf.dtype.itemsize for leaf in [*jax.tree.leaves(shape), *args])
    return pl.pallas_call(
        kernel,
        out_shape=shape,
        in_specs=[pl.BlockSpec(memory_space=pltpu.VMEM)] * len(args),
        out_specs=jax.tree.map(lambda _: pl.BlockSpec(memory_space=pltpu.VMEM), shape),
        compiler_params=pltpu.CompilerParams(vmem_limit_bytes=VMEM_BYTES),
        cost_estimate=pl.CostEstimate(flops=flops, bytes_accessed=moved, transcendentals=0),
    )(*args)


def local(voltages, station_flags, filter_taps, kernel_rows, kernel_cols, cell_index):
    station_rows, width = voltages.shape[2:]
    taps, two_fine, _ = filter_taps.shape
    sub_u, sub_v = kernel_rows.shape[2], kernel_cols.shape[2]
    chips = lax.axis_size("chip")
    row_total = ROWS_DEV * lax.axis_size(EVERYONE)
    channels = two_fine // 2 * lax.axis_size("role") * lax.axis_size("band")
    frames = width // two_fine - taps + 1
    scale_factor = 4.0 / math.sqrt(channels * sub_u * sub_v) / frames
    each = frames // chips
    sub_rows = sub_u + sub_v

    swap = [(core, 1 - core) for core in range(CORES)]
    other = lax.ppermute(voltages, "core", swap)
    tables = call(
        tables_kernel,
        (
            jax.ShapeDtypeStruct((2 * row_total, 6 * sub_u), jnp.bfloat16),
            jax.ShapeDtypeStruct((2 * MW, 6 * sub_v), jnp.bfloat16),
        ),
        (),
        flops=2 * voltages.size * two_fine * taps,
    )
    packed = call(
        pack_kernel,
        jax.ShapeDtypeStruct((8, two_fine), jnp.float32),
        (station_flags.reshape(1, -1), cell_index.reshape(2, -1), kernel_rows, kernel_cols, tables[0]),
    )
    other_packed = lax.ppermute(packed, "core", swap)
    flops = 2 * station_rows * taps * two_fine * two_fine
    part = call(
        own_kernel,
        jax.ShapeDtypeStruct((frames * sub_rows, two_fine), jnp.float32),
        (voltages, filter_taps, kernel_rows, kernel_cols, packed),
        flops=frames * flops,
    )

    summed = (other, filter_taps, kernel_rows, kernel_cols, other_packed, part)
    after = ()
    got = []
    for step in range(1, chips):
        made = call(
            functools.partial(far_kernel, step, each),
            jax.ShapeDtypeStruct((each * sub_rows + PAD_ROWS, two_fine), jnp.bfloat16),
            (packed, *summed, *after),
            flops=each * flops,
        )
        after = (made,)
        got.append(lax.ppermute(made, "chip", [(source, source ^ step) for source in range(chips)]))
    lanes = each * two_fine // 2
    sides = call(
        functools.partial(near_kernel, each),
        (
            jax.ShapeDtypeStruct((2 * row_total, lanes), jnp.float32),
            jax.ShapeDtypeStruct((2 * MW, lanes), jnp.float32),
        ),
        (*summed, *tables, *after),
        flops=each * flops,
    )
    image = call(
        functools.partial(image_kernel, each),
        jax.ShapeDtypeStruct((row_total, MW), jnp.float32),
        (packed, other_packed, *sides, *tables, *got),
    )
    rows = lax.all_to_all(image, EVERYONE, split_axis=0, concat_axis=0, tiled=True)
    return call(
        functools.partial(final_kernel, scale_factor),
        jax.ShapeDtypeStruct((ROWS_DEV, MW), jnp.float32),
        (rows.reshape(-1, ROWS_DEV, MW),),
    )


def solution(mesh):
    roles, bands, turns = (mesh.shape[name] for name in ("role", "band", "turn"))
    split = Mesh(mesh.devices.reshape(roles, bands, turns // CORES, CORES), EVERYONE)
    in_specs = (
        P(("role", "band"), None, TURN, None),
        P(TURN),
        P(),
        P(("role", "band"), None, None, None),
        P(("role", "band"), None, None, None),
        P(None, EVERYONE, None),
    )
    out_specs = P(EVERYONE, None)
    return jax.shard_map(local, mesh=split, in_specs=in_specs, out_specs=out_specs, check_vma=False)
```
